32 devices in a mesh: scene: 16 (over z, y, core), frame: 2 (over x).
Axes of the slice: x: 2, y: 2, z: 4, core: 2. Of those that a mesh axis runs over, the one named last changes fastest.
Arguments:
- tokens: bfloat16 [4096, 1024], P(('scene', 'frame')), may hold values from -6 to 6
- cotangent: bfloat16 [4096, 1024], P(('scene', 'frame')), may hold values from -6 to 6
- scene_ids: int32 [4096], P(('scene', 'frame')), may hold values from 0 to 63, as said below
- frame_index: int32 [4096], P(('scene', 'frame')), may hold values from 0 to 3, as said below
- qkv_weight: bfloat16 [2, 1024, 3072], P(None, ('scene', 'frame')), may hold values from -0.1875 to 0.1875
- qkv_bias: bfloat16 [2, 3072], P(None, ('scene', 'frame')), may hold values from -1.796875 to 1.796875
- proj_weight: bfloat16 [2, 1024, 1024], P(None, ('scene', 'frame')), may hold values from -2 to 2
- fc1_weight: bfloat16 [2, 1024, 4096], P(None, ('scene', 'frame')), may hold values from -0.1875 to 0.1875
- fc1_bias: bfloat16 [2, 4096], P(None, ('scene', 'frame')), may hold values from -1.796875 to 1.796875
- fc2_weight: bfloat16 [2, 4096, 1024], P(None, ('scene', 'frame')), may hold values from -0.09375 to 0.09375
- out_bias: bfloat16 [2, 2, 1024], P(None, None, ('scene', 'frame')), may hold values from -1.796875 to 1.796875
- norm_gain: bfloat16 [2, 2, 1024], P(None, None, ('scene', 'frame')), may hold values from 0.5 to 1.5
- norm_bias: bfloat16 [2, 2, 1024], P(None, None, ('scene', 'frame')), may hold values from -1.796875 to 1.796875
- layer_scale: bfloat16 [2, 2, 1024], P(None, None, ('scene', 'frame')), may hold values from 0.29882812 to 1
- qk_gain: bfloat16 [2, 2, 64], replicated, may hold values from 0.5 to 1.5
- qk_bias: bfloat16 [2, 2, 64], replicated, may hold values from -1.796875 to 1.796875
Outputs:
- activations: bfloat16 [4096, 1024], P(('scene', 'frame'))
- input_grad: bfloat16 [4096, 1024], P(('scene', 'frame'))
- qkv_weight_grad: float32 [2, 1024, 3072], P(None, ('scene', 'frame'))
- qkv_bias_grad: float32 [2, 3072], P(None, ('scene', 'frame'))
- proj_weight_grad: float32 [2, 1024, 1024], P(None, ('scene', 'frame'))
- fc1_weight_grad: float32 [2, 1024, 4096], P(None, ('scene', 'frame'))
- fc1_bias_grad: float32 [2, 4096], P(None, ('scene', 'frame'))
- fc2_weight_grad: float32 [2, 4096, 1024], P(None, ('scene', 'frame'))
- out_bias_grad: float32 [2, 2, 1024], P(None, None, ('scene', 'frame'))
- norm_gain_grad: float32 [2, 2, 1024], P(None, None, ('scene', 'frame'))
- norm_bias_grad: float32 [2, 2, 1024], P(None, None, ('scene', 'frame'))
- layer_scale_grad: float32 [2, 2, 1024], P(None, None, ('scene', 'frame'))
- qk_gain_grad: float32 [2, 2, 64], replicated
- qk_bias_grad: float32 [2, 2, 64], replicated
The draws below stay inside these ranges and needn't reach their ends.
Inputs may be any that keep to these rules, and one draw needn't show every extreme that they name: `scene_ids`: tokens of one scene are whole consecutive frames of 64 tokens within the tokens of one index of scene; a scene's id is the number of its first frame among all frames; index 0 of scene holds a single scene; the last frame of the last index of scene is a scene of its own. `frame_index`: the frame's position within its scene, counted from 0, equal for the 64 tokens of one frame.
All inputs are finite; a program needn't handle non-finite values.
Results may differ from the reference program's by a relative error of at most 0.014.
Values may be sent and summed in bfloat16 or wider, within the bound.
No kernel may reach another device: no remote copies, remote signals or barrier semaphores. Data moves between devices by JAX's collectives and lax.ppermute only.
A program may use at most 320 MiB of HBM per device.

```python
import math
import jax
import jax.numpy as jnp
from jax import lax

D = 1024
HEADS = 16
HD = 64
FF = 4096
FRAME_TOK = 64
FR_DEV = 2
TOK_DEV = 128
TOKENS = 4096
N_SCENE = 16
N_FRAME = 2


def scene_layout(key):
    key = jax.random.fold_in(key, 31)
    per_group = FR_DEV * N_FRAME
    position = jnp.arange(per_group, dtype=jnp.int32)[None, :]
    group_number = jnp.arange(N_SCENE, dtype=jnp.int32)[:, None]
    starts = jax.random.randint(key, (N_SCENE, per_group), 0, 3) == 0
    starts = starts & (group_number != 0) | (position == 0)
    starts = starts | (position == per_group - 1) & (group_number == N_SCENE - 1)
    first_frame = lax.cummax(jnp.where(starts, position, 0), axis=1)
    scene_number = group_number * per_group + first_frame
    frame_number = position - first_frame
    scene_number = jnp.repeat(scene_number.reshape(-1), FRAME_TOK, total_repeat_length=N_SCENE * per_group * FRAME_TOK)
    frame_number = jnp.repeat(frame_number.reshape(-1), FRAME_TOK, total_repeat_length=N_SCENE * per_group * FRAME_TOK)
    return (scene_number.astype(jnp.int32), frame_number.astype(jnp.int32))


def draw_scene_ids(key, part):
    return scene_layout(key)[0]


def draw_frame_index(key, part):
    return scene_layout(key)[1]


def strengthened(values, rng, source, target, parts, factor):
    owner, partner = [(jnp.arange(values.shape[axis_at]) // (values.shape[axis_at] // parts)).reshape([-1 if axis == axis_at else 1 for axis in range(values.ndim)]) for axis_at in (source, target)]
    chosen = jax.random.permutation(rng, parts)[partner]
    strong = (owner == chosen) | (owner == (partner + parts // 2) % parts)
    return jnp.where(strong, factor * values, values)


def block_scale(stream_key, dims, split, smallest, top_value):
    loudness, own = 1.0, jax.random.fold_in(stream_key, 6)
    for dim, parts in split:
        heights = jnp.exp(jax.random.uniform(jax.random.fold_in(own, dim), (parts,), jnp.float32, smallest / len(split), top_value / len(split)))
        loudness = loudness * jnp.repeat(heights, dims[dim] // parts).reshape([-1 if axis == dim else 1 for axis in range(len(dims))])
    return loudness


def gaussian(stream_key, shape, width, bound, cuts=(), kind=jnp.bfloat16):
    values = jax.random.normal(stream_key, shape, jnp.float32) * width
    if len(cuts) > 0:
        values = block_scale(stream_key, shape, cuts, -0.22, 0.18) * values
    return jnp.clip(values, min=-bound, max=bound).astype(kind)


def gaussian_with(rng, shape, scale, limit, shards, heavy, kind=jnp.bfloat16):
    drawn = scale * jax.random.normal(rng, shape, jnp.float32)
    if shards:
        drawn = drawn * block_scale(rng, shape, shards, -0.22, 0.18)
    return jnp.clip(strengthened(drawn, jax.random.fold_in(rng, 3), *heavy), -limit, limit).astype(kind)


def setup_inputs(seed: int = 0) -> dict:
    key_list = jax.random.split(jax.random.key(seed), 17)
    return {
        "tokens": gaussian(key_list[0], (TOKENS, D), 1.0, 6.0, ((0, 32),)),
        "cotangent": gaussian_with(key_list[1], (TOKENS, D), 1.0, 6.0, ((0, 32),), (0, 1, 32, 2.75)),
        "scene_ids": draw_scene_ids(jax.random.fold_in(key_list[16], 71), 0),
        "frame_index": draw_frame_index(jax.random.fold_in(key_list[16], 71), 0),
        "qkv_weight": gaussian(key_list[4], (2, D, 3 * D), D ** -0.5, 0.1875, ((1, 32),)),
        "qkv_bias": gaussian(key_list[5], (2, 3 * D), 0.3, 1.796875, ((1, 32),)),
        "proj_weight": gaussian(key_list[6], (2, D, D), (D // 128) ** -0.5, 2.0, ((1, 32),)),
        "fc1_weight": gaussian(key_list[7], (2, D, FF), D ** -0.5, 0.1875, ((1, 32),)),
        "fc1_bias": gaussian(key_list[8], (2, FF), 0.3, 1.796875, ((1, 32),)),
        "fc2_weight": gaussian(key_list[9], (2, FF, D), FF ** -0.5, 0.09375, ((1, 32),)),
        "out_bias": gaussian(key_list[10], (2, 2, D), 0.3, 1.796875, ((2, 32),)),
        "norm_gain": jnp.clip(1.0 + 0.1 * jax.random.normal(key_list[11], (2, 2, D), jnp.float32), 0.5, 1.5).astype(jnp.bfloat16),
        "norm_bias": gaussian(key_list[12], (2, 2, D), 0.3, 1.796875, ((2, 32),)),
        "layer_scale": jnp.clip(jnp.exp(math.log(1.0) - 1.2078867 * jax.random.uniform(key_list[13], (2, 2, D), jnp.float32) ** block_scale(key_list[13], (2, 2, D), ((2, 32),), -0.2, 0.2)), 0.29882812, 1.0).astype(jnp.bfloat16),
        "qk_gain": jnp.clip(1.0 + 0.1 * jax.random.normal(key_list[14], (2, 2, HD), jnp.float32), 0.5, 1.5).astype(jnp.bfloat16),
        "qk_bias": gaussian(key_list[15], (2, 2, HD), 0.3, 1.796875),
    }


EPSILON = 1e-06
HIGHEST = lax.Precision.HIGHEST

@jax.custom_vjp
def low(v):
    return lax.optimization_barrier(v.astype(jnp.bfloat16)).astype(jnp.float32)

@jax.custom_vjp
def low_back(v):
    return v

def low_keep(v):
    return (low(v), None)

def low_pass(kept, grad):
    return (grad,)

def back_keep(v):
    return (v, None)

def back_low(kept, grad):
    return (low(grad),)
low.defvjp(low_keep, low_pass)
low_back.defvjp(back_keep, back_low)

def layer_norm(values_in, gain_vec, shift_vec):
    center = values_in - lax.optimization_barrier(jnp.mean(values_in, axis=-1, keepdims=True))
    spread = lax.optimization_barrier(jnp.mean(center * center, axis=-1, keepdims=True))
    return center * lax.rsqrt(spread + EPSILON) * gain_vec + shift_vec

def matmul(left_side, right_side):
    return jnp.dot(left_side, right_side, precision=HIGHEST)

def exact_gelu(values_in):
    return jax.nn.gelu(values_in, approximate=False)

def attend_group(queries, key_rows, value_rows, scene_col, frame_col, use_frame):
    row_count = queries.shape[0]
    block_rows = math.gcd(row_count, 512)
    block_count = row_count // block_rows
    query_blocks = queries.reshape(block_count, block_rows, HEADS, HD)
    scene_blocks = scene_col.reshape(block_count, block_rows)
    frame_blocks = frame_col.reshape(block_count, block_rows)

    def one_block(pieces):
        query_part, scene_part, frame_part = pieces
        scores = low_back(HD ** (-0.5) * jnp.einsum('qhd,khd->hqk', query_part, key_rows, precision=HIGHEST))
        allowed = scene_part[:, None] == scene_col[None, :]
        if use_frame:
            allowed = allowed & (frame_part[:, None] == frame_col[None, :])
        scores = jnp.where(allowed[None], scores, -jnp.inf)
        weights = low(jax.nn.softmax(scores, axis=-1))
        return jnp.einsum('hqk,khd->qhd', weights, value_rows, precision=HIGHEST)
    result = lax.map(jax.checkpoint(one_block), (query_blocks, scene_blocks, frame_blocks))
    return result.reshape(row_count, HEADS, HD)

def attend_all(queries, key_rows, value_rows, scene_col, frame_col, group_rows, use_frame):
    row_count = queries.shape[0]
    groups = row_count // group_rows
    shaped = (groups, group_rows, HEADS, HD)

    def one_group(pieces):
        return attend_group(pieces[0], pieces[1], pieces[2], pieces[3], pieces[4], use_frame)
    result = lax.map(one_group, (queries.reshape(shaped), key_rows.reshape(shaped), value_rows.reshape(shaped), scene_col.reshape(groups, group_rows), frame_col.reshape(groups, group_rows)))
    return result.reshape(row_count, HEADS, HD)

def one_layer(stream, params, scene_col, frame_col, group_rows, use_frame):
    weight_qkv, bias_qkv, weight_proj, weight_up, bias_up, weight_down, out_shift, gains, shifts, scales, head_gain, head_shift = params
    row_count = stream.shape[0]
    first_normed = low(layer_norm(stream, gains[0], shifts[0]))
    mixed = (low_back(matmul(first_normed, weight_qkv)) + bias_qkv).reshape(row_count, 3, HEADS, HD)
    queries = low(layer_norm(mixed[:, 0], head_gain[0], head_shift[0]))
    key_rows = low(layer_norm(mixed[:, 1], head_gain[1], head_shift[1]))
    value_rows = low(mixed[:, 2])
    attended = attend_all(queries, key_rows, value_rows, scene_col, frame_col, group_rows, use_frame)
    flat_out = low_back(low(attended.reshape(row_count, D)))
    branch_one = low_back(matmul(flat_out, weight_proj)) + out_shift[0]
    middle = stream + scales[0] * branch_one
    second_normed = low(layer_norm(middle, gains[1], shifts[1]))
    hidden = low(exact_gelu(low_back(matmul(second_normed, weight_up)) + bias_up))
    branch_two = low_back(matmul(hidden, weight_down)) + out_shift[1]
    return middle + scales[1] * branch_two

def reference(tokens, cotangent, scene_ids, frame_index, qkv_weight, qkv_bias, proj_weight, fc1_weight, fc1_bias, fc2_weight, out_bias, norm_gain, norm_bias, layer_scale, qk_gain, qk_bias):
    weights = (qkv_weight, qkv_bias, proj_weight, fc1_weight, fc1_bias, fc2_weight, out_bias, norm_gain, norm_bias, layer_scale, qk_gain, qk_bias)
    weights = tuple((member.astype(jnp.float32) for member in weights))

    def forward(stream, params):
        for depth in range(2):
            group_rows = TOK_DEV if depth == 0 else TOK_DEV * N_FRAME
            stream = one_layer(stream, tuple((member[depth] for member in params)), scene_ids, frame_index, group_rows, depth == 0)
        return stream
    output, pullback = jax.vjp(forward, tokens.astype(jnp.float32), weights)
    grad_stream, grad_weights = pullback(cotangent.astype(jnp.float32))
    return (output.astype(jnp.bfloat16), grad_stream.astype(jnp.bfloat16), grad_weights[0], grad_weights[1], grad_weights[2], grad_weights[3], grad_weights[4], grad_weights[5], grad_weights[6], grad_weights[7], grad_weights[8], grad_weights[9], grad_weights[10], grad_weights[11])
```

```python
import jax
import jax.numpy as jnp
import numpy as np
from jax import lax
from jax.sharding import Mesh
from jax.sharding import PartitionSpec as P

EPSILON = 1e-06
FRAME_TOK = 64
LOW = jnp.bfloat16
WIDE = jnp.float32
EVERY = ("outer", "inner", "core", "frame")
REST = ("outer", "inner")
TEAM = ("core", "frame")


def dot(left, right):
    return jnp.dot(left, right, preferred_element_type=WIDE)


def dot_tn(left, right):
    return lax.dot_general(left, right, (((0,), (0,)), ((), ())), preferred_element_type=WIDE)


def dot_nt(left, right):
    return lax.dot_general(left, right, (((1,), (1,)), ((), ())), preferred_element_type=WIDE)


def normed(values):
    center = values - jnp.mean(values, axis=-1, keepdims=True)
    rate = lax.rsqrt(jnp.mean(center * center, axis=-1, keepdims=True) + EPSILON)
    return center * rate, rate


def normed_back(grad, unit, rate, gain):
    inner = grad * gain
    mean_one = jnp.mean(inner, axis=-1, keepdims=True)
    mean_two = jnp.mean(inner * unit, axis=-1, keepdims=True)
    return rate * (inner - mean_one - unit * mean_two)


def swap(values, axis):
    return lax.ppermute(values, axis, [(0, 1), (1, 0)])


def team_gather(values):
    if lax.axis_size("frame") == 2:
        pair = jnp.concatenate([values, swap(values, "frame")], axis=0)
    else:
        pair = lax.all_gather(values, "frame", axis=0, tiled=True)
    return jnp.concatenate([pair, swap(pair, "core")], axis=0)


def team_sum(parts):
    half = parts.shape[0] // 2
    pair = parts[:half] + swap(parts[half:].astype(LOW), "core").astype(WIDE)
    if lax.axis_size("frame") == 2:
        rows = half // 2
        return pair[:rows] + swap(pair[rows:].astype(LOW), "frame").astype(WIDE)
    return lax.psum_scatter(pair.astype(LOW), "frame", scatter_dimension=0, tiled=True).astype(WIDE)


def head_split(flat, heads):
    return flat.reshape(flat.shape[0], heads, flat.shape[1] // heads)


def attend_scores(queries, keys, ids, use_frame):
    scale = queries.shape[-1] ** (-0.5)
    scores = jnp.einsum("gqhd,gkhd->ghqk", queries, keys, preferred_element_type=WIDE) * scale
    if use_frame:
        return scores
    allowed = ids[:, :, None] == ids[:, None, :]
    return jnp.where(allowed[:, None], scores, -jnp.inf)


def in_groups(flat, group):
    return flat.reshape((flat.shape[0] // group, group) + flat.shape[1:])


def attend(queries, keys, values, ids, use_frame, group):
    queries, keys, values, ids = (in_groups(m, group) for m in (queries, keys, values, ids))
    scores = attend_scores(queries, keys, ids, use_frame)
    top = jnp.max(scores, axis=-1, keepdims=True)
    log_sum = top + jnp.log(jnp.sum(jnp.exp(scores - top), axis=-1, keepdims=True))
    probs = jnp.exp(scores - log_sum).astype(LOW)
    out = jnp.einsum("ghqk,gkhd->gqhd", probs, values, preferred_element_type=WIDE)
    return out.reshape(-1, out.shape[2] * out.shape[3]), log_sum


def attend_back(queries, keys, values, ids, use_frame, group, log_sum, grad_out):
    queries, keys, values, ids, grad_out = (
        in_groups(m, group) for m in (queries, keys, values, ids, grad_out)
    )
    scale = queries.shape[-1] ** (-0.5)
    scores = attend_scores(queries, keys, ids, use_frame)
    probs = jnp.exp(scores - log_sum)
    grad_probs = jnp.einsum("gqhd,gkhd->ghqk", grad_out, values, preferred_element_type=WIDE)
    delta = jnp.sum(probs * grad_probs, axis=-1, keepdims=True)
    grad_scores = (probs * (grad_probs - delta)).astype(LOW)
    grad_q = jnp.einsum("ghqk,gkhd->gqhd", grad_scores, keys, preferred_element_type=WIDE) * scale
    grad_k = jnp.einsum("ghqk,gqhd->gkhd", grad_scores, queries, preferred_element_type=WIDE) * scale
    grad_v = jnp.einsum(
        "ghqk,gqhd->gkhd", probs.astype(LOW), grad_out, preferred_element_type=WIDE
    )
    return tuple(m.reshape((-1,) + m.shape[2:]) for m in (grad_q, grad_k, grad_v))


def exact_gelu(values):
    return jax.nn.gelu(values, approximate=False)


def exchange_columns(values, count):
    rows, team, width = values.shape
    cores = 2
    frames = team // cores
    parts = values.reshape(rows, cores, frames, width).transpose(1, 2, 0, 3)
    here_x = lax.axis_index("frame")
    here_c = lax.axis_index("core")
    if frames == 2:
        keep = lax.dynamic_index_in_dim(parts, here_x, 1, keepdims=False)
        send = lax.dynamic_index_in_dim(parts, 1 - here_x, 1, keepdims=False)
        came = swap(send, "frame")
        both = jnp.stack([jnp.where(here_x == 0, keep, came), jnp.where(here_x == 0, came, keep)], axis=1)
    else:
        both = lax.all_to_all(parts, "frame", 1, 1, tiled=True)
    keep = lax.dynamic_index_in_dim(both, here_c, 0, keepdims=False)
    send = lax.dynamic_index_in_dim(both, 1 - here_c, 0, keepdims=False)
    came = swap(send, "core")
    out = jnp.stack([jnp.where(here_c == 0, keep, came), jnp.where(here_c == 0, came, keep)], axis=0)
    return out.reshape(team, rows, width)


def spread(count, team):
    rest = count // team
    return [(i, (i % rest) * team + i // rest) for i in range(count)]


def widen(rows, width):
    height, columns = rows.shape
    parts = columns // width
    if parts == 1:
        return rows
    return rows.reshape(height, parts, width).transpose(1, 0, 2).reshape(parts * height, width)


def narrow(stacked, height):
    lead = stacked.shape[:-2]
    parts = stacked.shape[-2] // height
    if parts == 1:
        return stacked
    width = stacked.shape[-1]
    shaped = stacked.reshape(lead + (parts, height, width))
    return jnp.moveaxis(shaped, -3, -2).reshape(lead + (height, parts * width))


def rest_gather(values):
    return lax.all_gather(values, REST, axis=0, tiled=False)


def rest_sum(values):
    return lax.psum_scatter(values, REST, scatter_dimension=0, tiled=False)


def on_device(
    tokens,
    cotangent,
    scene_ids,
    frame_index,
    qkv_weight,
    qkv_bias,
    proj_weight,
    fc1_weight,
    fc1_bias,
    fc2_weight,
    out_bias,
    norm_gain,
    norm_bias,
    layer_scale,
    qk_gain,
    qk_bias,
):
    frames = lax.axis_size("frame")
    team = 2 * frames
    rest = lax.axis_size("outer") * lax.axis_size("inner")
    count = team * rest
    rows, width = tokens.shape
    head_size = qk_gain.shape[-1]
    heads = width // head_size // team
    part = heads * head_size
    hidden_all = fc1_weight.shape[-1]
    hidden = hidden_all // team
    mine = lax.axis_index("core") * frames + lax.axis_index("frame")
    shard_rows = qkv_weight.shape[1]
    fc2_rows = fc2_weight.shape[1]

    small = jnp.concatenate(
        [m.reshape(-1) for m in (qkv_bias, fc1_bias, out_bias, norm_gain, norm_bias, layer_scale)]
    )
    small = lax.all_gather(small, EVERY, axis=0, tiled=False)
    sizes = [m.size for m in (qkv_bias, fc1_bias, out_bias, norm_gain, norm_bias, layer_scale)]
    cuts = np.cumsum([0] + sizes)
    small = [small[:, cuts[i] : cuts[i + 1]].astype(WIDE) for i in range(6)]
    bias_qkv = small[0].reshape(count, 2, -1).transpose(1, 0, 2).reshape(2, 3, team, part)
    bias_qkv = lax.dynamic_index_in_dim(bias_qkv, mine, 2, keepdims=False).reshape(2, 3 * part)
    bias_up = small[1].reshape(rest, team, 2, -1)
    bias_up = lax.dynamic_index_in_dim(bias_up, mine, 1, keepdims=False)
    bias_up = bias_up.transpose(1, 0, 2).reshape(2, hidden)
    out_shift, gains, shifts, scales = (
        m.reshape(count, 2, 2, -1).transpose(1, 2, 0, 3).reshape(2, 2, width) for m in small[2:]
    )

    proj_here = lax.ppermute(proj_weight, EVERY, spread(count, team))
    packs = []
    for depth in range(2):
        qkv_part = exchange_columns(
            qkv_weight[depth].reshape(shard_rows, 3, team, part).transpose(0, 2, 1, 3).reshape(shard_rows, team, 3 * part),
            count,
        ).reshape(team * shard_rows, 3 * part)
        up_part = exchange_columns(
            fc1_weight[depth]
            .reshape(shard_rows, rest, team, hidden // rest)
            .transpose(0, 2, 1, 3)
            .reshape(shard_rows, team, hidden),
            count,
        ).reshape(team * shard_rows, hidden)
        attn_part = jnp.concatenate([qkv_part, widen(proj_here[depth], part)], axis=1)
        down_part = widen(fc2_weight[depth], hidden)
        packs.append(jnp.concatenate([attn_part, up_part, down_part], axis=0))

    unit = team * shard_rows

    def unpack(pack):
        attn, up, down = pack[:, :unit], pack[:, unit : 2 * unit], pack[:, 2 * unit :]
        weight_qkv = attn[..., : 3 * part].reshape(width, 3 * part)
        weight_proj = narrow(attn[..., 3 * part :], shard_rows).reshape(part, width)
        return (
            weight_qkv,
            weight_proj,
            up.reshape(width, hidden),
            narrow(down, fc2_rows).reshape(hidden, width),
        )

    weights = [unpack(rest_gather(packs[depth])) for depth in range(2)]

    ids = scene_ids.reshape(1, rows)
    if frames == 2:
        ids = jnp.concatenate([ids, swap(ids, "frame")], axis=0)
    else:
        ids = lax.all_gather(ids, "frame", axis=0, tiled=True)
    ids = jnp.concatenate([ids, swap(ids, "core")], axis=0).reshape(team * rows)

    stream = tokens.astype(WIDE)
    saved = []
    for depth in range(2):
        weight_qkv, weight_proj, weight_up, weight_down = weights[depth]
        use_frame = depth == 0
        group = FRAME_TOK if use_frame else frames * rows
        unit_one, rate_one = normed(stream)
        first = (unit_one * gains[depth, 0] + shifts[depth, 0]).astype(LOW)
        first = team_gather(first)
        mixed = dot(first, weight_qkv) + bias_qkv[depth]
        gain_head, shift_head = qk_gain[depth].astype(WIDE), qk_bias[depth].astype(WIDE)
        unit_q, rate_q = normed(head_split(mixed[:, :part], heads))
        unit_k, rate_k = normed(head_split(mixed[:, part : 2 * part], heads))
        queries = (unit_q * gain_head[0] + shift_head[0]).astype(LOW)
        keys = (unit_k * gain_head[1] + shift_head[1]).astype(LOW)
        values = head_split(mixed[:, 2 * part :], heads).astype(LOW)
        attended, log_sum = attend(queries, keys, values, ids, use_frame, group)
        attended = attended.astype(LOW)
        branch_one = team_sum(dot(attended, weight_proj)) + out_shift[depth, 0]
        middle = stream + scales[depth, 0] * branch_one
        unit_two, rate_two = normed(middle)
        second = team_gather((unit_two * gains[depth, 1] + shifts[depth, 1]).astype(LOW))
        pre_act = dot(second, weight_up) + bias_up[depth]
        act = exact_gelu(pre_act).astype(LOW)
        branch_two = team_sum(dot(act, weight_down)) + out_shift[depth, 1]
        stream = middle + scales[depth, 1] * branch_two
        saved.append(
            (
                unit_one, rate_one, first, unit_q, rate_q, unit_k, rate_k, queries, keys, values,
                log_sum, attended, branch_one, unit_two, rate_two, second, pre_act, act, branch_two,
            )
        )

    grad = cotangent.astype(WIDE)
    sums = [None, None]
    pieces = [None, None]
    head_sums = [None, None]
    for depth in (1, 0):
        weight_qkv, weight_proj, weight_up, weight_down = weights[depth]
        use_frame = depth == 0
        group = FRAME_TOK if use_frame else frames * rows
        (
            unit_one, rate_one, first, unit_q, rate_q, unit_k, rate_k, queries, keys, values,
            log_sum, attended, branch_one, unit_two, rate_two, second, pre_act, act, branch_two,
        ) = saved[depth]
        scale_two = jnp.sum(grad * branch_two, axis=0)
        grad_branch = grad * scales[depth, 1]
        shift_two = jnp.sum(grad_branch, axis=0)
        branch_low = team_gather(grad_branch.astype(LOW))
        grad_down = dot_tn(act, branch_low).astype(LOW)
        grad_act = dot_nt(branch_low, weight_down)
        _, gelu_back = jax.vjp(exact_gelu, pre_act)
        grad_pre = gelu_back(grad_act)[0]
        sum_up = jnp.sum(grad_pre, axis=0)
        pre_low = grad_pre.astype(LOW)
        grad_up = dot_tn(second, pre_low).astype(LOW)
        grad_second = team_sum(dot_nt(pre_low, weight_up))
        gain_two = jnp.sum(grad_second * unit_two, axis=0)
        norm_shift_two = jnp.sum(grad_second, axis=0)
        grad_middle = grad + normed_back(grad_second, unit_two, rate_two, gains[depth, 1])
        scale_one = jnp.sum(grad_middle * branch_one, axis=0)
        grad_att = grad_middle * scales[depth, 0]
        shift_one = jnp.sum(grad_att, axis=0)
        att_low = team_gather(grad_att.astype(LOW))
        grad_proj = dot_tn(attended, att_low).astype(LOW)
        grad_flat = dot_nt(att_low, weight_proj).astype(LOW)
        grad_q, grad_k, grad_v = attend_back(
            queries, keys, values, ids, use_frame, group, log_sum, head_split(grad_flat, heads)
        )
        gain_head = qk_gain[depth].astype(WIDE)
        head_gain = jnp.stack(
            [jnp.sum(grad_q * unit_q, axis=(0, 1)), jnp.sum(grad_k * unit_k, axis=(0, 1))]
        )
        head_shift = jnp.stack([jnp.sum(grad_q, axis=(0, 1)), jnp.sum(grad_k, axis=(0, 1))])
        mixed_q = normed_back(grad_q, unit_q, rate_q, gain_head[0])
        mixed_k = normed_back(grad_k, unit_k, rate_k, gain_head[1])
        grad_mixed = jnp.concatenate(
            [m.reshape(team * rows, part) for m in (mixed_q, mixed_k, grad_v)], axis=1
        )
        sum_qkv = jnp.sum(grad_mixed, axis=0)
        mixed_low = grad_mixed.astype(LOW)
        grad_qkv = dot_tn(first, mixed_low).astype(LOW)
        grad_first = team_sum(dot_nt(mixed_low, weight_qkv))
        gain_one = jnp.sum(grad_first * unit_one, axis=0)
        norm_shift_one = jnp.sum(grad_first, axis=0)
        grad = grad_middle + normed_back(grad_first, unit_one, rate_one, gains[depth, 0])

        proj_wide = grad_proj.reshape(rest, shard_rows, team, part).transpose(0, 2, 1, 3)
        attn_pack = jnp.concatenate(
            [grad_qkv.reshape(rest, unit, 3 * part), proj_wide.reshape(rest, unit, part)], axis=2
        )
        down_wide = grad_down.reshape(rest, fc2_rows, width // hidden, hidden).transpose(0, 2, 1, 3)
        pack = jnp.concatenate(
            [attn_pack, grad_up.reshape(rest, unit, hidden), down_wide.reshape(rest, -1, hidden)], axis=1
        )
        pack = rest_sum(pack)
        attn, up, down = pack[:unit], pack[unit : 2 * unit], pack[2 * unit :]
        proj_mine = narrow(attn[:, 3 * part :], shard_rows)
        down_mine = narrow(down, fc2_rows)
        qkv_mine = exchange_columns(
            attn[:, : 3 * part].reshape(team, shard_rows, 3 * part).transpose(1, 0, 2), count
        )
        qkv_mine = (
            qkv_mine.reshape(team, shard_rows, 3, part).transpose(1, 2, 0, 3).reshape(shard_rows, -1)
        )
        up_mine = exchange_columns(up.reshape(team, shard_rows, hidden).transpose(1, 0, 2), count)
        up_mine = (
            up_mine.reshape(team, shard_rows, rest, hidden // rest)
            .transpose(1, 2, 0, 3)
            .reshape(shard_rows, -1)
        )
        pieces[depth] = (qkv_mine, proj_mine, up_mine, down_mine)
        full_qkv = jnp.zeros((3, team, part), WIDE)
        full_qkv = lax.dynamic_update_slice(full_qkv, sum_qkv.reshape(3, 1, part), (0, mine, 0))
        full_up = jnp.zeros((rest, team, hidden // rest), WIDE)
        full_up = lax.dynamic_update_slice(full_up, sum_up.reshape(rest, 1, hidden // rest), (0, mine, 0))
        vectors = jnp.stack(
            [shift_one, shift_two, gain_one, gain_two, norm_shift_one, norm_shift_two, scale_one, scale_two]
        )
        sums[depth] = jnp.concatenate(
            [
                full_qkv.reshape(count, -1),
                full_up.reshape(count, -1),
                vectors.reshape(8, count, -1).transpose(1, 0, 2).reshape(count, -1),
            ],
            axis=1,
        )
        head_sums[depth] = jnp.stack([head_gain, head_shift])

    summed = lax.psum_scatter(jnp.concatenate(sums, axis=1), EVERY, scatter_dimension=0, tiled=False)
    summed = summed.reshape(2, -1)
    n_qkv, n_up = qkv_bias.shape[1], fc1_bias.shape[1]
    grad_bias_qkv = summed[:, :n_qkv]
    grad_bias_up = summed[:, n_qkv : n_qkv + n_up]
    vectors = summed[:, n_qkv + n_up :].reshape(2, 4, 2, -1)
    head_all = lax.psum(jnp.stack(head_sums), EVERY)
    proj_grad = lax.ppermute(
        jnp.stack([pieces[0][1], pieces[1][1]]), EVERY, [(b, a) for a, b in spread(count, team)]
    )

    def both(member):
        return jnp.stack([pieces[0][member], pieces[1][member]]).astype(WIDE)

    return (
        stream.astype(LOW),
        grad.astype(LOW),
        both(0),
        grad_bias_qkv,
        proj_grad.astype(WIDE),
        both(2),
        grad_bias_up,
        both(3),
        vectors[:, 0],
        vectors[:, 1],
        vectors[:, 2],
        vectors[:, 3],
        head_all[:, 0],
        head_all[:, 1],
    )


def solution(mesh):
    scenes, frames = mesh.shape["scene"], mesh.shape["frame"]
    rest = scenes // 2
    outer = 4 if rest % 4 == 0 else rest
    grid = Mesh(mesh.devices.reshape(outer, rest // outer, 2, frames), EVERY)
    by_rows = P(EVERY, None)
    second = P(None, EVERY)
    second_rows = P(None, EVERY, None)
    last = P(None, None, EVERY)
    return jax.shard_map(
        on_device,
        mesh=grid,
        in_specs=(
            by_rows, by_rows, P(EVERY), P(EVERY), second_rows, second, second_rows, second_rows,
            second, second_rows, last, last, last, last, P(), P(),
        ),
        out_specs=(
            by_rows, by_rows, second_rows, second, second_rows, second_rows, second, second_rows,
            last, last, last, last, P(), P(),
        ),
        check_vma=False,
    )
```

```python
import jax
import jax.numpy as jnp
import numpy as np
from jax import lax
from jax.experimental import pallas as pl
from jax.experimental.pallas import tpu as pltpu
from jax.sharding import Mesh
from jax.sharding import PartitionSpec as P

EPSILON = 1e-06
FRAME_TOK = 64
LOW = jnp.bfloat16
WIDE = jnp.float32
EVERY = ("outer", "inner", "core", "frame")
REST = ("outer", "inner")
TEAM = ("core", "frame")
HIGHEST = lax.Precision.HIGHEST
ROOT_HALF = 0.7071067811865476
ROOT_TWO_PI = 0.3989422804014327
VMEM_LIMIT = 56 * 1024 * 1024
OUT, GAIN, SHIFT, SCALE = 0, 4, 8, 12


def dot(left, right):
    return jnp.dot(left, right, preferred_element_type=WIDE)


def dot_tn(left, right):
    return lax.dot_general(left, right, (((0,), (0,)), ((), ())), preferred_element_type=WIDE)


def dot_nt(left, right):
    return lax.dot_general(left, right, (((1,), (1,)), ((), ())), preferred_element_type=WIDE)


def normed(values):
    center = values - jnp.mean(values, axis=-1, keepdims=True)
    rate = lax.rsqrt(jnp.mean(center * center, axis=-1, keepdims=True) + EPSILON)
    return center * rate, rate


def normed_back(grad, unit, rate, gain):
    inner = grad * gain
    mean_one = jnp.mean(inner, axis=-1, keepdims=True)
    mean_two = jnp.mean(inner * unit, axis=-1, keepdims=True)
    return rate * (inner - mean_one - unit * mean_two)


def shape_of(shape, dtype):
    return jax.ShapeDtypeStruct(shape, dtype)


def call(kernel, outs, args, name, flops=0, scratch=(), specs=None, scalars=0):
    vmem = pl.BlockSpec(memory_space=pltpu.VMEM)
    smem = pl.BlockSpec(memory_space=pltpu.SMEM)
    specs = specs or {}
    in_specs = [smem if i < scalars else specs.get(i, vmem) for i in range(len(args))]
    bytes_all = sum(m.size * m.dtype.itemsize for m in args)
    bytes_all += sum(int(np.prod(s.shape)) * s.dtype.itemsize for s in outs)
    return pl.pallas_call(
        kernel,
        out_shape=list(outs),
        in_specs=in_specs,
        out_specs=[vmem] * len(outs),
        scratch_shapes=list(scratch),
        compiler_params=pltpu.CompilerParams(vmem_limit_bytes=VMEM_LIMIT),
        cost_estimate=pl.CostEstimate(flops=flops, bytes_accessed=bytes_all, transcendentals=0),
        name=name,
    )(*args)


def swap(values, axis):
    return lax.ppermute(values, axis, [(0, 1), (1, 0)])


def cross(values):
    return lax.ppermute(values, TEAM, [(0, 3), (1, 2), (2, 1), (3, 0)])


def team_gather(values):
    if lax.axis_size("frame") == 2:
        far = swap(values, "frame")
        near = swap(values, "core")
        return [values, far, near, swap(far, "core")]
    both = lax.all_gather(values, "frame", axis=0, tiled=True)
    return [both, swap(both, "core")]


def team_sum(own, peer):
    if lax.axis_size("frame") == 2:
        far = own[1] + swap(peer[1], "core").astype(WIDE)
        came = swap(far.astype(LOW), "frame")
        return [own[0], swap(peer[0], "core"), came]
    total = own[0] + swap(peer[0], "core").astype(WIDE)
    return [lax.psum_scatter(total.astype(LOW), "frame", scatter_dimension=0, tiled=True).astype(WIDE)]


def exchange_columns(values):
    parts = values.transpose(1, 0, 2)
    frames = lax.axis_size("frame")
    parts = parts.reshape((2, frames) + parts.shape[1:])
    both = lax.all_to_all(parts, "frame", 1, 1, tiled=True)
    here = lax.axis_index("core")
    keep = lax.dynamic_index_in_dim(both, here, 0, keepdims=False)
    came = swap(lax.dynamic_index_in_dim(both, 1 - here, 0, keepdims=False), "core")
    out = jnp.stack([jnp.where(here == 0, keep, came), jnp.where(here == 0, came, keep)], axis=0)
    return out.reshape((2 * frames,) + out.shape[2:])


def split_weights(qkv, up, part, rest, me):
    rows = qkv.shape[0]
    width, hidden_all = qkv.shape[1] // 3, up.shape[1]
    lanes = hidden_all // 4 // rest

    def kernel(me_ref, qkv_ref, up_ref, *outs):
        for away, out in enumerate(outs):
            member = jnp.bitwise_xor(me_ref[0], away)
            for s in range(3):
                start = pl.multiple_of(s * width + member * part, 128)
                out[:, s * part : (s + 1) * part] = qkv_ref[:, pl.ds(start, part)]
            for f in range(rest):
                start = pl.multiple_of((f * 4 + member) * lanes, 128)
                at = 3 * part + f * lanes
                out[:, at : at + lanes] = up_ref[:, pl.ds(start, lanes)]

    out = shape_of((rows, 3 * part + hidden_all // 4), qkv.dtype)
    return call(kernel, [out] * 4, [me, qkv, up], "split_weights", scalars=1)


def pack_weights(pieces, proj, part, me):
    rows = proj.shape[0]
    hidden = pieces[0].shape[1] - 3 * part

    def kernel(me_ref, p0, p1, p2, p3, proj_ref, attn, up):
        for away, ref in enumerate((p0, p1, p2, p3)):
            member = jnp.bitwise_xor(me_ref[0], away)
            start = pl.multiple_of(member * rows, rows)
            attn[pl.ds(start, rows), : 3 * part] = ref[:, : 3 * part]
            up[pl.ds(start, rows), :] = ref[:, 3 * part :]
        for j in range(4):
            attn[j * rows : (j + 1) * rows, 3 * part :] = proj_ref[:, j * part : (j + 1) * part]

    outs = [shape_of((4 * rows, 4 * part), LOW), shape_of((4 * rows, hidden), LOW)]
    return call(kernel, outs, [me, *pieces, proj], "pack_weights", scalars=1)


def spread(count, team):
    rest = count // team
    return [(i, (i % rest) * team + i // rest) for i in range(count)]


def widen(rows, width):
    height, columns = rows.shape
    parts = columns // width
    if parts == 1:
        return rows
    return rows.reshape(height, parts, width).transpose(1, 0, 2).reshape(parts * height, width)


def narrow(stacked, height):
    lead = stacked.shape[:-2]
    parts = stacked.shape[-2] // height
    if parts == 1:
        return stacked
    width = stacked.shape[-1]
    shaped = stacked.reshape(lead + (parts, height, width))
    return jnp.moveaxis(shaped, -3, -2).reshape(lead + (height, parts * width))


def ring_order(outer, inner):
    order = []
    for a in range(outer):
        row = range(1, inner) if a % 2 == 0 else range(inner - 1, 0, -1)
        order += [a * inner + b for b in row]
    return order + [a * inner for a in range(outer - 1, -1, -1)]


def ring_table():
    outer, inner = lax.axis_size("outer"), lax.axis_size("inner")
    order = ring_order(outer, inner)
    rest = outer * inner
    place = {team: i for i, team in enumerate(order)}
    table = np.array(
        [
            [[order[(place[f] + sign * k) % rest] for k in range(rest)] for sign in (-1, 1)]
            for f in range(rest)
        ],
        np.int32,
    )
    here = lax.axis_index("outer") * inner + lax.axis_index("inner")
    return lax.dynamic_index_in_dim(jnp.asarray(table), here, 0, keepdims=False)


def ring_shift(values, sign):
    order = ring_order(lax.axis_size("outer"), lax.axis_size("inner"))
    rest = len(order)
    return lax.ppermute(values, REST, [(order[i], order[(i + sign) % rest]) for i in range(rest)])


def ring_step(low_half, high_half):
    low_half, high_half = ring_shift(low_half, 1), ring_shift(high_half, -1)
    return lax.optimization_barrier((low_half, high_half))


def ring_gather(low_half, high_half, table, joined):
    rest = table.shape[1]
    rows, columns = low_half.shape
    back, ahead = [low_half], [high_half]
    for _ in range(rest - 1):
        low_half, high_half = ring_step(low_half, high_half)
        back.append(low_half)
        ahead.append(high_half)

    def kernel(table_ref, *refs):
        outs = refs[2 * rest :]
        for k in range(rest):
            if joined:
                outs[0][table_ref[0, k], :rows, :] = refs[k][...]
                outs[0][table_ref[1, k], rows:, :] = refs[rest + k][...]
            else:
                outs[0][table_ref[0, k], :, :] = refs[k][...]
                outs[1][table_ref[1, k], :, :] = refs[rest + k][...]

    if joined:
        outs = [shape_of((rest, 2 * rows, columns), LOW)]
    else:
        outs = [shape_of((rest, rows, columns), LOW)] * 2
    return call(kernel, outs, [table, *back, *ahead], "assemble", scalars=1)


def ring_sum(low_parts, high_parts, table, joined):
    rest = table.shape[1]
    _, rows, columns = low_parts.shape
    rows = rows // 2 if joined else rows

    def step(k, came):
        last = k == rest
        dtype = WIDE if last else LOW

        def kernel(table_ref, *refs):
            ins, outs = refs[: len(refs) - 2], refs[len(refs) - 2 :]
            for i in range(2):
                value = ins[i][0]
                if came:
                    value = (value.astype(WIDE) + ins[2 + i][...].astype(WIDE)).astype(dtype)
                outs[i][...] = value

        whole = pl.BlockSpec((rows, columns), lambda i, t: (0, 0))
        grid_spec = pltpu.PrefetchScalarGridSpec(
            num_scalar_prefetch=1,
            grid=(1,),
            in_specs=[
                pl.BlockSpec((1, rows, columns), lambda i, t: (t[0, k % rest], 0, 0)),
                pl.BlockSpec(
                    (1, rows, columns), lambda i, t: (t[1, k % rest], 1 if joined else 0, 0)
                ),
            ]
            + [whole] * len(came),
            out_specs=[whole, whole],
        )
        return pl.pallas_call(
            kernel,
            grid_spec=grid_spec,
            out_shape=[shape_of((rows, columns), dtype)] * 2,
            cost_estimate=pl.CostEstimate(
                flops=0, bytes_accessed=12 * rows * columns, transcendentals=0
            ),
            name="ring_add",
        )(table, low_parts, high_parts, *came)

    came = step(1, [])
    for k in range(2, rest + 1):
        came = step(k, ring_step(*came))
    return came


def small_gather(values):
    out = values[None]
    for axis in ("frame", "core", "inner", "outer"):
        size, here, step = lax.axis_size(axis), lax.axis_index(axis), 1
        while step < size:
            came = lax.ppermute(out, axis, [(i, i ^ step) for i in range(size)])
            first = (here & step) == 0
            out = jnp.concatenate([jnp.where(first, out, came), jnp.where(first, came, out)], axis=0)
            step *= 2
    return out


def small_sum(split, common):
    for axis in ("outer", "inner"):
        size, here = lax.axis_size(axis), lax.axis_index(axis)
        step = size // 2
        while step >= 1:
            half = split.shape[1] // 2
            bit = (here // step) % 2
            keep = lax.dynamic_slice_in_dim(split, bit * half, half, 1)
            send = lax.dynamic_slice_in_dim(split, (1 - bit) * half, half, 1)
            pairs = [(i, i ^ step) for i in range(size)]
            packed = jnp.concatenate([send.reshape(-1), common.reshape(-1)])
            came = lax.ppermute(packed, axis, pairs)
            split = keep + came[: keep.size].reshape(keep.shape)
            common = common + came[keep.size :].reshape(common.shape)
            step //= 2
    return split, common


def head_means(part, head_size):
    row = lax.broadcasted_iota(jnp.int32, (part, part), 0) // head_size
    column = lax.broadcasted_iota(jnp.int32, (part, part), 1) // head_size
    return jnp.where(row == column, 1.0 / head_size, 0.0).astype(WIDE)


def head_mean(values, matrix):
    return jnp.dot(values, matrix, precision=HIGHEST, preferred_element_type=WIDE)


def head_normed(values, matrix):
    center = values - head_mean(values, matrix)
    rate = lax.rsqrt(head_mean(center * center, matrix) + EPSILON)
    return center * rate, rate


def join(refs, out_ref):
    start = 0
    for ref in refs:
        out_ref[start : start + ref.shape[0], :] = ref[...]
        start += ref.shape[0]


def spans(refs):
    start = 0
    for ref in refs:
        yield start, start + ref.shape[0], ref
        start += ref.shape[0]


def flat_rows(ref, first, height, columns):
    block = ref[:, first : first + height, columns]
    return block.reshape(block.shape[0] * height, block.shape[2])


def tiles_of(total, group, block):
    for base in range(0, total, group):
        for start in range(base, base + group, block):
            yield start, base


def allowed_of(ids_col, ids_row, start, base, block, group, use_frame):
    if use_frame:
        row = lax.broadcasted_iota(jnp.int32, (block, group), 0) // FRAME_TOK
        column = lax.broadcasted_iota(jnp.int32, (block, group), 1) // FRAME_TOK
        return row == column
    return ids_col[start : start + block, :] == ids_row[:, base : base + group]


def plan(frames, rows, use_frame):
    group = 2 * FRAME_TOK if use_frame else frames * rows
    return group, min(group, 256)


def part_shapes(pieces, width):
    half = len(pieces) // 2
    return [shape_of((m.shape[0], width), WIDE if i < half else LOW) for i, m in enumerate(pieces)]


def attn_forward(pieces, weights, bias, head_gain, head_shift, ids, head_size, frames, use_frame):
    attn, proj, height, wide = weights
    rest, unit, _ = attn.shape
    width, part = rest * unit, head_gain.shape[-1]
    total = sum(m.shape[0] for m in pieces)
    count = len(pieces)
    group, block = plan(frames, total // (2 * frames), use_frame)
    lanes = min(128, part)
    per = lanes // head_size
    scale = head_size ** (-0.5)

    def kernel(*refs):
        piece_refs = refs[:count]
        wq, wp, bias_ref, gain_ref, shift_ref, ids_col, ids_row = refs[count : count + 7]
        first, raw, qkv, lse, flat = refs[count + 7 : count + 12]
        outs = refs[count + 12 :]
        join(piece_refs, first)
        matrix = head_means(part, head_size)
        mixed = dot(first[...], flat_rows(wq, 0, unit, slice(0, 3 * part))) + bias_ref[...]
        raw[...] = mixed[:, : 2 * part]
        for i in range(2):
            unit_i, _ = head_normed(mixed[:, i * part : (i + 1) * part], matrix)
            value = unit_i * gain_ref[i : i + 1, :] + shift_ref[i : i + 1, :]
            qkv[:, i * part : (i + 1) * part] = value.astype(LOW)
        qkv[:, 2 * part :] = mixed[:, 2 * part :].astype(LOW)
        place = lax.broadcasted_iota(jnp.int32, (1, lanes), 1) // head_size
        for start, base in tiles_of(total, group, block):
            allowed = allowed_of(ids_col, ids_row, start, base, block, group, use_frame)
            stats = []
            for lane in range(0, part, lanes):
                query = qkv[start : start + block, lane : lane + lanes] * jnp.asarray(scale, LOW)
                key = qkv[base : base + group, part + lane : part + lane + lanes]
                value = qkv[base : base + group, 2 * part + lane : 2 * part + lane + lanes]
                out = jnp.zeros((block, lanes), WIDE)
                for h in range(per):
                    mask = place == h
                    scores = dot_nt(jnp.where(mask, query, jnp.zeros_like(query)), key)
                    scores = jnp.where(allowed, scores, -jnp.inf)
                    top = jnp.max(scores, axis=-1, keepdims=True)
                    weight = jnp.exp(scores - top)
                    norm = jnp.sum(weight, axis=-1, keepdims=True)
                    stats.append(top + jnp.log(norm))
                    probs = (weight * (1.0 / norm)).astype(LOW)
                    out = jnp.where(mask, dot(probs, value), out)
                flat[start : start + block, lane : lane + lanes] = out.astype(LOW)
            lse[start : start + block, :] = jnp.concatenate(stats, axis=1)
        for a in range(0, width, wide):
            b = a + wide
            chunk = flat_rows(wp, a // wide * height, height, slice(wp.shape[2] - wide, wp.shape[2]))
            for start, stop, ref in spans(outs):
                ref[:, a:b] = dot(flat[start:stop, :], chunk).astype(ref.dtype)

    outs = [
        shape_of((total, width), LOW),
        shape_of((total, 2 * part), WIDE),
        shape_of((total, 3 * part), LOW),
        shape_of((total, part // head_size), WIDE),
        shape_of((total, part), LOW),
    ] + part_shapes(pieces, width)
    args = list(pieces) + [attn, proj, bias, head_gain, head_shift, ids.reshape(-1, 1), ids.reshape(1, -1)]
    flops = 2 * total * (width * 4 * part + group * 2 * part)
    res = call(kernel, outs, args, "attn_forward", flops)
    return res[:5], res[5 : 5 + count // 2], res[5 + count // 2 :]


def attn_backward(pieces, weights, head_gain, kept, ids, head_size, frames, use_frame):
    _, raw, qkv, lse, _ = kept
    attn, proj, height, wide = weights
    rest, unit, _ = attn.shape
    width, part = rest * unit, head_gain.shape[-1]
    total = sum(m.shape[0] for m in pieces)
    count = len(pieces)
    group, block = plan(frames, total // (2 * frames), use_frame)
    lanes = min(128, part)
    per = lanes // head_size
    scale = head_size ** (-0.5)

    def kernel(*refs):
        piece_refs = refs[:count]
        wq, wp, gain_ref, raw_ref, qkv_ref, lse_ref, ids_col, ids_row = refs[count : count + 8]
        joined, low_mixed, sums, head_sums = refs[count + 8 : count + 12]
        outs = refs[count + 12 : count + 12 + count]
        grad_out, grad_three = refs[count + 12 + count :]
        join(piece_refs, joined)
        grad_flat = jnp.zeros((total, part), WIDE)
        for a in range(0, width, wide):
            b = a + wide
            chunk = flat_rows(wp, a // wide * height, height, slice(wp.shape[2] - wide, wp.shape[2]))
            grad_flat += dot_nt(joined[:, a:b], chunk)
        grad_out[...] = grad_flat.astype(LOW)
        place = lax.broadcasted_iota(jnp.int32, (1, lanes), 1) // head_size
        for start, base in tiles_of(total, group, block):
            allowed = allowed_of(ids_col, ids_row, start, base, block, group, use_frame)
            stats = lse_ref[start : start + block, :]
            for lane in range(0, part, lanes):
                query = qkv_ref[start : start + block, lane : lane + lanes] * jnp.asarray(scale, LOW)
                key = qkv_ref[base : base + group, part + lane : part + lane + lanes]
                value = qkv_ref[base : base + group, 2 * part + lane : 2 * part + lane + lanes]
                grad_here = grad_out[start : start + block, lane : lane + lanes]
                grad_q = jnp.zeros((block, lanes), WIDE)
                grad_k = jnp.zeros((group, lanes), WIDE)
                grad_v = jnp.zeros((group, lanes), WIDE)
                for h in range(per):
                    mask = place == h
                    head = lane // head_size + h
                    scores = dot_nt(jnp.where(mask, query, jnp.zeros_like(query)), key)
                    probs = jnp.exp(jnp.where(allowed, scores - stats[:, head : head + 1], -jnp.inf))
                    grad_p = dot_nt(jnp.where(mask, grad_here, jnp.zeros_like(grad_here)), value)
                    delta = jnp.sum(probs * grad_p, axis=-1, keepdims=True)
                    grad_s = (probs * (grad_p - delta)).astype(LOW)
                    grad_q = jnp.where(mask, dot(grad_s, key), grad_q)
                    grad_k = jnp.where(mask, dot_tn(grad_s, query), grad_k)
                    grad_v = jnp.where(mask, dot_tn(probs.astype(LOW), grad_here), grad_v)
                grad_three[start : start + block, lane : lane + lanes] = grad_q * scale
                for at, grad in ((part, grad_k), (2 * part, grad_v)):
                    spot = (slice(base, base + group), slice(at + lane, at + lane + lanes))
                    if start == base:
                        grad_three[spot] = grad
                    else:
                        grad_three[spot] = grad_three[spot] + grad
        matrix = head_means(part, head_size)
        for i in range(2):
            here = slice(i * part, (i + 1) * part)
            grad = grad_three[:, here]
            unit_i, rate = head_normed(raw_ref[:, here], matrix)
            head_sums[i : i + 1, :] = jnp.sum(grad * unit_i, axis=0, keepdims=True)
            head_sums[2 + i : 3 + i, :] = jnp.sum(grad, axis=0, keepdims=True)
            inner = grad * gain_ref[i : i + 1, :]
            mean_one = head_mean(inner, matrix)
            mean_two = head_mean(inner * unit_i, matrix)
            result = rate * (inner - mean_one - unit_i * mean_two)
            sums[:, here] = jnp.sum(result, axis=0, keepdims=True)
            low_mixed[:, here] = result.astype(LOW)
        result = grad_three[:, 2 * part :]
        sums[:, 2 * part :] = jnp.sum(result, axis=0, keepdims=True)
        low_mixed[:, 2 * part :] = result.astype(LOW)
        weight = flat_rows(wq, 0, unit, slice(0, 3 * part))
        for start, stop, ref in spans(outs):
            ref[...] = dot_nt(low_mixed[start:stop, :], weight).astype(ref.dtype)

    outs = [
        shape_of((total, width), LOW),
        shape_of((total, 3 * part), LOW),
        shape_of((1, 3 * part), WIDE),
        shape_of((4, part), WIDE),
    ] + part_shapes(pieces, width)
    scratch = [pltpu.VMEM((total, part), LOW), pltpu.VMEM((total, 3 * part), WIDE)]
    args = list(pieces) + [attn, proj, head_gain, raw, qkv, lse, ids.reshape(-1, 1), ids.reshape(1, -1)]
    flops = 2 * total * (width * 4 * part + group * 5 * part)
    res = call(kernel, outs, args, "attn_backward", flops, scratch)
    return res[:4], res[4 : 4 + count // 2], res[4 + count // 2 :]


def attn_weight_grads(first, low_mixed, flat, att_low, rest, height):
    width, part = first.shape[1], flat.shape[1]
    unit = width // rest
    wide = width * height // unit

    def kernel(first_ref, mixed_ref, flat_ref, att_ref, out):
        product = dot_tn(first_ref[...], mixed_ref[...]).astype(LOW)
        out[:, :, : 3 * part] = product.reshape(rest, unit, 3 * part)
        product = dot_tn(flat_ref[...], att_ref[...]).astype(LOW)
        for j in range(unit // height):
            chunk = product[:, j * wide : (j + 1) * wide].reshape(rest, height, wide)
            out[:, j * height : (j + 1) * height, 3 * part :] = chunk

    flops = 8 * first.shape[0] * width * part
    out = shape_of((rest, unit, 4 * part), LOW)
    return call(kernel, [out], [first, low_mixed, flat, att_low], "attn_weight_grads", flops)[0]


def mlp_forward(pieces, weight_up, weight_down, bias):
    rest, unit, hidden = weight_up.shape
    width = rest * unit
    total = sum(m.shape[0] for m in pieces)
    count = len(pieces)

    def kernel(*refs):
        piece_refs = refs[:count]
        up, down, bias_ref = refs[count : count + 3]
        second, act, slope = refs[count + 3 : count + 6]
        outs = refs[count + 6 :]
        join(piece_refs, second)
        pre = dot(second[...], flat_rows(up, 0, unit, slice(None))) + bias_ref[...]
        below = 0.5 * (1.0 + lax.erf(pre * ROOT_HALF))
        act[...] = (pre * below).astype(LOW)
        slope[...] = (below + pre * (ROOT_TWO_PI * jnp.exp(-0.5 * pre * pre))).astype(LOW)
        weight = flat_rows(down, 0, down.shape[1], slice(None))
        for start, stop, ref in spans(outs):
            ref[...] = dot(act[start:stop, :], weight).astype(ref.dtype)

    outs = [
        shape_of((total, width), LOW),
        shape_of((total, hidden), LOW),
        shape_of((total, hidden), LOW),
    ] + part_shapes(pieces, width)
    args = list(pieces) + [weight_up, weight_down, bias]
    res = call(kernel, outs, args, "mlp_forward", 4 * total * width * hidden)
    return res[:3], res[3 : 3 + count // 2], res[3 + count // 2 :]


def mlp_backward(pieces, weight_up, weight_down, slope):
    rest, unit, hidden = weight_up.shape
    width = rest * unit
    total = sum(m.shape[0] for m in pieces)
    count = len(pieces)

    def kernel(*refs):
        piece_refs = refs[:count]
        up, down, slope_ref = refs[count : count + 3]
        joined, low_pre, sums = refs[count + 3 : count + 6]
        outs = refs[count + 6 :]
        join(piece_refs, joined)
        weight = flat_rows(down, 0, down.shape[1], slice(None))
        grad = dot_nt(joined[...], weight) * slope_ref[...].astype(WIDE)
        sums[...] = jnp.sum(grad, axis=0, keepdims=True)
        low_pre[...] = grad.astype(LOW)
        weight = flat_rows(up, 0, unit, slice(None))
        for start, stop, ref in spans(outs):
            ref[...] = dot_nt(low_pre[start:stop, :], weight).astype(ref.dtype)

    outs = [
        shape_of((total, width), LOW),
        shape_of((total, hidden), LOW),
        shape_of((1, hidden), WIDE),
    ] + part_shapes(pieces, width)
    args = list(pieces) + [weight_up, weight_down, slope]
    res = call(kernel, outs, args, "mlp_backward", 4 * total * width * hidden)
    return res[:3], res[3 : 3 + count // 2], res[3 + count // 2 :]


def added(refs):
    total = refs[0][...]
    for ref in refs[1:]:
        total = total + ref[...].astype(WIDE)
    return total


def row_of(vectors, kind, depth, which):
    at = kind + 2 * depth + which
    return vectors[at : at + 1, :]


def first_norm(tokens, vectors):
    def kernel(tokens_ref, vec, low):
        unit, _ = normed(tokens_ref[...].astype(WIDE))
        low[...] = (unit * row_of(vec, GAIN, 0, 0) + row_of(vec, SHIFT, 0, 0)).astype(LOW)

    return call(kernel, [shape_of(tokens.shape, LOW)], [tokens, vectors], "first_norm")[0]


def branch_norm(stream, terms, vectors, depth, which):
    after = (depth, 1) if which == 0 else (depth + 1, 0)

    def kernel(stream_ref, *refs):
        (vec, branch, result, low), term_refs = refs[-4:], refs[:-4]
        value = added(term_refs) + row_of(vec, OUT, depth, which)
        branch[...] = value
        value = stream_ref[...].astype(WIDE) + row_of(vec, SCALE, depth, which) * value
        result[...] = value
        unit, _ = normed(value)
        low[...] = (unit * row_of(vec, GAIN, *after) + row_of(vec, SHIFT, *after)).astype(LOW)

    outs = [shape_of(stream.shape, WIDE), shape_of(stream.shape, WIDE), shape_of(stream.shape, LOW)]
    return call(kernel, outs, [stream, *terms, vectors], "branch_norm")


def turn(middle, terms, cotangent, vectors):
    def kernel(middle_ref, *refs):
        (cot, vec, result, low, sums), term_refs = refs[-5:], refs[:-5]
        branch = added(term_refs) + row_of(vec, OUT, 1, 1)
        scale = row_of(vec, SCALE, 1, 1)
        result[...] = (middle_ref[...] + scale * branch).astype(LOW)
        grad = cot[...].astype(WIDE)
        grad_branch = grad * scale
        low[...] = grad_branch.astype(LOW)
        sums[0:1, :] = jnp.sum(grad * branch, axis=0, keepdims=True)
        sums[1:2, :] = jnp.sum(grad_branch, axis=0, keepdims=True)

    shape = middle.shape
    outs = [shape_of(shape, LOW), shape_of(shape, LOW), shape_of((2, shape[1]), WIDE)]
    return call(kernel, outs, [middle, *terms, cotangent, vectors], "turn")


def norm_back(grad, terms, stream, branch, vectors, depth, which, before):
    def kernel(*refs):
        grad_ref, stream_ref, vec = refs[0], refs[1], refs[2]
        inputs = 4 if before else 3
        term_refs = refs[inputs : inputs + len(terms)]
        result, low, sums = (refs[inputs + len(terms) :] + (None,))[:3] if before else (
            None, refs[inputs + len(terms)], refs[inputs + len(terms) + 1],
        )
        came = added(term_refs)
        unit, rate = normed(stream_ref[...].astype(WIDE))
        sums[0:1, :] = jnp.sum(came * unit, axis=0, keepdims=True)
        sums[1:2, :] = jnp.sum(came, axis=0, keepdims=True)
        value = grad_ref[...].astype(WIDE)
        value = value + normed_back(came, unit, rate, row_of(vec, GAIN, depth, which))
        if not before:
            low[...] = value.astype(LOW)
            return
        result[...] = value
        sums[2:3, :] = jnp.sum(value * refs[3][...], axis=0, keepdims=True)
        value = value * row_of(vec, SCALE, *before)
        sums[3:4, :] = jnp.sum(value, axis=0, keepdims=True)
        low[...] = value.astype(LOW)

    shape = grad.shape
    outs = [shape_of(shape, LOW), shape_of((4 if before else 2, shape[1]), WIDE)]
    args = [grad, stream, vectors]
    if before:
        outs = [shape_of(shape, WIDE)] + outs
        args = args + [branch]
    return call(kernel, outs, args + list(terms), "norm_back")


def split_grads(grads, me):
    rows, width = grads[0].shape[0] * len(grads) // 4, grads[0].shape[1]

    def kernel(me_ref, *refs):
        ins, outs = refs[: len(grads)], refs[len(grads) : len(grads) + 4]
        joined = refs[-1]
        join(ins, joined)
        for away, out in enumerate(outs):
            member = jnp.bitwise_xor(me_ref[0], away)
            out[...] = joined[pl.ds(pl.multiple_of(member * rows, rows), rows), :].astype(LOW)

    scratch = [pltpu.VMEM((4 * rows, width), WIDE)]
    out = shape_of((rows, width), LOW)
    return call(kernel, [out] * 4, [me, *grads], "split_grads", scratch=scratch, scalars=1)


def place_grads(qkv_pieces, up_pieces, proj, down, part, rest, me):
    rows, hidden = up_pieces[0][0].shape
    width = 4 * part
    lanes = hidden // rest

    def kernel(me_ref, *refs):
        pieces, (proj_ref, down0, down1) = refs[:16], refs[16:19]
        qkv_out, up_out, proj_out, down_out = refs[19:]
        for depth in range(2):
            for away in range(4):
                member = jnp.bitwise_xor(me_ref[0], away)
                ref = pieces[4 * depth + away]
                for s in range(3):
                    start = pl.multiple_of(s * width + member * part, 128)
                    value = ref[:, s * part : (s + 1) * part].astype(WIDE)
                    qkv_out[depth, :, pl.ds(start, part)] = value
                ref = pieces[8 + 4 * depth + away]
                for f in range(rest):
                    start = pl.multiple_of((f * 4 + member) * lanes, 128)
                    value = ref[:, f * lanes : (f + 1) * lanes].astype(WIDE)
                    up_out[depth, :, pl.ds(start, lanes)] = value
            down_out[depth] = (down0, down1)[depth][...]
        proj_out[...] = proj_ref[...].astype(WIDE)

    outs = [
        shape_of((2, rows, 3 * width), WIDE),
        shape_of((2, rows, 4 * hidden), WIDE),
        shape_of(proj.shape, WIDE),
        shape_of((2,) + down[0].shape, WIDE),
    ]
    args = [me, *qkv_pieces[0], *qkv_pieces[1], *up_pieces[0], *up_pieces[1], proj, *down]
    return call(kernel, outs, args, "place_grads", scalars=1)


def on_device(
    tokens,
    cotangent,
    scene_ids,
    frame_index,
    qkv_weight,
    qkv_bias,
    proj_weight,
    fc1_weight,
    fc1_bias,
    fc2_weight,
    out_bias,
    norm_gain,
    norm_bias,
    layer_scale,
    qk_gain,
    qk_bias,
):
    frames = lax.axis_size("frame")
    team = 2 * frames
    rest = lax.axis_size("outer") * lax.axis_size("inner")
    count = team * rest
    rows, width = tokens.shape
    head_size = qk_gain.shape[-1]
    heads = width // head_size // team
    part = heads * head_size
    hidden = fc1_weight.shape[-1] // team
    mine = lax.axis_index("core") * frames + lax.axis_index("frame")
    here = lax.axis_index("outer") * lax.axis_size("inner") + lax.axis_index("inner")
    me = mine.reshape(1).astype(jnp.int32)
    shard_rows = qkv_weight.shape[1]
    fc2_rows = fc2_weight.shape[1]
    unit = team * shard_rows
    table = ring_table()
    quick = frames == 2 and shard_rows % 32 == 0 and part % 128 == 0 and (hidden // rest) % 128 == 0

    shards = []
    proj_here = lax.ppermute(proj_weight, EVERY, spread(count, team))
    for depth in range(2):
        if quick:
            split = split_weights(qkv_weight[depth], fc1_weight[depth], part, rest, me)
            pieces = [split[0], swap(split[1], "frame"), swap(split[2], "core"), cross(split[3])]
            attn, up = pack_weights(pieces, proj_here[depth], part, me)
            down = fc2_weight[depth]
        else:
            attn = exchange_columns(
                qkv_weight[depth]
                .reshape(shard_rows, 3, team, part)
                .transpose(0, 2, 1, 3)
                .reshape(shard_rows, team, 3 * part)
            ).reshape(unit, 3 * part)
            attn = jnp.concatenate([attn, widen(proj_here[depth], part)], axis=1)
            up = exchange_columns(
                fc1_weight[depth]
                .reshape(shard_rows, rest, team, hidden // rest)
                .transpose(0, 2, 1, 3)
                .reshape(shard_rows, team, hidden)
            ).reshape(unit, hidden)
            down = widen(fc2_weight[depth], hidden)
        shards.append((attn, up, down))

    weights = []
    for depth in range(2):
        attn, up, down = shards[depth]
        (attn,) = ring_gather(attn[: unit // 2], attn[unit // 2 :], table, True)
        up, down = ring_gather(up, down, table, False)
        if quick:
            weights.append(((attn, attn, shard_rows, part), up, down))
        else:
            proj = narrow(attn[:, :, 3 * part :], shard_rows).reshape(1, part, width)
            down = narrow(down, fc2_rows).reshape(1, hidden, width)
            weights.append(((attn, proj, part, width), up, down))

    small_parts = (qkv_bias, fc1_bias, out_bias, norm_gain, norm_bias, layer_scale)
    small = small_gather(jnp.concatenate([m.reshape(-1) for m in small_parts])).astype(WIDE)
    n_qkv, n_up = qkv_bias.size, fc1_bias.size
    bias_qkv = small[:, :n_qkv].reshape(count, 2, -1).transpose(1, 0, 2).reshape(2, 3, team, part)
    bias_qkv = lax.dynamic_index_in_dim(bias_qkv, mine, 2, keepdims=False).reshape(2, 3 * part)
    bias_up = small[:, n_qkv : n_qkv + n_up].reshape(rest, team, 2, -1)
    bias_up = lax.dynamic_index_in_dim(bias_up, mine, 1, keepdims=False)
    bias_up = bias_up.transpose(1, 0, 2).reshape(2, hidden)
    vectors = small[:, n_qkv + n_up :].reshape(count, 16, -1).transpose(1, 0, 2).reshape(16, width)
    head_gain = jnp.tile(qk_gain.astype(WIDE), (1, 1, heads))
    head_shift = jnp.tile(qk_bias.astype(WIDE), (1, 1, heads))

    ids = jnp.concatenate([m.reshape(-1) for m in team_gather(scene_ids.reshape(1, rows))])

    streams, middles, branches, kept = [tokens], [], [], []
    low = first_norm(tokens, vectors)
    for depth in range(2):
        attn_weights, weight_up, weight_down = weights[depth]
        kept_attn, own, peer = attn_forward(
            team_gather(low), attn_weights, bias_qkv[depth : depth + 1], head_gain[depth], head_shift[depth],
            ids, head_size, frames, depth == 0,
        )
        branch_one, middle, low = branch_norm(streams[depth], team_sum(own, peer), vectors, depth, 0)
        kept_mlp, own, peer = mlp_forward(team_gather(low), weight_up, weight_down, bias_up[depth : depth + 1])
        terms = team_sum(own, peer)
        branch_two = None
        if depth == 0:
            branch_two, stream, low = branch_norm(middle, terms, vectors, 0, 1)
            streams.append(stream)
        middles.append(middle)
        branches.append((branch_one, branch_two))
        kept.append((kept_attn, kept_mlp))

    activations, low, turn_sums = turn(middles[1], terms, cotangent, vectors)
    grad = cotangent
    rows_of = {(SCALE, 1, 1): turn_sums[0], (OUT, 1, 1): turn_sums[1]}
    sums_up, sums_qkv, head_sums = [None, None], [None, None], [None, None]
    finals = [None, None]
    for depth in (1, 0):
        attn_weights, weight_up, weight_down = weights[depth]
        kept_attn, (second, act, slope) = kept[depth]
        first, flat = kept_attn[0], kept_attn[4]
        (branch_low, pre_low, sum_up), own, peer = mlp_backward(team_gather(low), weight_up, weight_down, slope)
        sums_up[depth] = sum_up
        grad_down = dot_tn(act, branch_low).astype(LOW)
        grad_up = dot_tn(second, pre_low).astype(LOW)
        grad_middle, low, sums = norm_back(
            grad, team_sum(own, peer), middles[depth], branches[depth][0], vectors, depth, 1, (depth, 0)
        )
        for kind, place, row in ((GAIN, 1, 0), (SHIFT, 1, 1), (SCALE, 0, 2), (OUT, 0, 3)):
            rows_of[kind, depth, place] = sums[row]
        (att_low, mixed_low, sum_qkv, head_sum), own, peer = attn_backward(
            team_gather(low), attn_weights, head_gain[depth], kept_attn, ids, head_size, frames, depth == 0
        )
        sums_qkv[depth], head_sums[depth] = sum_qkv, head_sum
        terms = team_sum(own, peer)
        if depth == 1:
            grad, low, sums = norm_back(
                grad_middle, terms, streams[1], branches[0][1], vectors, 1, 0, (0, 1)
            )
            rows_of[SCALE, 0, 1], rows_of[OUT, 0, 1] = sums[2], sums[3]
        else:
            input_grad, sums = norm_back(grad_middle, terms, tokens, None, vectors, 0, 0, None)
        rows_of[GAIN, depth, 0], rows_of[SHIFT, depth, 0] = sums[0], sums[1]

        grad_up = grad_up.reshape(rest, unit, hidden)
        if quick:
            grad_down = grad_down.reshape(rest, fc2_rows, width)
            attn = attn_weight_grads(first, mixed_low, flat, att_low, rest, shard_rows)
        else:
            grad_down = grad_down.reshape(rest, fc2_rows, width // hidden, hidden)
            grad_down = grad_down.transpose(0, 2, 1, 3).reshape(rest, -1, hidden)
            grad_qkv = dot_tn(first, mixed_low).astype(LOW).reshape(rest, unit, 3 * part)
            grad_proj = dot_tn(flat, att_low).astype(LOW).reshape(rest, shard_rows, team, part)
            grad_proj = grad_proj.transpose(0, 2, 1, 3).reshape(rest, unit, part)
            attn = jnp.concatenate([grad_qkv, grad_proj], axis=2)
        up_sum, down_sum = ring_sum(grad_up, grad_down, table, False)
        attn_sum = ring_sum(attn, attn, table, True)
        if quick:
            up_pieces = split_grads([up_sum], me)
            qkv_pieces = split_grads([m[:, : 3 * part] for m in attn_sum], me)
            up_pieces, qkv_pieces = (
                [m[0], swap(m[1], "frame"), swap(m[2], "core"), cross(m[3])] for m in (up_pieces, qkv_pieces)
            )
            proj_sum = jnp.concatenate([m[:, 3 * part :] for m in attn_sum], axis=0)
            finals[depth] = (qkv_pieces, up_pieces, narrow(proj_sum, shard_rows).astype(LOW), down_sum)
        else:
            attn_sum = jnp.concatenate(attn_sum, axis=0)
            qkv_mine = exchange_columns(
                attn_sum[:, : 3 * part].astype(LOW).reshape(team, shard_rows, 3 * part).transpose(1, 0, 2)
            )
            qkv_mine = qkv_mine.reshape(team, shard_rows, 3, part).transpose(1, 2, 0, 3)
            up_mine = exchange_columns(up_sum.astype(LOW).reshape(team, shard_rows, hidden).transpose(1, 0, 2))
            up_mine = up_mine.reshape(team, shard_rows, rest, hidden // rest).transpose(1, 2, 0, 3)
            finals[depth] = (
                qkv_mine.reshape(shard_rows, -1),
                up_mine.reshape(shard_rows, -1),
                narrow(attn_sum[:, 3 * part :], shard_rows).astype(LOW),
                narrow(down_sum, fc2_rows),
            )

    proj_grad = lax.ppermute(
        jnp.stack([finals[0][2], finals[1][2]]), EVERY, [(b, a) for a, b in spread(count, team)]
    )
    if quick:
        qkv_grad, up_grad, proj_grad, down_grad = place_grads(
            [finals[0][0], finals[1][0]], [finals[0][1], finals[1][1]], proj_grad,
            [finals[0][3], finals[1][3]], part, rest, me,
        )
    else:
        proj_grad = proj_grad.astype(WIDE)
        qkv_grad, up_grad, down_grad = (
            jnp.stack([finals[0][i], finals[1][i]]).astype(WIDE) for i in (0, 1, 3)
        )

    names = [(kind, depth, place) for kind in (OUT, GAIN, SHIFT, SCALE) for depth in (0, 1) for place in (0, 1)]
    token_sums = jnp.stack([rows_of[name] for name in names])
    full_qkv = lax.dynamic_update_slice(
        jnp.zeros((6, team, part), WIDE),
        jnp.concatenate(sums_qkv, axis=0).reshape(6, 1, part),
        (0, mine, 0),
    ).reshape(6, width)
    head_all = jnp.stack(head_sums).reshape(-1, heads, head_size).sum(axis=1).reshape(1, -1)
    head_all = jnp.pad(head_all, ((0, 0), (0, width - head_all.shape[1])))
    team_rows = jnp.concatenate([token_sums, full_qkv, head_all], axis=0)
    team_rows = team_rows + swap(team_rows, "core")
    if frames == 2:
        team_rows = team_rows + swap(team_rows, "frame")
    else:
        team_rows = lax.psum(team_rows, "frame")
    sums_up = jnp.concatenate(sums_up, axis=0).reshape(2, rest, hidden // rest)
    sums_up = jnp.pad(sums_up, ((0, 0), (0, 0), (0, (width - hidden) // rest))).reshape(2, width)
    split = jnp.concatenate([team_rows[:16], sums_up], axis=0)
    split, common = small_sum(split, team_rows[16:])
    vector_grads = lax.dynamic_slice_in_dim(split[:16], mine * (width // count), width // count, 1)
    vector_grads = vector_grads.reshape(4, 2, 2, -1)
    grad_bias_qkv = common[:6].reshape(2, -1)
    grad_bias_qkv = lax.dynamic_slice_in_dim(
        grad_bias_qkv, (here * team + mine) * qkv_bias.shape[1], qkv_bias.shape[1], 1
    )
    head_all = common[6, : 8 * head_size].reshape(2, 2, 2, head_size)
    return (
        activations,
        input_grad,
        qkv_grad,
        grad_bias_qkv,
        proj_grad,
        up_grad,
        split[16:, : hidden // rest],
        down_grad,
        vector_grads[0],
        vector_grads[1],
        vector_grads[2],
        vector_grads[3],
        head_all[:, 0],
        head_all[:, 1],
    )


def solution(mesh):
    scenes, frames = mesh.shape["scene"], mesh.shape["frame"]
    rest = scenes // 2
    outer = 4 if rest % 4 == 0 else rest
    grid = Mesh(mesh.devices.reshape(outer, rest // outer, 2, frames), EVERY)
    by_rows = P(EVERY, None)
    second = P(None, EVERY)
    second_rows = P(None, EVERY, None)
    last = P(None, None, EVERY)
    return jax.shard_map(
        on_device,
        mesh=grid,
        in_specs=(
            by_rows, by_rows, P(EVERY), P(EVERY), second_rows, second, second_rows, second_rows,
            second, second_rows, last, last, last, last, P(), P(),
        ),
        out_specs=(
            by_rows, by_rows, second_rows, second, second_rows, second_rows, second, second_rows,
            last, last, last, last, P(), P(),
        ),
        check_vma=False,
    )
```

```python
import jax
import jax.numpy as jnp
import numpy as np
from jax import lax
from jax.experimental import pallas as pl
from jax.experimental.pallas import tpu as pltpu
from jax.sharding import Mesh
from jax.sharding import PartitionSpec as P

EPSILON = 1e-06
FRAME_TOK = 64
LOW = jnp.bfloat16
WIDE = jnp.float32
EVERY = ("outer", "inner", "core", "frame")
REST = ("outer", "inner")
TEAM = ("core", "frame")
HIGHEST = lax.Precision.HIGHEST
ROOT_HALF = 0.7071067811865476
ROOT_TWO_PI = 0.3989422804014327
MEBI = 1024 * 1024
OUT, GAIN, SHIFT, SCALE = 0, 4, 8, 12


def dot(left, right):
    return jnp.dot(left, right, preferred_element_type=WIDE)


def dot_tn(left, right):
    return lax.dot_general(left, right, (((0,), (0,)), ((), ())), preferred_element_type=WIDE)


def dot_nt(left, right):
    return lax.dot_general(left, right, (((1,), (1,)), ((), ())), preferred_element_type=WIDE)


def normed(values):
    center = values - jnp.mean(values, axis=-1, keepdims=True)
    rate = lax.rsqrt(jnp.mean(center * center, axis=-1, keepdims=True) + EPSILON)
    return center * rate, rate


def normed_back(grad, unit, rate, gain):
    inner = grad * gain
    mean_one = jnp.mean(inner, axis=-1, keepdims=True)
    mean_two = jnp.mean(inner * unit, axis=-1, keepdims=True)
    return rate * (inner - mean_one - unit * mean_two)


def shape_of(shape, dtype):
    return jax.ShapeDtypeStruct(shape, dtype)


def call(kernel, outs, args, name, flops=0, scratch=(), scalars=0, far_in=(), far_out=()):
    hbm = pl.BlockSpec(memory_space=pltpu.HBM)
    vmem = pl.BlockSpec(memory_space=pltpu.VMEM)
    smem = pl.BlockSpec(memory_space=pltpu.SMEM)
    in_specs = [smem if i < scalars else hbm if i in far_in else vmem for i in range(len(args))]
    bytes_all = sum(m.size * m.dtype.itemsize for m in args)
    bytes_all += sum(int(np.prod(s.shape)) * s.dtype.itemsize for s in outs)
    sized = [s for s in scratch if hasattr(s, "shape") and s.memory_space == pltpu.VMEM]
    held = sum(int(np.prod(s.shape)) * s.dtype.itemsize for s in sized)
    limit = (held * 5 // 4 + bytes_all * 2 // 5 if flops else bytes_all) + (8 if flops else 3) * MEBI
    args = [pltpu.with_memory_space_constraint(m, pltpu.HBM) if i in far_in else m for i, m in enumerate(args)]
    outs = [pltpu.HBM(m.shape, m.dtype) if i in far_out else m for i, m in enumerate(outs)]
    return pl.pallas_call(
        kernel,
        out_shape=list(outs),
        in_specs=in_specs,
        out_specs=[hbm if i in far_out else vmem for i in range(len(outs))],
        scratch_shapes=list(scratch),
        compiler_params=pltpu.CompilerParams(vmem_limit_bytes=limit),
        cost_estimate=pl.CostEstimate(flops=flops, bytes_accessed=bytes_all, transcendentals=0),
        name=name,
    )(*args)


def swap(values, axis):
    return lax.ppermute(values, axis, [(0, 1), (1, 0)])


def cross(values):
    return lax.ppermute(values, TEAM, [(0, 3), (1, 2), (2, 1), (3, 0)])


def team_gather(values, work=None, pump=None):
    if lax.axis_size("frame") == 2:
        far = swap(values, "frame")
        near = swap(work(values) if work else values, "core")
        far = pump(far) if pump else far
        return [values, far, near, swap(far, "core")]
    both = lax.all_gather(values, "frame", axis=0, tiled=True)
    return [both, swap(both, "core")]


def team_sum(own, peer, work=None):
    if lax.axis_size("frame") == 2:
        far = own[1] + swap(peer[1], "core").astype(WIDE)
        came = swap(far.astype(LOW), "frame")
        near = swap(work(peer[0]) if work else peer[0], "core")
        return [own[0], near, came]
    total = own[0] + swap(peer[0], "core").astype(WIDE)
    return [lax.psum_scatter(total.astype(LOW), "frame", scatter_dimension=0, tiled=True).astype(WIDE)]


def exchange_columns(values):
    parts = values.transpose(1, 0, 2)
    frames = lax.axis_size("frame")
    parts = parts.reshape((2, frames) + parts.shape[1:])
    both = lax.all_to_all(parts, "frame", 1, 1, tiled=True)
    here = lax.axis_index("core")
    keep = lax.dynamic_index_in_dim(both, here, 0, keepdims=False)
    came = swap(lax.dynamic_index_in_dim(both, 1 - here, 0, keepdims=False), "core")
    out = jnp.stack([jnp.where(here == 0, keep, came), jnp.where(here == 0, came, keep)], axis=0)
    return out.reshape((2 * frames,) + out.shape[2:])


SMALL_ROWS = 16


def split_weights(depth, weights, vectors, part, rest, me):
    qkv, up = weights
    _, rows, width = qkv.shape
    width //= 3
    hidden = up.shape[2] // 4
    lanes = hidden // rest
    extra = SMALL_ROWS if vectors else 0

    def kernel(me_ref, qkv_ref, up_ref, *refs):
        small, outs = refs[: len(refs) - 4], refs[-4:]
        for away, out in enumerate(outs):
            member = jnp.bitwise_xor(me_ref[0], away)
            for s in range(3):
                start = pl.multiple_of(s * width + member * part, 128)
                out[:rows, s * part : (s + 1) * part] = qkv_ref[depth, :, pl.ds(start, part)]
            for f in range(rest):
                start = pl.multiple_of((f * 4 + member) * lanes, 128)
                at = 3 * part + f * lanes
                out[:rows, at : at + lanes] = up_ref[depth, :, pl.ds(start, lanes)]
            if not vectors:
                continue
            out[rows:, :] = jnp.zeros((extra, out.shape[1]), LOW)
            bias_qkv, bias_up, ids = small[:3]
            for i, ref in enumerate(small[3:]):
                for d in range(2):
                    for j in range(2):
                        at = rows + 4 * i + 2 * d + j
                        out[at : at + 1, : ref.shape[2]] = ref[d, j : j + 1, :]
            out[rows : rows + 2, 128 : 128 + bias_qkv.shape[1]] = bias_qkv[...]
            out[rows : rows + 2, 256 : 256 + bias_up.shape[1]] = bias_up[...]
            out[rows : rows + 1, 512 : 512 + ids.shape[1]] = ids[...].astype(WIDE).astype(LOW)

    out = shape_of((rows + extra, 3 * part + hidden), qkv.dtype)
    return call(kernel, [out] * 4, [me, qkv, up, *vectors], "split_weights", scalars=1)


def pack_weights(pieces, proj, depth, part, me, vectors):
    rows = proj.shape[1]
    half = 2 * rows
    hidden = pieces[0].shape[1] - 3 * part

    def kernel(me_ref, p0, p1, p2, p3, proj_ref, low_half, high_half, up, *refs):
        attn, small = refs[-2], refs[-1]
        for away, ref in enumerate((p0, p1, p2, p3)):
            member = jnp.bitwise_xor(me_ref[0], away)
            start = pl.multiple_of(member * rows, rows)
            attn[pl.ds(start, rows), : 3 * part] = ref[:rows, : 3 * part]
            up[pl.ds(start, rows), :] = ref[:rows, 3 * part :]
            if vectors:
                small[member] = ref[rows:, :640]
        for j in range(4):
            attn[j * rows : (j + 1) * rows, 3 * part :] = proj_ref[depth, :, j * part : (j + 1) * part]
        low_half[:half, :] = attn[:half, :]
        high_half[...] = attn[half:, :]
        if vectors:
            low_half[half:, :] = jnp.zeros((SMALL_ROWS, 4 * part), LOW)
            for at, start, size in ((0, 0, 32), (128, 128, 96), (512, 256, 128)):
                joined = [small[m, :, start : start + size].astype(WIDE) for m in range(4)]
                value = jnp.concatenate(joined, axis=1).astype(LOW)
                low_half[half:, at : at + 4 * size] = value

    extra = SMALL_ROWS if vectors else 0
    outs = [
        shape_of((half + extra, 4 * part), LOW),
        shape_of((half, 4 * part), LOW),
        shape_of((4 * rows, hidden), LOW),
    ]
    scratch = [pltpu.VMEM((4 * rows, 4 * part), LOW), pltpu.VMEM((4, SMALL_ROWS, 640), LOW)]
    return call(kernel, outs, [me, *pieces, proj], "pack_weights", scratch=scratch, scalars=1)


def unpack_vectors(pieces, rows, table, me):
    rest, width = len(pieces), pieces[0].shape[1]
    part = width // 4

    def kernel(me_ref, table_ref, *refs):
        vec, bias_qkv, bias_up, small, whole, semaphores = refs[rest:]
        copies = []
        for k in range(rest):
            source = refs[k].at[pl.ds(rows, SMALL_ROWS), :]
            copies.append(pltpu.make_async_copy(source, small.at[table_ref[0, k]], semaphores.at[k]))
            copies[-1].start()
        wait_all(copies)
        for f in range(rest):
            vec[:, f * 128 : (f + 1) * 128] = small[f, :, :128].astype(WIDE)
            whole[:, f * 384 : (f + 1) * 384] = small[f, :, 128:512].astype(WIDE)
            start = pl.multiple_of(512 + me_ref[0] * 128, 128)
            bias_up[:, f * 128 : (f + 1) * 128] = small[f, :, pl.ds(start, 128)].astype(WIDE)
        for s in range(3):
            start = pl.multiple_of(s * width + me_ref[0] * part, 128)
            bias_qkv[:, s * part : (s + 1) * part] = whole[:, pl.ds(start, part)]

    outs = [shape_of((16, width), WIDE), shape_of((16, 3 * part), WIDE), shape_of((16, width), WIDE)]
    scratch = [
        pltpu.VMEM((rest, SMALL_ROWS, width), LOW),
        pltpu.VMEM((16, 3 * width), WIDE),
        pltpu.SemaphoreType.DMA((rest,)),
    ]
    args = [me, table, *pieces]
    return call(kernel, outs, args, "unpack_vectors", 0, scratch, 2, far_in=range(2, 2 + rest))


def spread(count, team):
    rest = count // team
    return [(i, (i % rest) * team + i // rest) for i in range(count)]


def widen(rows, width):
    height, columns = rows.shape
    parts = columns // width
    if parts == 1:
        return rows
    return rows.reshape(height, parts, width).transpose(1, 0, 2).reshape(parts * height, width)


def narrow(stacked, height):
    lead = stacked.shape[:-2]
    parts = stacked.shape[-2] // height
    if parts == 1:
        return stacked
    width = stacked.shape[-1]
    shaped = stacked.reshape(lead + (parts, height, width))
    return jnp.moveaxis(shaped, -3, -2).reshape(lead + (height, parts * width))


def ring_order(outer, inner):
    order = []
    for a in range(outer):
        row = range(1, inner) if a % 2 == 0 else range(inner - 1, 0, -1)
        order += [a * inner + b for b in row]
    return order + [a * inner for a in range(outer - 1, -1, -1)]


def ring_table():
    outer, inner = lax.axis_size("outer"), lax.axis_size("inner")
    order = ring_order(outer, inner)
    rest = outer * inner
    place = {team: i for i, team in enumerate(order)}
    table = np.array(
        [
            [[order[(place[f] + sign * k) % rest] for k in range(rest)] for sign in (-1, 1)]
            for f in range(rest)
        ],
        np.int32,
    )
    here = lax.axis_index("outer") * inner + lax.axis_index("inner")
    return lax.dynamic_index_in_dim(jnp.asarray(table), here, 0, keepdims=False)


def ring_shift(values, sign):
    order = ring_order(lax.axis_size("outer"), lax.axis_size("inner"))
    rest = len(order)
    return lax.ppermute(values, REST, [(order[i], order[(i + sign) % rest]) for i in range(rest)])


def ring_step(low_half, high_half):
    low_half, high_half = ring_shift(low_half, 1), ring_shift(high_half, -1)
    return lax.optimization_barrier((low_half, high_half))


class RingGather:
    def __init__(self, low_half, high_half, rest):
        self.rest = rest
        self.back, self.ahead = [low_half], [high_half]
        self.came = (ring_shift(low_half, 1), ring_shift(high_half, -1))

    def take(self, came):
        self.back.append(came[0])
        self.ahead.append(came[1])
        self.came = None
        if len(self.back) < self.rest:
            self.came = (ring_shift(came[0], 1), ring_shift(came[1], -1))


def steps(count, ring):
    came = ()
    for _ in range(count):
        if ring.came is None:
            break
        came = tie(*ring.came)
        ring.take(came)
    return came


class Pieces:
    def __init__(self, rows, *lists):
        self.rows = rows
        self.lists = lists
        self.args = [m for arrays, _, _ in lists for m in arrays]
        self.count = len(self.args)
        height = sum(min(arrays[0].shape[0], arrays[-1].shape[0], rows) for arrays, _, _ in lists)
        self.shape = (len(lists[0][0]), height, self.args[0].shape[1])

    def start(self, refs, table_ref, target, semaphores):
        copies = []
        for arrays, side, first in self.lists:
            for k in range(len(arrays)):
                source = refs[len(copies)].at[pl.ds(0, self.rows), :]
                spot = target.at[table_ref[side, k], pl.ds(first, self.rows), :]
                copies.append(pltpu.make_async_copy(source, spot, semaphores.at[len(copies)]))
                copies[-1].start()
        return copies


class Whole:
    count = 1

    def __init__(self, array, first, rows):
        self.first = first
        self.args = [array]
        self.shape = (array.shape[0], rows, array.shape[2])

    def start(self, refs, table_ref, target, semaphores):
        source = refs[0].at[:, pl.ds(self.first, self.shape[1]), :]
        copy = pltpu.make_async_copy(source, target, semaphores.at[0])
        copy.start()
        return [copy]


def wait_all(copies):
    for copy in copies:
        copy.wait()


def tie(*values):
    return lax.optimization_barrier(values)


class RingSums:
    def __init__(self, rest):
        self.rest = rest
        self.active = []
        self.waiting = []
        self.came = None
        self.started = []

    def work(self, value):
        if self.came is not None:
            self.came = tie(*self.came, value)[:2]
        self.pump()
        started, self.started = self.started, []
        return tie(value, *started)[0] if started else value

    def add(self, low_parts, high_parts, done):
        self.waiting.append(
            {"parts": (low_parts, high_parts), "rows": low_parts[0].shape[0], "done": done, "hop": 0}
        )

    def pump(self, *values):
        if self.came is not None:
            tied = tie(*values, *self.came)
            values, self.came = tied[: len(values)], tied[len(values) :]
        rings = self.active + self.waiting
        self.waiting = []
        if not rings:
            return values if len(values) != 1 else values[0]
        columns = rings[0]["parts"][0][0].shape[1]
        moving, ended, plans, args = 0, [], [], []
        start = 0
        for ring in rings:
            came_at = start if ring["hop"] else None
            if ring["hop"]:
                start += ring["rows"]
            args += [ring["parts"][side][ring["hop"]] for side in range(2)]
            ring["hop"] += 1
            if ring["hop"] == self.rest:
                plans.append((ring["rows"], came_at, None))
                ended.append(ring)
            else:
                plans.append((ring["rows"], came_at, moving))
                moving += ring["rows"]
        came = list(self.came) if self.came is not None else []

        size = sum(rows for rows, _, _ in plans)

        def kernel(*refs):
            came_refs = refs[: len(came)]
            part_refs = refs[len(came) : len(came) + len(args)]
            outs, local, semaphores = refs[len(came) + len(args) : -2], refs[-2], refs[-1]
            copies, at = [], 0
            for i, (rows, _, _) in enumerate(plans):
                for side in range(2):
                    spot = local.at[side, pl.ds(at, rows), :]
                    copies.append(
                        pltpu.make_async_copy(part_refs[2 * i + side], spot, semaphores.at[2 * i + side])
                    )
                    copies[-1].start()
                at += rows
            for copy in copies:
                copy.wait()
            final, at = (2 if moving else 0), 0
            for rows, came_at, goes_to in plans:
                for side in range(2):
                    value = local[side, at : at + rows, :]
                    if came_at is not None:
                        other = came_refs[side][came_at : came_at + rows, :]
                        value = value.astype(WIDE) + other.astype(WIDE)
                    if goes_to is None:
                        outs[final + side][...] = value.astype(WIDE)
                    else:
                        outs[side][goes_to : goes_to + rows, :] = value.astype(LOW)
                if goes_to is None:
                    final += 2
                at += rows

        outs = [shape_of((moving, columns), LOW)] * 2 if moving else []
        for ring in ended:
            outs += [shape_of((ring["rows"], columns), WIDE)] * 2
        scratch = [pltpu.VMEM((2, size, columns), LOW), pltpu.SemaphoreType.DMA((len(args),))]
        far_in = range(len(came), len(came) + len(args))
        res = call(kernel, outs, came + args, "ring_add", 0, scratch, far_in=far_in)
        at = 2 if moving else 0
        for ring in ended:
            ring["done"](res[at], res[at + 1])
            at += 2
        self.active = [ring for ring in rings if ring["hop"] < self.rest]
        self.started += list(res[:2])
        self.came = (ring_shift(res[0], 1), ring_shift(res[1], -1)) if moving else None
        return values if len(values) != 1 else values[0]

    def busy(self):
        return bool(self.active or self.waiting)


def hop_order(low_parts, high_parts, table):
    rest = table.shape[1]
    return [
        [lax.dynamic_index_in_dim(parts, table[side, k % rest], 0, keepdims=False) for k in range(1, rest + 1)]
        for side, parts in ((0, low_parts), (1, high_parts))
    ]


def small_gather(values):
    out = values[None]
    for axis in ("frame", "core", "inner", "outer"):
        size, here, step = lax.axis_size(axis), lax.axis_index(axis), 1
        while step < size:
            came = lax.ppermute(out, axis, [(i, i ^ step) for i in range(size)])
            first = (here & step) == 0
            out = jnp.concatenate([jnp.where(first, out, came), jnp.where(first, came, out)], axis=0)
            step *= 2
    return out


def small_sum(split, common):
    for axis in ("outer", "inner"):
        size, here = lax.axis_size(axis), lax.axis_index(axis)
        step = size // 2
        while step >= 1:
            half = split.shape[1] // 2
            bit = (here // step) % 2
            keep = lax.dynamic_slice_in_dim(split, bit * half, half, 1)
            send = lax.dynamic_slice_in_dim(split, (1 - bit) * half, half, 1)
            pairs = [(i, i ^ step) for i in range(size)]
            packed = jnp.concatenate([send.reshape(-1), common.reshape(-1)])
            came = lax.ppermute(packed, axis, pairs)
            split = keep + came[: keep.size].reshape(keep.shape)
            common = common + came[keep.size :].reshape(common.shape)
            step //= 2
    return split, common


def head_means(part, head_size):
    row = lax.broadcasted_iota(jnp.int32, (part, part), 0) // head_size
    column = lax.broadcasted_iota(jnp.int32, (part, part), 1) // head_size
    return jnp.where(row == column, 1.0 / head_size, 0.0).astype(WIDE)


def head_mean(values, matrix):
    return jnp.dot(values, matrix, precision=HIGHEST, preferred_element_type=WIDE)


def head_normed(values, matrix):
    center = values - head_mean(values, matrix)
    rate = lax.rsqrt(head_mean(center * center, matrix) + EPSILON)
    return center * rate, rate


def join(refs, out_ref):
    start = 0
    for ref in refs:
        out_ref[start : start + ref.shape[0], :] = ref[...]
        start += ref.shape[0]


def spans(refs):
    start = 0
    for ref in refs:
        yield start, start + ref.shape[0], ref
        start += ref.shape[0]


def flat_rows(ref, first, height, columns):
    block = ref[:, first : first + height, columns]
    return block.reshape(block.shape[0] * height, block.shape[2])


def tiles_of(total, group, block):
    for base in range(0, total, group):
        for start in range(base, base + group, block):
            yield start, base


def allowed_of(ids_col, ids_row, start, base, block, group, use_frame):
    if use_frame:
        row = lax.broadcasted_iota(jnp.int32, (block, group), 0) // FRAME_TOK
        column = lax.broadcasted_iota(jnp.int32, (block, group), 1) // FRAME_TOK
        return row == column
    return ids_col[start : start + block, :] == ids_row[:, base : base + group]


def plan(frames, rows, use_frame):
    group = 2 * FRAME_TOK if use_frame else frames * rows
    return group, min(group, 256)


def part_shapes(pieces, width):
    half = len(pieces) // 2
    return [shape_of((m.shape[0], width), WIDE if i < half else LOW) for i, m in enumerate(pieces)]


def load_semaphores(sources):
    return [pltpu.SemaphoreType.DMA((source.count,)) for source in sources]


def start_loads(sources, table_ref, far_refs, targets, semaphores):
    at, copies = 0, []
    for source, target, semaphore in zip(sources, targets, semaphores):
        copies.append(source.start(far_refs[at : at + source.count], table_ref, target, semaphore))
        at += source.count
    return copies


def attn_forward(pieces, weights, bias, head_gain, head_shift, ids, head_size, frames, use_frame, vectors=None):
    attn, proj, height, wide, table = weights
    sources = [attn] if proj is None else [attn, proj]
    far = [m for source in sources for m in source.args]
    rest, unit, _ = attn.shape
    width, part = rest * unit, head_gain.shape[-1]
    total = sum(m.shape[0] for m in pieces)
    count = len(pieces)
    group, block = plan(frames, total // (2 * frames), use_frame)
    lanes = min(128, part)
    per = lanes // head_size
    scale = head_size ** (-0.5)
    more = 0 if vectors is None else 1

    def kernel(table_ref, *refs):
        far_refs, refs = refs[: len(far)], refs[len(far) :]
        semaphores, refs = refs[-len(sources) :], refs[: -len(sources)]
        targets, refs = refs[-len(sources) :], refs[: -len(sources)]
        copies = start_loads(sources, table_ref, far_refs, targets, semaphores)
        wq, wp = targets[0], targets[-1]
        piece_refs = refs[:count]
        bias_ref, gain_ref, shift_ref, ids_col, ids_row = refs[count : count + 5]
        first, raw, qkv, lse, flat = refs[count + 5 + more : count + 10 + more]
        outs = refs[count + 10 + more :]
        if more:
            vec = refs[count + 5]
            for start, stop, ref in spans(piece_refs):
                unit_one, _ = normed(ref[...].astype(WIDE))
                value = unit_one * row_of(vec, GAIN, 0, 0) + row_of(vec, SHIFT, 0, 0)
                first[start:stop, :] = value.astype(LOW)
        else:
            join(piece_refs, first)
        matrix = head_means(part, head_size)
        for group_copies in copies:
            wait_all(group_copies)
        mixed = dot(first[...], flat_rows(wq, 0, unit, slice(0, 3 * part))) + bias_ref[...]
        raw[...] = mixed[:, : 2 * part]
        for i in range(2):
            unit_i, _ = head_normed(mixed[:, i * part : (i + 1) * part], matrix)
            value = unit_i * gain_ref[i : i + 1, :] + shift_ref[i : i + 1, :]
            qkv[:, i * part : (i + 1) * part] = value.astype(LOW)
        qkv[:, 2 * part :] = mixed[:, 2 * part :].astype(LOW)
        place = lax.broadcasted_iota(jnp.int32, (1, lanes), 1) // head_size
        for start, base in tiles_of(total, group, block):
            allowed = allowed_of(ids_col, ids_row, start, base, block, group, use_frame)
            stats = []
            for lane in range(0, part, lanes):
                query = qkv[start : start + block, lane : lane + lanes] * jnp.asarray(scale, LOW)
                key = qkv[base : base + group, part + lane : part + lane + lanes]
                value = qkv[base : base + group, 2 * part + lane : 2 * part + lane + lanes]
                out = jnp.zeros((block, lanes), WIDE)
                for h in range(per):
                    mask = place == h
                    scores = dot_nt(jnp.where(mask, query, jnp.zeros_like(query)), key)
                    scores = jnp.where(allowed, scores, -jnp.inf)
                    top = jnp.max(scores, axis=-1, keepdims=True)
                    weight = jnp.exp(scores - top)
                    norm = jnp.sum(weight, axis=-1, keepdims=True)
                    stats.append(top + jnp.log(norm))
                    probs = (weight * (1.0 / norm)).astype(LOW)
                    out = jnp.where(mask, dot(probs, value), out)
                flat[start : start + block, lane : lane + lanes] = out.astype(LOW)
            lse[start : start + block, :] = jnp.concatenate(stats, axis=1)
        for a in range(0, width, wide):
            b = a + wide
            chunk = flat_rows(wp, a // wide * height, height, slice(wp.shape[2] - wide, wp.shape[2]))
            for start, stop, ref in spans(outs):
                ref[:, a:b] = dot(flat[start:stop, :], chunk).astype(ref.dtype)

    outs = [
        shape_of((total, width), LOW),
        shape_of((total, 2 * part), WIDE),
        shape_of((total, 3 * part), LOW),
        shape_of((total, part // head_size), WIDE),
        shape_of((total, part), LOW),
    ] + part_shapes(pieces, width)
    outs += [shape_of(source.shape, LOW) for source in sources]
    args = [table] + far + list(pieces)
    args += [bias, head_gain, head_shift, ids.reshape(-1, 1), ids.reshape(1, -1)]
    args += [vectors] if more else []
    flops = 2 * total * (width * 4 * part + group * 2 * part)
    scratch = load_semaphores(sources)
    res = call(kernel, outs, args, "attn_forward", flops, scratch, 1, far_in=range(1, 1 + len(far)))
    weights = (res[5 + count], None if proj is None else res[6 + count], height, wide)
    return res[:5], res[5 : 5 + count // 2], res[5 + count // 2 : 5 + count], weights


def attn_backward(pieces, weights, head_gain, kept, ids, head_size, frames, use_frame):
    _, raw, qkv, lse, _ = kept
    attn, proj, height, wide = weights
    rest, unit, _ = attn.shape
    width, part = rest * unit, head_gain.shape[-1]
    total = sum(m.shape[0] for m in pieces)
    count = len(pieces)
    group, block = plan(frames, total // (2 * frames), use_frame)
    lanes = min(128, part)
    per = lanes // head_size
    scale = head_size ** (-0.5)
    extra = 0 if proj is None else 1

    def kernel(*refs):
        piece_refs, wq, wp = refs[:count], refs[count], refs[count + extra]
        refs = refs[extra + 1 :]
        gain_ref, raw_ref, qkv_ref, lse_ref, ids_col, ids_row = refs[count : count + 6]
        joined, low_mixed, sums, head_sums = refs[count + 6 : count + 10]
        outs = refs[count + 10 : count + 10 + count]
        grad_out, grad_three = refs[count + 10 + count :]
        join(piece_refs, joined)
        grad_flat = jnp.zeros((total, part), WIDE)
        for a in range(0, width, wide):
            b = a + wide
            chunk = flat_rows(wp, a // wide * height, height, slice(wp.shape[2] - wide, wp.shape[2]))
            grad_flat += dot_nt(joined[:, a:b], chunk)
        grad_out[...] = grad_flat.astype(LOW)
        place = lax.broadcasted_iota(jnp.int32, (1, lanes), 1) // head_size
        for start, base in tiles_of(total, group, block):
            allowed = allowed_of(ids_col, ids_row, start, base, block, group, use_frame)
            stats = lse_ref[start : start + block, :]
            for lane in range(0, part, lanes):
                query = qkv_ref[start : start + block, lane : lane + lanes] * jnp.asarray(scale, LOW)
                key = qkv_ref[base : base + group, part + lane : part + lane + lanes]
                value = qkv_ref[base : base + group, 2 * part + lane : 2 * part + lane + lanes]
                grad_here = grad_out[start : start + block, lane : lane + lanes]
                grad_q = jnp.zeros((block, lanes), WIDE)
                grad_k = jnp.zeros((group, lanes), WIDE)
                grad_v = jnp.zeros((group, lanes), WIDE)
                for h in range(per):
                    mask = place == h
                    head = lane // head_size + h
                    scores = dot_nt(jnp.where(mask, query, jnp.zeros_like(query)), key)
                    probs = jnp.exp(jnp.where(allowed, scores - stats[:, head : head + 1], -jnp.inf))
                    grad_p = dot_nt(jnp.where(mask, grad_here, jnp.zeros_like(grad_here)), value)
                    delta = jnp.sum(probs * grad_p, axis=-1, keepdims=True)
                    grad_s = (probs * (grad_p - delta)).astype(LOW)
                    grad_q = jnp.where(mask, dot(grad_s, key), grad_q)
                    grad_k = jnp.where(mask, dot_tn(grad_s, query), grad_k)
                    grad_v = jnp.where(mask, dot_tn(probs.astype(LOW), grad_here), grad_v)
                grad_three[start : start + block, lane : lane + lanes] = grad_q * scale
                for at, grad in ((part, grad_k), (2 * part, grad_v)):
                    spot = (slice(base, base + group), slice(at + lane, at + lane + lanes))
                    if start == base:
                        grad_three[spot] = grad
                    else:
                        grad_three[spot] = grad_three[spot] + grad
        matrix = head_means(part, head_size)
        for i in range(2):
            here = slice(i * part, (i + 1) * part)
            grad = grad_three[:, here]
            unit_i, rate = head_normed(raw_ref[:, here], matrix)
            head_sums[i : i + 1, :] = jnp.sum(grad * unit_i, axis=0, keepdims=True)
            head_sums[2 + i : 3 + i, :] = jnp.sum(grad, axis=0, keepdims=True)
            inner = grad * gain_ref[i : i + 1, :]
            mean_one = head_mean(inner, matrix)
            mean_two = head_mean(inner * unit_i, matrix)
            result = rate * (inner - mean_one - unit_i * mean_two)
            sums[:, here] = jnp.sum(result, axis=0, keepdims=True)
            low_mixed[:, here] = result.astype(LOW)
        result = grad_three[:, 2 * part :]
        sums[:, 2 * part :] = jnp.sum(result, axis=0, keepdims=True)
        low_mixed[:, 2 * part :] = result.astype(LOW)
        weight = flat_rows(wq, 0, unit, slice(0, 3 * part))
        for start, stop, ref in spans(outs):
            ref[...] = dot_nt(low_mixed[start:stop, :], weight).astype(ref.dtype)

    outs = [
        shape_of((total, width), LOW),
        shape_of((total, 3 * part), LOW),
        shape_of((1, 3 * part), WIDE),
        shape_of((4, part), WIDE),
    ] + part_shapes(pieces, width)
    scratch = [pltpu.VMEM((total, part), LOW), pltpu.VMEM((total, 3 * part), WIDE)]
    args = list(pieces) + [attn] + ([] if proj is None else [proj])
    args += [head_gain, raw, qkv, lse, ids.reshape(-1, 1), ids.reshape(1, -1)]
    flops = 2 * total * (width * 4 * part + group * 5 * part)
    res = call(kernel, outs, args, "attn_backward", flops, scratch)
    return res[:4], res[4 : 4 + count // 2], res[4 + count // 2 :]


def attn_weight_grads(first, low_mixed, flat, att_low, rest, height, table):
    width, part = first.shape[1], flat.shape[1]
    unit = width // rest
    wide = width * height // unit

    def kernel(table_ref, first_ref, mixed_ref, flat_ref, att_ref, *refs):
        outs, packed, semaphores = refs[:-2], refs[-2], refs[-1]
        product = dot_tn(first_ref[...], mixed_ref[...]).astype(LOW)
        packed[:, :, : 3 * part] = product.reshape(rest, unit, 3 * part)
        product = dot_tn(flat_ref[...], att_ref[...]).astype(LOW)
        for j in range(unit // height):
            chunk = product[:, j * wide : (j + 1) * wide].reshape(rest, height, wide)
            packed[:, j * height : (j + 1) * height, 3 * part :] = chunk
        copies = []
        for k in range(rest):
            for side in range(2):
                source = packed.at[table_ref[side, (k + 1) % rest], pl.ds(side * (unit // 2), unit // 2), :]
                at = side * rest + k
                copies.append(pltpu.make_async_copy(source, outs[at], semaphores.at[at]))
                copies[-1].start()
        for copy in copies:
            copy.wait()

    flops = 8 * first.shape[0] * width * part
    outs = [shape_of((unit // 2, 4 * part), LOW)] * (2 * rest)
    scratch = [pltpu.VMEM((rest, unit, 4 * part), LOW), pltpu.SemaphoreType.DMA((2 * rest,))]
    args = [table, first, low_mixed, flat, att_low]
    res = call(kernel, outs, args, "attn_weight_grads", flops, scratch, 1, far_out=range(len(outs)))
    return res[:rest], res[rest:]


def mlp_weight_grads(second, pre_low, act, branch_low, rest, table):
    width, hidden = second.shape[1], act.shape[1]

    def kernel(table_ref, second_ref, pre_ref, act_ref, branch_ref, *refs):
        outs, packs, semaphores = refs[:-3], refs[-3:-1], refs[-1]
        copies = []
        for side, (left, right) in enumerate(((second_ref, pre_ref), (act_ref, branch_ref))):
            pack = packs[side]
            pack[...] = dot_tn(left[...], right[...]).astype(LOW).reshape(pack.shape)
            for k in range(rest):
                at = side * rest + k
                source = pack.at[table_ref[side, (k + 1) % rest]]
                copies.append(pltpu.make_async_copy(source, outs[at], semaphores.at[at]))
                copies[-1].start()
        for copy in copies:
            copy.wait()

    flops = 4 * second.shape[0] * width * hidden
    up, down = (width // rest, hidden), (hidden // rest, width)
    outs = [shape_of(up, LOW)] * rest + [shape_of(down, LOW)] * rest
    scratch = [pltpu.VMEM((rest,) + m, LOW) for m in (up, down)] + [pltpu.SemaphoreType.DMA((2 * rest,))]
    args = [table, second, pre_low, act, branch_low]
    res = call(kernel, outs, args, "mlp_weight_grads", flops, scratch, 1, far_out=range(len(outs)))
    return res[:rest], res[rest:]


def mlp_forward(pieces, sources, table, bias):
    rest, unit, hidden = sources[0].shape
    width = rest * unit
    far = [m for source in sources for m in source.args]
    total = sum(m.shape[0] for m in pieces)
    count = len(pieces)

    def kernel(table_ref, *refs):
        far_refs, refs, (up, down), semaphores = refs[: len(far)], refs[len(far) : -4], refs[-4:-2], refs[-2:]
        copies, more_copies = start_loads(sources, table_ref, far_refs, (up, down), semaphores)
        piece_refs = refs[:count]
        bias_ref = refs[count]
        second, act, slope = refs[count + 1 : count + 4]
        outs = refs[count + 4 :]
        join(piece_refs, second)
        wait_all(copies)
        pre = dot(second[...], flat_rows(up, 0, unit, slice(None))) + bias_ref[...]
        below = 0.5 * (1.0 + lax.erf(pre * ROOT_HALF))
        act[...] = (pre * below).astype(LOW)
        slope[...] = (below + pre * (ROOT_TWO_PI * jnp.exp(-0.5 * pre * pre))).astype(LOW)
        wait_all(more_copies)
        weight = flat_rows(down, 0, down.shape[1], slice(None))
        for start, stop, ref in spans(outs):
            ref[...] = dot(act[start:stop, :], weight).astype(ref.dtype)

    outs = [
        shape_of((total, width), LOW),
        shape_of((total, hidden), LOW),
        shape_of((total, hidden), LOW),
    ] + part_shapes(pieces, width)
    outs += [shape_of(source.shape, LOW) for source in sources]
    args = [table] + far + list(pieces) + [bias]
    flops, far_in = 4 * total * width * hidden, range(1, 1 + len(far))
    res = call(kernel, outs, args, "mlp_forward", flops, load_semaphores(sources), 1, far_in=far_in)
    return res[:3], res[3 : 3 + count // 2], res[3 + count // 2 : 3 + count], res[3 + count :]


def mlp_backward(pieces, weight_up, weight_down, slope):
    rest, unit, hidden = weight_up.shape
    width = rest * unit
    total = sum(m.shape[0] for m in pieces)
    count = len(pieces)

    def kernel(*refs):
        piece_refs = refs[:count]
        up, down, slope_ref = refs[count : count + 3]
        joined, low_pre, sums = refs[count + 3 : count + 6]
        outs = refs[count + 6 :]
        join(piece_refs, joined)
        weight = flat_rows(down, 0, down.shape[1], slice(None))
        grad = dot_nt(joined[...], weight) * slope_ref[...].astype(WIDE)
        sums[...] = jnp.sum(grad, axis=0, keepdims=True)
        low_pre[...] = grad.astype(LOW)
        weight = flat_rows(up, 0, unit, slice(None))
        for start, stop, ref in spans(outs):
            ref[...] = dot_nt(low_pre[start:stop, :], weight).astype(ref.dtype)

    outs = [
        shape_of((total, width), LOW),
        shape_of((total, hidden), LOW),
        shape_of((1, hidden), WIDE),
    ] + part_shapes(pieces, width)
    args = list(pieces) + [weight_up, weight_down, slope]
    res = call(kernel, outs, args, "mlp_backward", 4 * total * width * hidden)
    return res[:3], res[3 : 3 + count // 2], res[3 + count // 2 :]


def added(refs):
    total = refs[0][...]
    for ref in refs[1:]:
        total = total + ref[...].astype(WIDE)
    return total


def row_of(vectors, kind, depth, which):
    at = kind + 2 * depth + which
    return vectors[at : at + 1, :]


def branch_norm(stream, terms, vectors, depth, which):
    after = (depth, 1) if which == 0 else (depth + 1, 0)

    def kernel(stream_ref, *refs):
        (vec, branch, result, low), term_refs = refs[-4:], refs[:-4]
        value = added(term_refs) + row_of(vec, OUT, depth, which)
        branch[...] = value
        value = stream_ref[...].astype(WIDE) + row_of(vec, SCALE, depth, which) * value
        result[...] = value
        unit, _ = normed(value)
        low[...] = (unit * row_of(vec, GAIN, *after) + row_of(vec, SHIFT, *after)).astype(LOW)

    outs = [shape_of(stream.shape, WIDE), shape_of(stream.shape, WIDE), shape_of(stream.shape, LOW)]
    return call(kernel, outs, [stream, *terms, vectors], "branch_norm")


def turn(middle, terms, cotangent, vectors):
    def kernel(middle_ref, *refs):
        (cot, vec, result, low, sums), term_refs = refs[-5:], refs[:-5]
        branch = added(term_refs) + row_of(vec, OUT, 1, 1)
        scale = row_of(vec, SCALE, 1, 1)
        result[...] = (middle_ref[...] + scale * branch).astype(LOW)
        grad = cot[...].astype(WIDE)
        grad_branch = grad * scale
        low[...] = grad_branch.astype(LOW)
        sums[0:1, :] = jnp.sum(grad * branch, axis=0, keepdims=True)
        sums[1:2, :] = jnp.sum(grad_branch, axis=0, keepdims=True)

    shape = middle.shape
    outs = [shape_of(shape, LOW), shape_of(shape, LOW), shape_of((2, shape[1]), WIDE)]
    return call(kernel, outs, [middle, *terms, cotangent, vectors], "turn")


def norm_back(grad, terms, stream, branch, vectors, depth, which, before):
    def kernel(*refs):
        grad_ref, stream_ref, vec = refs[0], refs[1], refs[2]
        inputs = 4 if before else 3
        term_refs = refs[inputs : inputs + len(terms)]
        result, low, sums = (refs[inputs + len(terms) :] + (None,))[:3] if before else (
            None, refs[inputs + len(terms)], refs[inputs + len(terms) + 1],
        )
        came = added(term_refs)
        unit, rate = normed(stream_ref[...].astype(WIDE))
        sums[0:1, :] = jnp.sum(came * unit, axis=0, keepdims=True)
        sums[1:2, :] = jnp.sum(came, axis=0, keepdims=True)
        value = grad_ref[...].astype(WIDE)
        value = value + normed_back(came, unit, rate, row_of(vec, GAIN, depth, which))
        if not before:
            low[...] = value.astype(LOW)
            return
        result[...] = value
        sums[2:3, :] = jnp.sum(value * refs[3][...], axis=0, keepdims=True)
        value = value * row_of(vec, SCALE, *before)
        sums[3:4, :] = jnp.sum(value, axis=0, keepdims=True)
        low[...] = value.astype(LOW)

    shape = grad.shape
    outs = [shape_of(shape, LOW), shape_of((4 if before else 2, shape[1]), WIDE)]
    args = [grad, stream, vectors]
    if before:
        outs = [shape_of(shape, WIDE)] + outs
        args = args + [branch]
    return call(kernel, outs, args + list(terms), "norm_back")


def split_grads(grads, me):
    rows, width = grads[0].shape[0] * len(grads) // 4, grads[0].shape[1]

    def kernel(me_ref, *refs):
        ins, outs = refs[: len(grads)], refs[len(grads) : len(grads) + 4]
        joined = refs[-1]
        join(ins, joined)
        for away, out in enumerate(outs):
            member = jnp.bitwise_xor(me_ref[0], away)
            out[...] = joined[pl.ds(pl.multiple_of(member * rows, rows), rows), :].astype(LOW)

    scratch = [pltpu.VMEM((4 * rows, width), grads[0].dtype)]
    out = shape_of((rows, width), LOW)
    return call(kernel, [out] * 4, [me, *grads], "split_grads", scratch=scratch, scalars=1)


def place_grads(qkv_pieces, up_pieces, proj, down, part, rest, me):
    rows, hidden = up_pieces[0][0].shape
    width = 4 * part
    lanes = hidden // rest

    def kernel(me_ref, *refs):
        pieces, (proj_ref, down0, down1) = refs[:16], refs[16:19]
        qkv_out, up_out, proj_out, down_out = refs[19:]
        for depth in range(2):
            for away in range(4):
                member = jnp.bitwise_xor(me_ref[0], away)
                ref = pieces[4 * depth + away]
                for s in range(3):
                    start = pl.multiple_of(s * width + member * part, 128)
                    value = ref[:, s * part : (s + 1) * part].astype(WIDE)
                    qkv_out[depth, :, pl.ds(start, part)] = value
                ref = pieces[8 + 4 * depth + away]
                for f in range(rest):
                    start = pl.multiple_of((f * 4 + member) * lanes, 128)
                    value = ref[:, f * lanes : (f + 1) * lanes].astype(WIDE)
                    up_out[depth, :, pl.ds(start, lanes)] = value
            down_out[depth] = (down0, down1)[depth][...].astype(WIDE)
        proj_out[...] = proj_ref[...].astype(WIDE)

    outs = [
        shape_of((2, rows, 3 * width), WIDE),
        shape_of((2, rows, 4 * hidden), WIDE),
        shape_of(proj.shape, WIDE),
        shape_of((2,) + down[0].shape, WIDE),
    ]
    args = [me, *qkv_pieces[0], *qkv_pieces[1], *up_pieces[0], *up_pieces[1], proj, *down]
    return call(kernel, outs, args, "place_grads", scalars=1)


def on_device(
    tokens,
    cotangent,
    scene_ids,
    frame_index,
    qkv_weight,
    qkv_bias,
    proj_weight,
    fc1_weight,
    fc1_bias,
    fc2_weight,
    out_bias,
    norm_gain,
    norm_bias,
    layer_scale,
    qk_gain,
    qk_bias,
):
    frames = lax.axis_size("frame")
    team = 2 * frames
    rest = lax.axis_size("outer") * lax.axis_size("inner")
    count = team * rest
    rows, width = tokens.shape
    head_size = qk_gain.shape[-1]
    heads = width // head_size // team
    part = heads * head_size
    hidden = fc1_weight.shape[-1] // team
    mine = lax.axis_index("core") * frames + lax.axis_index("frame")
    here = lax.axis_index("outer") * lax.axis_size("inner") + lax.axis_index("inner")
    me = mine.reshape(1).astype(jnp.int32)
    shard_rows = qkv_weight.shape[1]
    fc2_rows = fc2_weight.shape[1]
    unit = team * shard_rows
    table = ring_table()
    quick = frames == 2 and shard_rows % 32 == 0 and part % 128 == 0 and (hidden // rest) % 128 == 0
    quick = quick and hidden == width and width // count == 32 and count * rows // FRAME_TOK <= 256

    small_parts = (qkv_bias, fc1_bias, out_bias, norm_gain, norm_bias, layer_scale)
    head_gain = jnp.tile(qk_gain.astype(WIDE), (1, 1, heads))
    head_shift = jnp.tile(qk_bias.astype(WIDE), (1, 1, heads))
    weights = []
    if quick:
        proj_here = lax.ppermute(proj_weight, EVERY, spread(count, team))
        shards, below = [], None
        for depth in range(2):
            small = (qkv_bias, fc1_bias, scene_ids.reshape(1, rows)) + small_parts[2:]
            split = split_weights(depth, (qkv_weight, fc1_weight), () if depth else small, part, rest, me)
            pieces = [split[0], swap(split[1], "frame"), swap(split[2], "core"), cross(split[3])]
            if depth == 0:
                below = pieces
            shards.append(pack_weights(pieces, proj_here, depth, part, me, depth == 0))
        ids = jnp.concatenate([m[shard_rows, 512 : 512 + rows] for m in below]).astype(jnp.int32)
        tokens_all = team_gather(tokens)
        half = unit // 2
        rings = []
        for depth in range(2):
            low_half, high_half, up = shards[depth]
            rings.append(RingGather(low_half, high_half, rest))
            rings.append(RingGather(up, fc2_weight[depth], rest))
            for ring in rings[-2:]:
                steps(rest, ring)
        vectors, bias_qkv, bias_up = unpack_vectors(rings[0].back, half, table, me)
    else:
        proj_here = lax.ppermute(proj_weight, EVERY, spread(count, team))
        for depth in range(2):
            attn = exchange_columns(
                qkv_weight[depth]
                .reshape(shard_rows, 3, team, part)
                .transpose(0, 2, 1, 3)
                .reshape(shard_rows, team, 3 * part)
            ).reshape(unit, 3 * part)
            attn = jnp.concatenate([attn, widen(proj_here[depth], part)], axis=1)
            up = exchange_columns(
                fc1_weight[depth]
                .reshape(shard_rows, rest, team, hidden // rest)
                .transpose(0, 2, 1, 3)
                .reshape(shard_rows, team, hidden)
            ).reshape(unit, hidden)
            down = widen(fc2_weight[depth], hidden)
            attn, up, down = (lax.all_gather(m, REST, axis=0, tiled=False) for m in (attn, up, down))
            proj = Whole(narrow(attn[:, :, 3 * part :], shard_rows).reshape(1, part, width), 0, part)
            down = Whole(narrow(down, fc2_rows).reshape(1, hidden, width), 0, hidden)
            weights.append(((Whole(attn, 0, unit), proj, part, width, table), (Whole(up, 0, unit), down)))
        small = small_gather(jnp.concatenate([m.reshape(-1) for m in small_parts])).astype(WIDE)
        n_qkv, n_up = qkv_bias.size, fc1_bias.size
        bias_qkv = small[:, :n_qkv].reshape(count, 2, -1).transpose(1, 0, 2).reshape(2, 3, team, part)
        bias_qkv = lax.dynamic_index_in_dim(bias_qkv, mine, 2, keepdims=False).reshape(2, 3 * part)
        bias_up = small[:, n_qkv : n_qkv + n_up].reshape(rest, team, 2, -1)
        bias_up = lax.dynamic_index_in_dim(bias_up, mine, 1, keepdims=False)
        bias_up = bias_up.transpose(1, 0, 2).reshape(2, hidden)
        vectors = small[:, n_qkv + n_up :].reshape(count, 16, -1).transpose(1, 0, 2).reshape(16, width)
        ids = jnp.concatenate([m.reshape(-1) for m in team_gather(scene_ids.reshape(1, rows))])
        tokens_all = team_gather(tokens)

    gathered = []
    streams, middles, branches, kept = [tokens], [], [], []
    for depth in range(2):
        work = None
        if quick:
            ring = rings[2 * depth]
            attn_source = Pieces(half, (ring.back, 0, 0), (ring.ahead, 1, half))
            attn_weights = (attn_source, None, shard_rows, part, table)
        else:
            attn_weights, mlp_sources = weights[depth]
        kept_attn, own, peer, attn_weights = attn_forward(
            team_gather(low, work, work) if depth else tokens_all, attn_weights, bias_qkv[depth : depth + 1],
            head_gain[depth], head_shift[depth], ids, head_size, frames, depth == 0, None if depth else vectors,
        )
        terms = team_sum(own, peer, work)
        branch_one, middle, low = branch_norm(streams[depth], terms, vectors, depth, 0)
        pieces = team_gather(low, work, work)
        if quick:
            ring = rings[2 * depth + 1]
            mlp_sources = (Pieces(unit, (ring.back, 0, 0)), Pieces(unit, (ring.ahead, 1, 0)))
        kept_mlp, own, peer, mlp_weights = mlp_forward(pieces, mlp_sources, table, bias_up[depth : depth + 1])
        gathered.append((attn_weights, mlp_weights))
        terms = team_sum(own, peer, work)
        branch_two = None
        if depth == 0:
            branch_two, stream, low = branch_norm(middle, terms, vectors, 0, 1)
            streams.append(stream)
        middles.append(middle)
        branches.append((branch_one, branch_two))
        kept.append((kept_attn, kept_mlp))

    activations, low, turn_sums = turn(middles[1], terms, cotangent, vectors)
    grad = cotangent
    rows_of = {(SCALE, 1, 1): turn_sums[0], (OUT, 1, 1): turn_sums[1]}
    sums_up, sums_qkv, head_sums = [None, None], [None, None], [None, None]
    finals = [{}, {}]
    ring = RingSums(rest)

    def end_mlp(depth):
        def end(up_sum, down_sum):
            if not quick:
                up = exchange_columns(up_sum.astype(LOW).reshape(team, shard_rows, hidden).transpose(1, 0, 2))
                up = up.reshape(team, shard_rows, rest, hidden // rest).transpose(1, 2, 0, 3)
                finals[depth].update(up=up.reshape(shard_rows, -1), down=narrow(down_sum, fc2_rows))
                return
            end_up(depth)(up_sum)
            finals[depth].update(down=down_sum)

        return end

    def end_up(depth):
        def end(*halves):
            m = split_grads(halves, me)
            finals[depth].update(up=[m[0], swap(m[1], "frame"), swap(m[2], "core"), cross(m[3])])

        return end

    def end_attn(depth):
        def end(low_sum, high_sum):
            if not quick:
                both = jnp.concatenate([low_sum, high_sum], axis=0)
                qkv = exchange_columns(
                    both[:, : 3 * part].astype(LOW).reshape(team, shard_rows, 3 * part).transpose(1, 0, 2)
                )
                qkv = qkv.reshape(team, shard_rows, 3, part).transpose(1, 2, 0, 3)
                proj = narrow(both[:, 3 * part :], shard_rows)
                finals[depth].update(qkv=qkv.reshape(shard_rows, -1), proj=proj.astype(LOW))
                return
            m = split_grads([low_sum[:, : 3 * part], high_sum[:, : 3 * part]], me)
            proj = jnp.concatenate([n[:, 3 * part :] for n in (low_sum, high_sum)], axis=0)
            finals[depth].update(
                qkv=[m[0], swap(m[1], "frame"), swap(m[2], "core"), cross(m[3])],
                proj=narrow(proj, shard_rows).astype(LOW),
            )

        return end

    for depth in (1, 0):
        attn_weights, (weight_up, weight_down) = gathered[depth]
        kept_attn, (second, act, slope) = kept[depth]
        first, flat = kept_attn[0], kept_attn[4]
        pieces = team_gather(low, ring.work)
        (branch_low, pre_low, sum_up), own, peer = mlp_backward(pieces, weight_up, weight_down, slope)
        sums_up[depth] = sum_up
        if quick:
            mlp_parts = mlp_weight_grads(second, pre_low, act, branch_low, rest, table)
        else:
            grad_up = dot_tn(second, pre_low).astype(LOW).reshape(rest, unit, hidden)
            grad_down = dot_tn(act, branch_low).astype(LOW)
            grad_down = grad_down.reshape(rest, fc2_rows, width // hidden, hidden)
            grad_down = grad_down.transpose(0, 2, 1, 3).reshape(rest, -1, hidden)
            mlp_parts = hop_order(grad_up, grad_down, table)
        ring.add(*mlp_parts, end_mlp(depth))
        terms = team_sum(own, peer, ring.work)
        grad_middle, low, sums = norm_back(
            grad, terms, middles[depth], branches[depth][0], vectors, depth, 1, (depth, 0)
        )
        for kind, place, row in ((GAIN, 1, 0), (SHIFT, 1, 1), (SCALE, 0, 2), (OUT, 0, 3)):
            rows_of[kind, depth, place] = sums[row]
        pieces = team_gather(low, ring.work, ring.pump)
        (att_low, mixed_low, sum_qkv, head_sum), own, peer = attn_backward(
            pieces, attn_weights, head_gain[depth], kept_attn, ids, head_size, frames, depth == 0
        )
        sums_qkv[depth], head_sums[depth] = sum_qkv, head_sum
        if quick:
            attn_parts = attn_weight_grads(first, mixed_low, flat, att_low, rest, shard_rows, table)
        else:
            grad_qkv = dot_tn(first, mixed_low).astype(LOW).reshape(rest, unit, 3 * part)
            grad_proj = dot_tn(flat, att_low).astype(LOW).reshape(rest, shard_rows, team, part)
            grad_proj = grad_proj.transpose(0, 2, 1, 3).reshape(rest, unit, part)
            attn = jnp.concatenate([grad_qkv, grad_proj], axis=2)
            attn_parts = hop_order(attn[:, : unit // 2], attn[:, unit // 2 :], table)
        ring.add(*attn_parts, end_attn(depth))
        terms = team_sum(own, peer, ring.work)
        if depth == 1:
            grad, low, sums = norm_back(
                grad_middle, terms, streams[1], branches[0][1], vectors, 1, 0, (0, 1)
            )
            rows_of[SCALE, 0, 1], rows_of[OUT, 0, 1] = sums[2], sums[3]
        else:
            input_grad, sums = norm_back(grad_middle, terms, tokens, None, vectors, 0, 0, None)
        rows_of[GAIN, depth, 0], rows_of[SHIFT, depth, 0] = sums[0], sums[1]
    while ring.busy():
        ring.pump()

    proj_grad = lax.ppermute(
        jnp.stack([finals[0]["proj"], finals[1]["proj"]]), EVERY, [(b, a) for a, b in spread(count, team)]
    )
    if quick:
        qkv_grad, up_grad, proj_grad, down_grad = place_grads(
            [m["qkv"] for m in finals], [m["up"] for m in finals], proj_grad,
            [m["down"] for m in finals], part, rest, me,
        )
    else:
        proj_grad = proj_grad.astype(WIDE)
        qkv_grad, up_grad, down_grad = (
            jnp.stack([m[name] for m in finals]).astype(WIDE) for name in ("qkv", "up", "down")
        )

    names = [(kind, depth, place) for kind in (OUT, GAIN, SHIFT, SCALE) for depth in (0, 1) for place in (0, 1)]
    token_sums = jnp.stack([rows_of[name] for name in names])
    full_qkv = lax.dynamic_update_slice(
        jnp.zeros((6, team, part), WIDE),
        jnp.concatenate(sums_qkv, axis=0).reshape(6, 1, part),
        (0, mine, 0),
    ).reshape(6, width)
    head_all = jnp.stack(head_sums).reshape(-1, heads, head_size).sum(axis=1).reshape(1, -1)
    head_all = jnp.pad(head_all, ((0, 0), (0, width - head_all.shape[1])))
    team_rows = jnp.concatenate([token_sums, full_qkv, head_all], axis=0)
    team_rows = team_rows + swap(team_rows, "core")
    if frames == 2:
        team_rows = team_rows + swap(team_rows, "frame")
    else:
        team_rows = lax.psum(team_rows, "frame")
    sums_up = jnp.concatenate(sums_up, axis=0).reshape(2, rest, hidden // rest)
    sums_up = jnp.pad(sums_up, ((0, 0), (0, 0), (0, (width - hidden) // rest))).reshape(2, width)
    split = jnp.concatenate([team_rows[:16], sums_up], axis=0)
    split, common = small_sum(split, team_rows[16:])
    vector_grads = lax.dynamic_slice_in_dim(split[:16], mine * (width // count), width // count, 1)
    vector_grads = vector_grads.reshape(4, 2, 2, -1)
    grad_bias_qkv = common[:6].reshape(2, -1)
    grad_bias_qkv = lax.dynamic_slice_in_dim(
        grad_bias_qkv, (here * team + mine) * qkv_bias.shape[1], qkv_bias.shape[1], 1
    )
    head_all = common[6, : 8 * head_size].reshape(2, 2, 2, head_size)
    return (
        activations,
        input_grad,
        qkv_grad,
        grad_bias_qkv,
        proj_grad,
        up_grad,
        split[16:, : hidden // rest],
        down_grad,
        vector_grads[0],
        vector_grads[1],
        vector_grads[2],
        vector_grads[3],
        head_all[:, 0],
        head_all[:, 1],
    )


def solution(mesh):
    scenes, frames = mesh.shape["scene"], mesh.shape["frame"]
    rest = scenes // 2
    outer = 4 if rest % 4 == 0 else rest
    grid = Mesh(mesh.devices.reshape(outer, rest // outer, 2, frames), EVERY)
    by_rows = P(EVERY, None)
    second = P(None, EVERY)
    second_rows = P(None, EVERY, None)
    last = P(None, None, EVERY)
    return jax.shard_map(
        on_device,
        mesh=grid,
        in_specs=(
            by_rows, by_rows, P(EVERY), P(EVERY), second_rows, second, second_rows, second_rows,
            second, second_rows, last, last, last, last, P(), P(),
        ),
        out_specs=(
            by_rows, by_rows, second_rows, second, second_rows, second_rows, second, second_rows,
            last, last, last, last, P(), P(),
        ),
        check_vma=False,
    )
```

```python
import jax
import jax.numpy as jnp
import numpy as np
from jax import lax
from jax.experimental import pallas as pl
from jax.experimental.pallas import tpu as pltpu
from jax.sharding import Mesh
from jax.sharding import PartitionSpec as P

EPSILON = 1e-06
FRAME_TOK = 64
LOW = jnp.bfloat16
WIDE = jnp.float32
EVERY = ("outer", "inner", "core", "frame")
REST = ("outer", "inner")
TEAM = ("core", "frame")
ROOT_HALF = 0.7071067811865476
ROOT_TWO_PI = 0.3989422804014327
MEBI = 1024 * 1024
OUT, GAIN, SHIFT, SCALE = 0, 4, 8, 12
HOPS = (0, 0, 1, 0, 1, 0, 1, 0) + (1, 0, 1, 0, 1, 0, 1, 0)


def dot(left, right):
    return jnp.dot(left, right, preferred_element_type=WIDE)


def dot_tn(left, right):
    return lax.dot_general(left, right, (((0,), (0,)), ((), ())), preferred_element_type=WIDE)


def dot_nt(left, right):
    return lax.dot_general(left, right, (((1,), (1,)), ((), ())), preferred_element_type=WIDE)


def normed(values):
    center = values - jnp.mean(values, axis=-1, keepdims=True)
    rate = lax.rsqrt(jnp.mean(center * center, axis=-1, keepdims=True) + EPSILON)
    return center * rate, rate


def normed_back(grad, unit, rate, gain):
    inner = grad * gain
    mean_one = jnp.mean(inner, axis=-1, keepdims=True)
    mean_two = jnp.mean(inner * unit, axis=-1, keepdims=True)
    return rate * (inner - mean_one - unit * mean_two)


def shape_of(shape, dtype):
    return jax.ShapeDtypeStruct(shape, dtype)


def call(kernel, outs, args, name, flops=0, scratch=(), scalars=0, far_in=(), far_out=()):
    hbm = pl.BlockSpec(memory_space=pltpu.HBM)
    vmem = pl.BlockSpec(memory_space=pltpu.VMEM)
    smem = pl.BlockSpec(memory_space=pltpu.SMEM)
    in_specs = [smem if i < scalars else hbm if i in far_in else vmem for i in range(len(args))]
    bytes_all = sum(m.size * m.dtype.itemsize for m in args)
    bytes_all += sum(int(np.prod(s.shape)) * s.dtype.itemsize for s in outs)
    sized = [s for s in scratch if hasattr(s, "shape") and s.memory_space == pltpu.VMEM]
    held = sum(int(np.prod(s.shape)) * s.dtype.itemsize for s in sized)
    limit = (held * 5 // 4 + bytes_all * 2 // 5 if flops else bytes_all) + (8 if flops else 3) * MEBI
    args = [pltpu.with_memory_space_constraint(m, pltpu.HBM) if i in far_in else m for i, m in enumerate(args)]
    outs = [pltpu.HBM(m.shape, m.dtype) if i in far_out else m for i, m in enumerate(outs)]
    return pl.pallas_call(
        kernel,
        out_shape=list(outs),
        in_specs=in_specs,
        out_specs=[hbm if i in far_out else vmem for i in range(len(outs))],
        scratch_shapes=list(scratch),
        compiler_params=pltpu.CompilerParams(vmem_limit_bytes=limit),
        cost_estimate=pl.CostEstimate(flops=flops, bytes_accessed=bytes_all, transcendentals=0),
        name=name,
    )(*args)


def swap(values, axis):
    return lax.ppermute(values, axis, [(0, 1), (1, 0)])


def cross(values):
    return lax.ppermute(values, TEAM, [(0, 3), (1, 2), (2, 1), (3, 0)])


def team_gather(values, work=None, pump=None):
    if lax.axis_size("frame") == 2:
        far = swap(values, "frame")
        near = swap(work(values) if work else values, "core")
        far = pump(far) if pump else far
        return [values, far, near, swap(far, "core")]
    both = lax.all_gather(values, "frame", axis=0, tiled=True)
    return [both, swap(both, "core")]


def team_sum(own, peer, work=None, pump=None):
    if lax.axis_size("frame") == 2:
        far = own[1] + swap(peer[1], "core").astype(WIDE)
        came = swap(far.astype(LOW), "frame")
        near = swap(work(peer[0]) if work else peer[0], "core")
        came = pump(came) if pump else came
        return [own[0], near, came]
    total = own[0] + swap(peer[0], "core").astype(WIDE)
    return [lax.psum_scatter(total.astype(LOW), "frame", scatter_dimension=0, tiled=True).astype(WIDE)]


def exchange_columns(values):
    parts = values.transpose(1, 0, 2)
    frames = lax.axis_size("frame")
    parts = parts.reshape((2, frames) + parts.shape[1:])
    both = lax.all_to_all(parts, "frame", 1, 1, tiled=True)
    here = lax.axis_index("core")
    keep = lax.dynamic_index_in_dim(both, here, 0, keepdims=False)
    came = swap(lax.dynamic_index_in_dim(both, 1 - here, 0, keepdims=False), "core")
    out = jnp.stack([jnp.where(here == 0, keep, came), jnp.where(here == 0, came, keep)], axis=0)
    return out.reshape((2 * frames,) + out.shape[2:])


SMALL_ROWS = 16


def split_weights(depth, weights, vectors, part, rest, me):
    qkv, up = weights
    _, rows, width = qkv.shape
    width //= 3
    hidden = up.shape[2] // 4
    lanes = hidden // rest
    extra = SMALL_ROWS if vectors else 0

    far = list(vectors)

    def kernel(me_ref, qkv_ref, up_ref, *refs):
        outs, small = refs[len(far) : len(far) + 4], refs[len(far) + 4 : -1]
        copies = []
        for source, target in zip(refs, small):
            copies.append(pltpu.make_async_copy(source, target, refs[-1].at[len(copies)]))
            copies[-1].start()
        wait_all(copies)
        for away, out in enumerate(outs):
            member = jnp.bitwise_xor(me_ref[0], away)
            for s in range(3):
                start = pl.multiple_of(s * width + member * part, 128)
                out[:rows, s * part : (s + 1) * part] = qkv_ref[depth, :, pl.ds(start, part)]
            for f in range(rest):
                start = pl.multiple_of((f * 4 + member) * lanes, 128)
                at = 3 * part + f * lanes
                out[:rows, at : at + lanes] = up_ref[depth, :, pl.ds(start, lanes)]
            if not vectors:
                continue
            out[rows:, :] = jnp.zeros((extra, out.shape[1]), LOW)
            bias_qkv, bias_up, ids = small[:3]
            for i, ref in enumerate(small[3:]):
                for d in range(2):
                    for j in range(2):
                        at = rows + 4 * i + 2 * d + j
                        out[at : at + 1, : ref.shape[2]] = ref[d, j : j + 1, :]
            out[rows : rows + 2, 128 : 128 + bias_qkv.shape[1]] = bias_qkv[...]
            out[rows : rows + 2, 256 : 256 + bias_up.shape[1]] = bias_up[...]
            out[rows : rows + 1, 512 : 512 + ids.shape[1]] = ids[...].astype(WIDE).astype(LOW)

    out = shape_of((rows + extra, 3 * part + hidden), qkv.dtype)
    scratch = [pltpu.VMEM(m.shape, m.dtype) for m in far] + [pltpu.SemaphoreType.DMA((len(far) + 1,))]
    args = [me, qkv, up, *far]
    return call(kernel, [out] * 4, args, "split_weights", 0, scratch, 1, far_in=range(3, 3 + len(far)))


def pack_weights(pieces, proj, down, depth, part, me, vectors):
    rows = proj.shape[1]
    unit = 4 * rows
    hidden = pieces[0].shape[1] - 3 * part

    def kernel(me_ref, p0, p1, p2, p3, proj_ref, down_ref, attn, up, small):
        for away, ref in enumerate((p0, p1, p2, p3)):
            member = jnp.bitwise_xor(me_ref[0], away)
            start = pl.multiple_of(member * rows, rows)
            attn[pl.ds(start, rows), : 3 * part] = ref[:rows, : 3 * part]
            up[pl.ds(start, rows), :] = ref[:rows, 3 * part :]
            if vectors:
                small[member] = ref[rows:, :640]
        for j in range(4):
            attn[j * rows : (j + 1) * rows, 3 * part :] = proj_ref[depth, :, j * part : (j + 1) * part]
        up[unit:, :] = down_ref[depth]
        if vectors:
            attn[unit:, :] = jnp.zeros((SMALL_ROWS, 4 * part), LOW)
            for at, start, size in ((0, 0, 32), (128, 128, 96), (512, 256, 128)):
                joined = [small[m, :, start : start + size].astype(WIDE) for m in range(4)]
                value = jnp.concatenate(joined, axis=1).astype(LOW)
                attn[unit:, at : at + 4 * size] = value

    extra = SMALL_ROWS if vectors else 0
    outs = [shape_of((unit + extra, 4 * part), LOW), shape_of((2 * unit, hidden), LOW)]
    scratch = [pltpu.VMEM((4, SMALL_ROWS, 640), LOW)]
    return call(kernel, outs, [me, *pieces, proj, down], "pack_weights", scratch=scratch, scalars=1)


def unpack_vectors(source, table, me):
    rest, _, width = source.shape
    part = width // 4

    def kernel(me_ref, table_ref, *refs):
        vec, bias_qkv, bias_up, small, whole, semaphores = refs[source.count :]
        wait_all(source.start(refs[: source.count], table_ref, small, semaphores))
        for f in range(rest):
            vec[:, f * 128 : (f + 1) * 128] = small[f, :, :128].astype(WIDE)
            whole[:, f * 384 : (f + 1) * 384] = small[f, :, 128:512].astype(WIDE)
            start = pl.multiple_of(512 + me_ref[0] * 128, 128)
            bias_up[:, f * 128 : (f + 1) * 128] = small[f, :, pl.ds(start, 128)].astype(WIDE)
        for s in range(3):
            start = pl.multiple_of(s * width + me_ref[0] * part, 128)
            bias_qkv[:, s * part : (s + 1) * part] = whole[:, pl.ds(start, part)]

    outs = [shape_of((16, width), WIDE), shape_of((16, 3 * part), WIDE), shape_of((16, width), WIDE)]
    scratch = [
        pltpu.VMEM((rest, SMALL_ROWS, width), LOW),
        pltpu.VMEM((16, 3 * width), WIDE),
        pltpu.SemaphoreType.DMA((source.count,)),
    ]
    args = [me, table, *source.args]
    return call(kernel, outs, args, "unpack_vectors", 0, scratch, 2, far_in=range(2, 2 + source.count))


def spread(count, team):
    rest = count // team
    return [(i, (i % rest) * team + i // rest) for i in range(count)]


def widen(rows, width):
    height, columns = rows.shape
    parts = columns // width
    if parts == 1:
        return rows
    return rows.reshape(height, parts, width).transpose(1, 0, 2).reshape(parts * height, width)


def narrow(stacked, height):
    lead = stacked.shape[:-2]
    parts = stacked.shape[-2] // height
    if parts == 1:
        return stacked
    width = stacked.shape[-1]
    shaped = stacked.reshape(lead + (parts, height, width))
    return jnp.moveaxis(shaped, -3, -2).reshape(lead + (height, parts * width))


def ring_order(outer, inner):
    order = []
    for a in range(outer):
        row = range(1, inner) if a % 2 == 0 else range(inner - 1, 0, -1)
        order += [a * inner + b for b in row]
    return order + [a * inner for a in range(outer - 1, -1, -1)]


def ring_table():
    outer, inner = lax.axis_size("outer"), lax.axis_size("inner")
    order = ring_order(outer, inner)
    rest = outer * inner
    place = {team: i for i, team in enumerate(order)}
    table = np.array(
        [
            [[order[(place[f] + sign * k) % rest] for k in range(rest)] for sign in (-1, 1)]
            for f in range(rest)
        ],
        np.int32,
    )
    here = lax.axis_index("outer") * inner + lax.axis_index("inner")
    return lax.dynamic_index_in_dim(jnp.asarray(table), here, 0, keepdims=False)


def ring_shift(values, sign):
    order = ring_order(lax.axis_size("outer"), lax.axis_size("inner"))
    rest = len(order)
    return lax.ppermute(values, REST, [(order[i], order[(i + sign) % rest]) for i in range(rest)])


def ring_step(low_half, high_half):
    low_half, high_half = ring_shift(low_half, 1), ring_shift(high_half, -1)
    return lax.optimization_barrier((low_half, high_half))


class RingGather:
    def __init__(self, shard, cut, rest):
        self.steps = rest // 2
        self.cut = cut
        self.back, self.ahead = [shard], [shard]
        self.came = (ring_shift(shard, 1), ring_shift(shard, -1))

    def take(self, came):
        self.back.append(came[0])
        self.ahead.append(came[1])
        self.came = None
        if len(self.back) == self.steps:
            came = (came[0][: self.cut], came[1][self.cut :])
        if len(self.back) <= self.steps:
            self.came = (ring_shift(came[0], 1), ring_shift(came[1], -1))

    def rows(self, first, count):
        out = []
        for side, arrays in enumerate((self.back, self.ahead)):
            out += [(m, side, k, 0, first, count) for k, m in enumerate(arrays[: self.steps]) if k or not side]
        stop = min(first + count, self.cut)
        if stop > first:
            out.append((self.back[self.steps], 0, self.steps, 0, first, stop - first))
        start = max(first, self.cut)
        if start < first + count:
            out.append(
                (self.ahead[self.steps], 1, self.steps, start - first, start - self.cut, first + count - start)
            )
        return Pieces(out, 2 * self.steps, count)


def steps(count, ring):
    came = ()
    for _ in range(count):
        if ring.came is None:
            break
        came = tie(*ring.came)
        ring.take(came)
    return came


class Pieces:
    def __init__(self, entries, rest, rows):
        self.entries = entries
        self.args = [entry[0] for entry in entries]
        self.count = len(entries)
        self.shape = (rest, rows, self.args[0].shape[1])

    def start(self, refs, table_ref, target, semaphores):
        copies = []
        for ref, (_, side, k, first, begin, rows) in zip(refs, self.entries):
            spot = target.at[table_ref[side, k], pl.ds(first, rows), :]
            copies.append(pltpu.make_async_copy(ref.at[pl.ds(begin, rows), :], spot, semaphores.at[len(copies)]))
            copies[-1].start()
        return copies


class Whole:
    count = 1

    def __init__(self, array, first, rows):
        self.first = first
        self.args = [array]
        self.shape = (array.shape[0], rows, array.shape[2])

    def start(self, refs, table_ref, target, semaphores):
        source = refs[0].at[:, pl.ds(self.first, self.shape[1]), :]
        copy = pltpu.make_async_copy(source, target, semaphores.at[0])
        copy.start()
        return [copy]


def wait_all(copies):
    for copy in copies:
        copy.wait()


def tie(*values):
    return lax.optimization_barrier(values)


class RingSums:
    def __init__(self, rest):
        self.steps = rest // 2
        self.active = []
        self.waiting = []
        self.came = None
        self.started = []
        self.plan = iter(HOPS)

    def work(self, value):
        if next(self.plan):
            if self.came is not None:
                self.came = tie(*self.came, value)[:2]
            self.hop()
        started, self.started = self.started, []
        return tie(value, *started)[0] if started else value

    def pump(self, value):
        return self.hop(value) if next(self.plan) else value

    def add(self, ahead, behind, own, done):
        self.waiting.append(
            {"parts": (ahead, behind), "own": own, "rows": own.shape[0], "done": done, "hop": 0}
        )
        self.started.append(own)

    def hop(self, *values):
        if self.came is not None:
            tied = tie(*values, *self.came)
            values, self.came = tied[: len(values)], tied[len(values) :]
        rings = self.active + self.waiting
        self.waiting = []
        result = values if len(values) != 1 else values[0]
        if not rings:
            return result
        columns = rings[0]["own"].shape[1]
        moving, start, ended, plans, args = 0, 0, [], [], []
        for ring in rings:
            rows, hop = ring["rows"], ring["hop"]
            came_rows = (0, rows // 2, rows)[min(hop, 2)]
            came_at = start
            start += came_rows
            if hop == self.steps:
                plans.append((rows, came_at, came_rows, None))
                args.append(ring["own"])
                ended.append(ring)
            else:
                plans.append((rows if hop else rows // 2, came_at, came_rows, moving))
                args += [ring["parts"][side][hop] for side in range(2)]
                moving += rows if hop else rows // 2
            ring["hop"] += 1
        came = list(self.came) if self.came is not None else []
        size = sum(m.shape[0] for m in args)

        def kernel(*refs):
            came_refs = refs[: len(came)]
            part_refs = refs[len(came) : len(came) + len(args)]
            outs, local, semaphores = refs[len(came) + len(args) : -2], refs[-2], refs[-1]
            copies, at = [], 0
            for ref in part_refs:
                spot = local.at[pl.ds(at, ref.shape[0]), :]
                copies.append(pltpu.make_async_copy(ref, spot, semaphores.at[len(copies)]))
                copies[-1].start()
                at += ref.shape[0]
            wait_all(copies)
            final, at = (2 if moving else 0), 0
            for rows, came_at, came_rows, goes_to in plans:
                others = [ref[came_at : came_at + came_rows, :] for ref in came_refs] if came_rows else []
                if goes_to is None:
                    total = local[at : at + rows, :].astype(WIDE)
                    total = total + others[0].astype(WIDE) + others[1].astype(WIDE)
                    outs[final][...] = total[: rows // 2]
                    outs[final + 1][...] = total[rows // 2 :]
                    final += 2
                    at += rows
                    continue
                for side in range(2):
                    outs[side][goes_to : goes_to + rows, :] = local[at : at + rows, :]
                    if came_rows:
                        first = side * came_rows if came_rows < rows else 0
                        total = local[at + first : at + first + came_rows, :].astype(WIDE)
                        total = (total + others[side].astype(WIDE)).astype(LOW)
                        outs[side][goes_to + first : goes_to + first + came_rows, :] = total
                    at += rows

        outs = [shape_of((moving, columns), LOW)] * 2 if moving else []
        for ring in ended:
            outs += [shape_of((ring["rows"] // 2, columns), WIDE)] * 2
        scratch = [pltpu.VMEM((size, columns), LOW), pltpu.SemaphoreType.DMA((len(args),))]
        far_in = range(len(came), len(came) + len(args))
        res = call(kernel, outs, came + args, "ring_add", 0, scratch, far_in=far_in)
        at = 2 if moving else 0
        for ring in ended:
            ring["done"](res[at], res[at + 1])
            at += 2
        self.active = [ring for ring in rings if ring["hop"] <= self.steps]
        self.started += list(res[:2])
        self.came = (ring_shift(res[0], 1), ring_shift(res[1], -1)) if moving else None
        return result

    def busy(self):
        return bool(self.active or self.waiting)


def hop_places(rest):
    steps = rest // 2
    return [(1, k) for k in range(steps, 0, -1)] + [(0, k) for k in range(steps, 0, -1)] + [(0, 0)]


def rest_sum(parts):
    return lax.psum_scatter(parts, REST, scatter_dimension=0, tiled=False)


def small_gather(values):
    out = values[None]
    for axis in ("frame", "core", "inner", "outer"):
        size, here, step = lax.axis_size(axis), lax.axis_index(axis), 1
        while step < size:
            came = lax.ppermute(out, axis, [(i, i ^ step) for i in range(size)])
            first = (here & step) == 0
            out = jnp.concatenate([jnp.where(first, out, came), jnp.where(first, came, out)], axis=0)
            step *= 2
    return out


def small_sum(split, common):
    for axis in ("outer", "inner"):
        size, here = lax.axis_size(axis), lax.axis_index(axis)
        step = size // 2
        while step >= 1:
            half = split.shape[1] // 2
            bit = (here // step) % 2
            keep = lax.dynamic_slice_in_dim(split, bit * half, half, 1)
            send = lax.dynamic_slice_in_dim(split, (1 - bit) * half, half, 1)
            pairs = [(i, i ^ step) for i in range(size)]
            packed = jnp.concatenate([send.reshape(-1), common.reshape(-1)])
            came = lax.ppermute(packed, axis, pairs)
            split = keep + came[: keep.size].reshape(keep.shape)
            common = common + came[keep.size :].reshape(common.shape)
            step //= 2
    return split, common


def head_means(part, head_size):
    row = lax.broadcasted_iota(jnp.int32, (part, part), 0) // head_size
    column = lax.broadcasted_iota(jnp.int32, (part, part), 1) // head_size
    return jnp.where(row == column, 1.0 / head_size, 0.0).astype(LOW)


def head_mean(values, matrix):
    high = values.astype(LOW)
    rest = (values - high.astype(WIDE)).astype(LOW)
    return dot(high, matrix) + dot(rest, matrix)


def head_normed(values, matrix):
    center = values - head_mean(values, matrix)
    rate = lax.rsqrt(head_mean(center * center, matrix) + EPSILON)
    return center * rate, rate


def join(refs, out_ref):
    start = 0
    for ref in refs:
        out_ref[start : start + ref.shape[0], :] = ref[...]
        start += ref.shape[0]


def spans(refs):
    start = 0
    for ref in refs:
        yield start, start + ref.shape[0], ref
        start += ref.shape[0]


def flat_rows(ref, first, height, columns):
    block = ref[:, first : first + height, columns]
    return block.reshape(block.shape[0] * height, block.shape[2])


def tiles_of(total, group, block):
    for base in range(0, total, group):
        for start in range(base, base + group, block):
            yield start, base


def allowed_of(ids_col, ids_row, start, base, block, group, use_frame):
    if use_frame:
        row = lax.broadcasted_iota(jnp.int32, (block, group), 0) // FRAME_TOK
        column = lax.broadcasted_iota(jnp.int32, (block, group), 1) // FRAME_TOK
        return row == column
    return ids_col[start : start + block, :] == ids_row[:, base : base + group]


def plan(frames, rows, use_frame):
    group = min(4 * FRAME_TOK, frames * rows) if use_frame else frames * rows
    return group, min(group, 256)


def part_shapes(pieces, width):
    half = len(pieces) // 2
    return [shape_of((m.shape[0], width), WIDE if i < half else LOW) for i, m in enumerate(pieces)]


def load_semaphores(sources):
    return [pltpu.SemaphoreType.DMA((source.count,)) for source in sources]


def start_loads(sources, table_ref, far_refs, targets, semaphores):
    at, copies = 0, []
    for source, target, semaphore in zip(sources, targets, semaphores):
        copies.append(source.start(far_refs[at : at + source.count], table_ref, target, semaphore))
        at += source.count
    return copies


def attn_forward(pieces, weights, bias, head_gain, head_shift, ids, head_size, frames, use_frame, vectors=None):
    attn, proj, height, wide, table = weights
    sources = [attn] if proj is None else [attn, proj]
    far = [m for source in sources for m in source.args]
    rest, unit, _ = attn.shape
    width, part = rest * unit, head_gain.shape[-1]
    total = sum(m.shape[0] for m in pieces)
    count = len(pieces)
    group, block = plan(frames, total // (2 * frames), use_frame)
    lanes = min(128, part)
    per = lanes // head_size
    scale = head_size ** (-0.5)
    more = 0 if vectors is None else 1

    def kernel(table_ref, *refs):
        far_refs, refs = refs[: len(far)], refs[len(far) :]
        semaphores, refs = refs[-len(sources) :], refs[: -len(sources)]
        targets, refs = refs[-len(sources) :], refs[: -len(sources)]
        copies = start_loads(sources, table_ref, far_refs, targets, semaphores)
        wq, wp = targets[0], targets[-1]
        piece_refs = refs[:count]
        bias_ref, gain_ref, shift_ref, ids_col, ids_row = refs[count : count + 5]
        first, raw, qkv, lse, flat = refs[count + 5 + more : count + 10 + more]
        outs = refs[count + 10 + more :]
        if more:
            vec = refs[count + 5]
            for start, stop, ref in spans(piece_refs):
                unit_one, _ = normed(ref[...].astype(WIDE))
                value = unit_one * row_of(vec, GAIN, 0, 0) + row_of(vec, SHIFT, 0, 0)
                first[start:stop, :] = value.astype(LOW)
        else:
            join(piece_refs, first)
        matrix = head_means(part, head_size)
        for group_copies in copies:
            wait_all(group_copies)
        mixed = dot(first[...], flat_rows(wq, 0, unit, slice(0, 3 * part))) + bias_ref[...]
        raw[...] = mixed[:, : 2 * part]
        for i in range(2):
            unit_i, _ = head_normed(mixed[:, i * part : (i + 1) * part], matrix)
            value = unit_i * gain_ref[i : i + 1, :] + shift_ref[i : i + 1, :]
            qkv[:, i * part : (i + 1) * part] = value.astype(LOW)
        qkv[:, 2 * part :] = mixed[:, 2 * part :].astype(LOW)
        place = lax.broadcasted_iota(jnp.int32, (1, lanes), 1) // head_size
        for start, base in tiles_of(total, group, block):
            allowed = allowed_of(ids_col, ids_row, start, base, block, group, use_frame)
            stats = []
            for lane in range(0, part, lanes):
                query = qkv[start : start + block, lane : lane + lanes] * jnp.asarray(scale, LOW)
                key = qkv[base : base + group, part + lane : part + lane + lanes]
                value = qkv[base : base + group, 2 * part + lane : 2 * part + lane + lanes]
                out = jnp.zeros((block, lanes), WIDE)
                for h in range(per):
                    mask = place == h
                    scores = dot_nt(jnp.where(mask, query, jnp.zeros_like(query)), key)
                    scores = jnp.where(allowed, scores, -jnp.inf)
                    top = jnp.max(scores, axis=-1, keepdims=True)
                    weight = jnp.exp(scores - top)
                    norm = jnp.sum(weight, axis=-1, keepdims=True)
                    stats.append(top + jnp.log(norm))
                    probs = (weight * (1.0 / norm)).astype(LOW)
                    out = jnp.where(mask, dot(probs, value), out)
                flat[start : start + block, lane : lane + lanes] = out.astype(LOW)
            lse[start : start + block, :] = jnp.concatenate(stats, axis=1)
        for a in range(0, width, wide):
            b = a + wide
            chunk = flat_rows(wp, a // wide * height, height, slice(wp.shape[2] - wide, wp.shape[2]))
            for start, stop, ref in spans(outs):
                ref[:, a:b] = dot(flat[start:stop, :], chunk).astype(ref.dtype)

    outs = [
        shape_of((total, width), LOW),
        shape_of((total, 2 * part), WIDE),
        shape_of((total, 3 * part), LOW),
        shape_of((total, part // head_size), WIDE),
        shape_of((total, part), LOW),
    ] + part_shapes(pieces, width)
    outs += [shape_of(source.shape, LOW) for source in sources]
    args = [table] + far + list(pieces)
    args += [bias, head_gain, head_shift, ids.reshape(-1, 1), ids.reshape(1, -1)]
    args += [vectors] if more else []
    flops = 2 * total * (width * 4 * part + group * 2 * part)
    scratch = load_semaphores(sources)
    res = call(kernel, outs, args, "attn_forward", flops, scratch, 1, far_in=range(1, 1 + len(far)))
    weights = (res[5 + count], None if proj is None else res[6 + count], height, wide)
    return res[:5], res[5 : 5 + count // 2], res[5 + count // 2 : 5 + count], weights


def attn_backward(pieces, weights, head_gain, kept, ids, head_size, frames, use_frame):
    _, raw, qkv, lse, _ = kept
    attn, proj, height, wide = weights
    rest, unit, _ = attn.shape
    width, part = rest * unit, head_gain.shape[-1]
    total = sum(m.shape[0] for m in pieces)
    count = len(pieces)
    group, block = plan(frames, total // (2 * frames), use_frame)
    lanes = min(128, part)
    per = lanes // head_size
    scale = head_size ** (-0.5)
    extra = 0 if proj is None else 1

    def kernel(*refs):
        piece_refs, wq, wp = refs[:count], refs[count], refs[count + extra]
        refs = refs[extra + 1 :]
        gain_ref, raw_ref, qkv_ref, lse_ref, ids_col, ids_row = refs[count : count + 6]
        joined, low_mixed, sums, head_sums = refs[count + 6 : count + 10]
        outs = refs[count + 10 : count + 10 + count]
        grad_out, grad_three = refs[count + 10 + count :]
        join(piece_refs, joined)
        grad_flat = jnp.zeros((total, part), WIDE)
        for a in range(0, width, wide):
            b = a + wide
            chunk = flat_rows(wp, a // wide * height, height, slice(wp.shape[2] - wide, wp.shape[2]))
            grad_flat += dot_nt(joined[:, a:b], chunk)
        grad_out[...] = grad_flat.astype(LOW)
        place = lax.broadcasted_iota(jnp.int32, (1, lanes), 1) // head_size
        for start, base in tiles_of(total, group, block):
            allowed = allowed_of(ids_col, ids_row, start, base, block, group, use_frame)
            stats = lse_ref[start : start + block, :]
            for lane in range(0, part, lanes):
                query = qkv_ref[start : start + block, lane : lane + lanes] * jnp.asarray(scale, LOW)
                key = qkv_ref[base : base + group, part + lane : part + lane + lanes]
                value = qkv_ref[base : base + group, 2 * part + lane : 2 * part + lane + lanes]
                grad_here = grad_out[start : start + block, lane : lane + lanes]
                grad_q = jnp.zeros((block, lanes), WIDE)
                grad_k = jnp.zeros((group, lanes), WIDE)
                grad_v = jnp.zeros((group, lanes), WIDE)
                for h in range(per):
                    mask = place == h
                    head = lane // head_size + h
                    scores = dot_nt(jnp.where(mask, query, jnp.zeros_like(query)), key)
                    probs = jnp.exp(jnp.where(allowed, scores - stats[:, head : head + 1], -jnp.inf))
                    grad_p = dot_nt(jnp.where(mask, grad_here, jnp.zeros_like(grad_here)), value)
                    delta = jnp.sum(probs * grad_p, axis=-1, keepdims=True)
                    grad_s = (probs * (grad_p - delta)).astype(LOW)
                    grad_q = jnp.where(mask, dot(grad_s, key), grad_q)
                    grad_k = jnp.where(mask, dot_tn(grad_s, query), grad_k)
                    grad_v = jnp.where(mask, dot_tn(probs.astype(LOW), grad_here), grad_v)
                grad_three[start : start + block, lane : lane + lanes] = grad_q * scale
                for at, grad in ((part, grad_k), (2 * part, grad_v)):
                    spot = (slice(base, base + group), slice(at + lane, at + lane + lanes))
                    if start == base:
                        grad_three[spot] = grad
                    else:
                        grad_three[spot] = grad_three[spot] + grad
        matrix = head_means(part, head_size)
        for i in range(2):
            here = slice(i * part, (i + 1) * part)
            grad = grad_three[:, here]
            unit_i, rate = head_normed(raw_ref[:, here], matrix)
            head_sums[i : i + 1, :] = jnp.sum(grad * unit_i, axis=0, keepdims=True)
            head_sums[2 + i : 3 + i, :] = jnp.sum(grad, axis=0, keepdims=True)
            inner = grad * gain_ref[i : i + 1, :]
            mean_one = head_mean(inner, matrix)
            mean_two = head_mean(inner * unit_i, matrix)
            result = rate * (inner - mean_one - unit_i * mean_two)
            sums[:, here] = jnp.sum(result, axis=0, keepdims=True)
            low_mixed[:, here] = result.astype(LOW)
        result = grad_three[:, 2 * part :]
        sums[:, 2 * part :] = jnp.sum(result, axis=0, keepdims=True)
        low_mixed[:, 2 * part :] = result.astype(LOW)
        weight = flat_rows(wq, 0, unit, slice(0, 3 * part))
        for start, stop, ref in spans(outs):
            ref[...] = dot_nt(low_mixed[start:stop, :], weight).astype(ref.dtype)

    outs = [
        shape_of((total, width), LOW),
        shape_of((total, 3 * part), LOW),
        shape_of((1, 3 * part), WIDE),
        shape_of((4, part), WIDE),
    ] + part_shapes(pieces, width)
    scratch = [pltpu.VMEM((total, part), LOW), pltpu.VMEM((total, 3 * part), WIDE)]
    args = list(pieces) + [attn] + ([] if proj is None else [proj])
    args += [head_gain, raw, qkv, lse, ids.reshape(-1, 1), ids.reshape(1, -1)]
    flops = 2 * total * (width * 4 * part + group * 5 * part)
    res = call(kernel, outs, args, "attn_backward", flops, scratch)
    return res[:4], res[4 : 4 + count // 2], res[4 + count // 2 :]


def attn_weight_grads(first, low_mixed, flat, att_low, rest, height, table):
    width, part = first.shape[1], flat.shape[1]
    unit = width // rest
    wide = width * height // unit
    places = hop_places(rest)
    steps = rest // 2

    def kernel(table_ref, first_ref, mixed_ref, flat_ref, att_ref, *refs):
        outs, packed, semaphores = refs[:-2], refs[-2], refs[-1]
        product = dot_tn(first_ref[...], mixed_ref[...]).astype(LOW)
        packed[:, :, : 3 * part] = product.reshape(rest, unit, 3 * part)
        product = dot_tn(flat_ref[...], att_ref[...]).astype(LOW)
        for j in range(unit // height):
            chunk = product[:, j * wide : (j + 1) * wide].reshape(rest, height, wide)
            packed[:, j * height : (j + 1) * height, 3 * part :] = chunk
        copies = []
        for i, (side, k) in enumerate(places):
            first_row = unit // 2 if i == steps else 0
            source = packed.at[table_ref[side, k], pl.ds(first_row, outs[i].shape[0]), :]
            copies.append(pltpu.make_async_copy(source, outs[i], semaphores.at[i]))
            copies[-1].start()
        wait_all(copies)

    flops = 8 * first.shape[0] * width * part
    outs = [shape_of((unit // 2 if k == steps else unit, 4 * part), LOW) for _, k in places]
    scratch = [pltpu.VMEM((rest, unit, 4 * part), LOW), pltpu.SemaphoreType.DMA((len(places),))]
    args = [table, first, low_mixed, flat, att_low]
    res = call(kernel, outs, args, "attn_weight_grads", flops, scratch, 1, far_out=range(len(outs)))
    return res[:steps], res[steps : 2 * steps], res[2 * steps]


def mlp_weight_grads(second, pre_low, act, branch_low, rest, table):
    width, hidden = second.shape[1], act.shape[1]
    rows = width // rest
    places = hop_places(rest)
    steps = rest // 2

    def kernel(table_ref, second_ref, pre_ref, act_ref, branch_ref, *refs):
        outs, packs, semaphores = refs[:-3], refs[-3:-1], refs[-1]
        copies = []
        for which, (left, right) in enumerate(((second_ref, pre_ref), (act_ref, branch_ref))):
            pack = packs[which]
            pack[...] = dot_tn(left[...], right[...]).astype(LOW).reshape(pack.shape)
            for i, (side, k) in enumerate(places):
                if k == steps and i // steps != which:
                    continue
                spot = outs[i].at[pl.ds(0 if k == steps else which * rows, rows), :]
                source = pack.at[table_ref[side, k]]
                copies.append(pltpu.make_async_copy(source, spot, semaphores.at[len(copies)]))
                copies[-1].start()
        wait_all(copies)

    flops = 4 * second.shape[0] * width * hidden
    outs = [shape_of((rows if k == steps else 2 * rows, width), LOW) for _, k in places]
    scratch = [pltpu.VMEM((rest, rows, width), LOW)] * 2 + [pltpu.SemaphoreType.DMA((2 * len(places),))]
    args = [table, second, pre_low, act, branch_low]
    res = call(kernel, outs, args, "mlp_weight_grads", flops, scratch, 1, far_out=range(len(outs)))
    return res[:steps], res[steps : 2 * steps], res[2 * steps]


def mlp_forward(pieces, sources, table, bias):
    rest, unit, hidden = sources[0].shape
    width = rest * unit
    far = [m for source in sources for m in source.args]
    total = sum(m.shape[0] for m in pieces)
    count = len(pieces)

    def kernel(table_ref, *refs):
        far_refs, refs, (up, down), semaphores = refs[: len(far)], refs[len(far) : -4], refs[-4:-2], refs[-2:]
        copies, more_copies = start_loads(sources, table_ref, far_refs, (up, down), semaphores)
        piece_refs = refs[:count]
        bias_ref = refs[count]
        second, act, slope = refs[count + 1 : count + 4]
        outs = refs[count + 4 :]
        join(piece_refs, second)
        wait_all(copies)
        pre = dot(second[...], flat_rows(up, 0, unit, slice(None))) + bias_ref[...]
        below = 0.5 * (1.0 + lax.erf(pre * ROOT_HALF))
        act[...] = (pre * below).astype(LOW)
        slope[...] = (below + pre * (ROOT_TWO_PI * jnp.exp(-0.5 * pre * pre))).astype(LOW)
        wait_all(more_copies)
        weight = flat_rows(down, 0, down.shape[1], slice(None))
        for start, stop, ref in spans(outs):
            ref[...] = dot(act[start:stop, :], weight).astype(ref.dtype)

    outs = [
        shape_of((total, width), LOW),
        shape_of((total, hidden), LOW),
        shape_of((total, hidden), LOW),
    ] + part_shapes(pieces, width)
    outs += [shape_of(source.shape, LOW) for source in sources]
    args = [table] + far + list(pieces) + [bias]
    flops, far_in = 4 * total * width * hidden, range(1, 1 + len(far))
    res = call(kernel, outs, args, "mlp_forward", flops, load_semaphores(sources), 1, far_in=far_in)
    return res[:3], res[3 : 3 + count // 2], res[3 + count // 2 : 3 + count], res[3 + count :]


def mlp_backward(pieces, weight_up, weight_down, slope):
    rest, unit, hidden = weight_up.shape
    width = rest * unit
    total = sum(m.shape[0] for m in pieces)
    count = len(pieces)

    def kernel(*refs):
        piece_refs = refs[:count]
        up, down, slope_ref = refs[count : count + 3]
        joined, low_pre, sums = refs[count + 3 : count + 6]
        outs = refs[count + 6 :]
        join(piece_refs, joined)
        weight = flat_rows(down, 0, down.shape[1], slice(None))
        grad = dot_nt(joined[...], weight) * slope_ref[...].astype(WIDE)
        sums[...] = jnp.sum(grad, axis=0, keepdims=True)
        low_pre[...] = grad.astype(LOW)
        weight = flat_rows(up, 0, unit, slice(None))
        for start, stop, ref in spans(outs):
            ref[...] = dot_nt(low_pre[start:stop, :], weight).astype(ref.dtype)

    outs = [
        shape_of((total, width), LOW),
        shape_of((total, hidden), LOW),
        shape_of((1, hidden), WIDE),
    ] + part_shapes(pieces, width)
    args = list(pieces) + [weight_up, weight_down, slope]
    res = call(kernel, outs, args, "mlp_backward", 4 * total * width * hidden)
    return res[:3], res[3 : 3 + count // 2], res[3 + count // 2 :]


def added(refs):
    total = refs[0][...]
    for ref in refs[1:]:
        total = total + ref[...].astype(WIDE)
    return total


def row_of(vectors, kind, depth, which):
    at = kind + 2 * depth + which
    return vectors[at : at + 1, :]


def branch_norm(stream, terms, vectors, depth, which):
    after = (depth, 1) if which == 0 else (depth + 1, 0)

    def kernel(stream_ref, *refs):
        (vec, branch, result, low), term_refs = refs[-4:], refs[:-4]
        value = added(term_refs) + row_of(vec, OUT, depth, which)
        branch[...] = value
        value = stream_ref[...].astype(WIDE) + row_of(vec, SCALE, depth, which) * value
        result[...] = value
        unit, _ = normed(value)
        low[...] = (unit * row_of(vec, GAIN, *after) + row_of(vec, SHIFT, *after)).astype(LOW)

    outs = [shape_of(stream.shape, WIDE), shape_of(stream.shape, WIDE), shape_of(stream.shape, LOW)]
    return call(kernel, outs, [stream, *terms, vectors], "branch_norm")


def turn(middle, terms, cotangent, vectors):
    def kernel(middle_ref, *refs):
        (cot, vec, result, low, sums), term_refs = refs[-5:], refs[:-5]
        branch = added(term_refs) + row_of(vec, OUT, 1, 1)
        scale = row_of(vec, SCALE, 1, 1)
        result[...] = (middle_ref[...] + scale * branch).astype(LOW)
        grad = cot[...].astype(WIDE)
        grad_branch = grad * scale
        low[...] = grad_branch.astype(LOW)
        sums[0:1, :] = jnp.sum(grad * branch, axis=0, keepdims=True)
        sums[1:2, :] = jnp.sum(grad_branch, axis=0, keepdims=True)

    shape = middle.shape
    outs = [shape_of(shape, LOW), shape_of(shape, LOW), shape_of((2, shape[1]), WIDE)]
    return call(kernel, outs, [middle, *terms, cotangent, vectors], "turn")


def norm_back(grad, terms, stream, branch, vectors, depth, which, before):
    def kernel(*refs):
        grad_ref, stream_ref, vec = refs[0], refs[1], refs[2]
        inputs = 4 if before else 3
        term_refs = refs[inputs : inputs + len(terms)]
        result, low, sums = (refs[inputs + len(terms) :] + (None,))[:3] if before else (
            None, refs[inputs + len(terms)], refs[inputs + len(terms) + 1],
        )
        came = added(term_refs)
        unit, rate = normed(stream_ref[...].astype(WIDE))
        sums[0:1, :] = jnp.sum(came * unit, axis=0, keepdims=True)
        sums[1:2, :] = jnp.sum(came, axis=0, keepdims=True)
        value = grad_ref[...].astype(WIDE)
        value = value + normed_back(came, unit, rate, row_of(vec, GAIN, depth, which))
        if not before:
            low[...] = value.astype(LOW)
            return
        result[...] = value
        sums[2:3, :] = jnp.sum(value * refs[3][...], axis=0, keepdims=True)
        value = value * row_of(vec, SCALE, *before)
        sums[3:4, :] = jnp.sum(value, axis=0, keepdims=True)
        low[...] = value.astype(LOW)

    shape = grad.shape
    outs = [shape_of(shape, LOW), shape_of((4 if before else 2, shape[1]), WIDE)]
    args = [grad, stream, vectors]
    if before:
        outs = [shape_of(shape, WIDE)] + outs
        args = args + [branch]
    return call(kernel, outs, args + list(terms), "norm_back")


def split_grads(grads, me):
    rows, width = grads[0].shape[0] * len(grads) // 4, grads[0].shape[1]

    def kernel(me_ref, *refs):
        ins, outs = refs[: len(grads)], refs[len(grads) : len(grads) + 4]
        joined = refs[-1]
        join(ins, joined)
        for away, out in enumerate(outs):
            member = jnp.bitwise_xor(me_ref[0], away)
            out[...] = joined[pl.ds(pl.multiple_of(member * rows, rows), rows), :].astype(LOW)

    scratch = [pltpu.VMEM((4 * rows, width), grads[0].dtype)]
    out = shape_of((rows, width), LOW)
    return call(kernel, [out] * 4, [me, *grads], "split_grads", scratch=scratch, scalars=1)


def place_grads(qkv_pieces, up_pieces, proj, down, part, rest, me):
    rows, hidden = up_pieces[0][0].shape
    width = 4 * part
    lanes = hidden // rest

    def kernel(me_ref, *refs):
        pieces, (proj_ref, down0, down1) = refs[:16], refs[16:19]
        qkv_out, up_out, proj_out, down_out = refs[19:]
        for depth in range(2):
            for away in range(4):
                member = jnp.bitwise_xor(me_ref[0], away)
                ref = pieces[4 * depth + away]
                for s in range(3):
                    start = pl.multiple_of(s * width + member * part, 128)
                    value = ref[:, s * part : (s + 1) * part].astype(WIDE)
                    qkv_out[depth, :, pl.ds(start, part)] = value
                ref = pieces[8 + 4 * depth + away]
                for f in range(rest):
                    start = pl.multiple_of((f * 4 + member) * lanes, 128)
                    value = ref[:, f * lanes : (f + 1) * lanes].astype(WIDE)
                    up_out[depth, :, pl.ds(start, lanes)] = value
            down_out[depth] = (down0, down1)[depth][...].astype(WIDE)
        proj_out[...] = proj_ref[...].astype(WIDE)

    outs = [
        shape_of((2, rows, 3 * width), WIDE),
        shape_of((2, rows, 4 * hidden), WIDE),
        shape_of(proj.shape, WIDE),
        shape_of((2,) + down[0].shape, WIDE),
    ]
    args = [me, *qkv_pieces[0], *qkv_pieces[1], *up_pieces[0], *up_pieces[1], proj, *down]
    return call(kernel, outs, args, "place_grads", scalars=1)


def on_device(
    tokens,
    cotangent,
    scene_ids,
    frame_index,
    qkv_weight,
    qkv_bias,
    proj_weight,
    fc1_weight,
    fc1_bias,
    fc2_weight,
    out_bias,
    norm_gain,
    norm_bias,
    layer_scale,
    qk_gain,
    qk_bias,
):
    frames = lax.axis_size("frame")
    team = 2 * frames
    rest = lax.axis_size("outer") * lax.axis_size("inner")
    count = team * rest
    rows, width = tokens.shape
    head_size = qk_gain.shape[-1]
    heads = width // head_size // team
    part = heads * head_size
    hidden = fc1_weight.shape[-1] // team
    mine = lax.axis_index("core") * frames + lax.axis_index("frame")
    here = lax.axis_index("outer") * lax.axis_size("inner") + lax.axis_index("inner")
    me = mine.reshape(1).astype(jnp.int32)
    shard_rows = qkv_weight.shape[1]
    fc2_rows = fc2_weight.shape[1]
    unit = team * shard_rows
    table = ring_table()
    quick = frames == 2 and shard_rows % 32 == 0 and part % 128 == 0 and (hidden // rest) % 128 == 0
    quick = quick and hidden == width and width // count == 32 and count * rows // FRAME_TOK <= 256

    small_parts = (qkv_bias, fc1_bias, out_bias, norm_gain, norm_bias, layer_scale)
    head_gain = jnp.tile(qk_gain.astype(WIDE), (1, 1, heads))
    head_shift = jnp.tile(qk_bias.astype(WIDE), (1, 1, heads))
    weights = []
    if quick:
        proj_here = lax.ppermute(proj_weight, EVERY, spread(count, team))
        shards, below = [], None
        for depth in range(2):
            small = (qkv_bias, fc1_bias, scene_ids.reshape(1, rows)) + small_parts[2:]
            split = split_weights(depth, (qkv_weight, fc1_weight), () if depth else small, part, rest, me)
            pieces = [split[0], swap(split[1], "frame"), swap(split[2], "core"), cross(split[3])]
            if depth == 0:
                below = pieces
            shards.append(pack_weights(pieces, proj_here, fc2_weight, depth, part, me, depth == 0))
        ids = jnp.concatenate([m[shard_rows, 512 : 512 + rows] for m in below]).astype(jnp.int32)
        tokens_all = team_gather(tokens)
        rings = []
        for depth in range(2):
            attn, both = shards[depth]
            rings.append((RingGather(attn, unit // 2, rest), RingGather(both, unit, rest)))
            for ring in rings[depth]:
                steps(rest, ring)
        vectors, bias_qkv, bias_up = unpack_vectors(rings[0][0].rows(unit, SMALL_ROWS), table, me)
    else:
        proj_here = lax.ppermute(proj_weight, EVERY, spread(count, team))
        for depth in range(2):
            attn = exchange_columns(
                qkv_weight[depth]
                .reshape(shard_rows, 3, team, part)
                .transpose(0, 2, 1, 3)
                .reshape(shard_rows, team, 3 * part)
            ).reshape(unit, 3 * part)
            attn = jnp.concatenate([attn, widen(proj_here[depth], part)], axis=1)
            up = exchange_columns(
                fc1_weight[depth]
                .reshape(shard_rows, rest, team, hidden // rest)
                .transpose(0, 2, 1, 3)
                .reshape(shard_rows, team, hidden)
            ).reshape(unit, hidden)
            down = widen(fc2_weight[depth], hidden)
            attn, up, down = (lax.all_gather(m, REST, axis=0, tiled=False) for m in (attn, up, down))
            proj = Whole(narrow(attn[:, :, 3 * part :], shard_rows).reshape(1, part, width), 0, part)
            down = Whole(narrow(down, fc2_rows).reshape(1, hidden, width), 0, hidden)
            weights.append(((Whole(attn, 0, unit), proj, part, width, table), (Whole(up, 0, unit), down)))
        small = small_gather(jnp.concatenate([m.reshape(-1) for m in small_parts])).astype(WIDE)
        n_qkv, n_up = qkv_bias.size, fc1_bias.size
        bias_qkv = small[:, :n_qkv].reshape(count, 2, -1).transpose(1, 0, 2).reshape(2, 3, team, part)
        bias_qkv = lax.dynamic_index_in_dim(bias_qkv, mine, 2, keepdims=False).reshape(2, 3 * part)
        bias_up = small[:, n_qkv : n_qkv + n_up].reshape(rest, team, 2, -1)
        bias_up = lax.dynamic_index_in_dim(bias_up, mine, 1, keepdims=False)
        bias_up = bias_up.transpose(1, 0, 2).reshape(2, hidden)
        vectors = small[:, n_qkv + n_up :].reshape(count, 16, -1).transpose(1, 0, 2).reshape(16, width)
        ids = jnp.concatenate([m.reshape(-1) for m in team_gather(scene_ids.reshape(1, rows))])
        tokens_all = team_gather(tokens)

    gathered = []
    streams, middles, branches, kept = [tokens], [], [], []
    for depth in range(2):
        work = None
        if quick:
            attn_weights = (rings[depth][0].rows(0, unit), None, shard_rows, part, table)
        else:
            attn_weights, mlp_sources = weights[depth]
        kept_attn, own, peer, attn_weights = attn_forward(
            team_gather(low, work, work) if depth else tokens_all, attn_weights, bias_qkv[depth : depth + 1],
            head_gain[depth], head_shift[depth], ids, head_size, frames, depth == 0, None if depth else vectors,
        )
        terms = team_sum(own, peer, work)
        branch_one, middle, low = branch_norm(streams[depth], terms, vectors, depth, 0)
        pieces = team_gather(low, work, work)
        if quick:
            mlp_sources = (rings[depth][1].rows(0, unit), rings[depth][1].rows(unit, unit))
        kept_mlp, own, peer, mlp_weights = mlp_forward(pieces, mlp_sources, table, bias_up[depth : depth + 1])
        gathered.append((attn_weights, mlp_weights))
        terms = team_sum(own, peer, work)
        branch_two = None
        if depth == 0:
            branch_two, stream, low = branch_norm(middle, terms, vectors, 0, 1)
            streams.append(stream)
        middles.append(middle)
        branches.append((branch_one, branch_two))
        kept.append((kept_attn, kept_mlp))

    activations, low, turn_sums = turn(middles[1], terms, cotangent, vectors)
    grad = cotangent
    names, token_sums = [(SCALE, 1, 1), (OUT, 1, 1)], [turn_sums]
    sums_up, sums_qkv, head_sums = [None, None], [None, None], [None, None]
    finals = [{}, {}]
    ring = RingSums(rest)

    def end_mlp(depth):
        def end(up_sum, down_sum):
            if not quick:
                up = exchange_columns(up_sum.astype(LOW).reshape(team, shard_rows, hidden).transpose(1, 0, 2))
                up = up.reshape(team, shard_rows, rest, hidden // rest).transpose(1, 2, 0, 3)
                finals[depth].update(up=up.reshape(shard_rows, -1), down=narrow(down_sum, fc2_rows))
                return
            end_up(depth)(up_sum)
            finals[depth].update(down=down_sum)

        return end

    def end_up(depth):
        def end(*halves):
            m = split_grads(halves, me)
            finals[depth].update(up=[m[0], swap(m[1], "frame"), swap(m[2], "core"), cross(m[3])])

        return end

    def end_attn(depth):
        def end(low_sum, high_sum):
            if not quick:
                both = jnp.concatenate([low_sum, high_sum], axis=0)
                qkv = exchange_columns(
                    both[:, : 3 * part].astype(LOW).reshape(team, shard_rows, 3 * part).transpose(1, 0, 2)
                )
                qkv = qkv.reshape(team, shard_rows, 3, part).transpose(1, 2, 0, 3)
                proj = narrow(both[:, 3 * part :], shard_rows)
                finals[depth].update(qkv=qkv.reshape(shard_rows, -1), proj=proj.astype(LOW))
                return
            m = split_grads([low_sum[:, : 3 * part], high_sum[:, : 3 * part]], me)
            proj = jnp.concatenate([n[:, 3 * part :] for n in (low_sum, high_sum)], axis=0)
            finals[depth].update(
                qkv=[m[0], swap(m[1], "frame"), swap(m[2], "core"), cross(m[3])],
                proj=narrow(proj, shard_rows).astype(LOW),
            )

        return end

    for depth in (1, 0):
        attn_weights, (weight_up, weight_down) = gathered[depth]
        kept_attn, (second, act, slope) = kept[depth]
        first, flat = kept_attn[0], kept_attn[4]
        pieces = team_gather(low, ring.work, ring.pump)
        (branch_low, pre_low, sum_up), own, peer = mlp_backward(pieces, weight_up, weight_down, slope)
        sums_up[depth] = sum_up
        if quick:
            mlp_parts = mlp_weight_grads(second, pre_low, act, branch_low, rest, table)
        else:
            grad_up = dot_tn(second, pre_low).astype(LOW).reshape(rest, unit, hidden)
            grad_down = dot_tn(act, branch_low).astype(LOW)
            grad_down = grad_down.reshape(rest, fc2_rows, width // hidden, hidden)
            grad_down = grad_down.transpose(0, 2, 1, 3).reshape(rest, -1, hidden)
            end_mlp(depth)(rest_sum(grad_up), rest_sum(grad_down))
        if quick:
            ring.add(*mlp_parts, end_mlp(depth))
        terms = team_sum(own, peer, ring.work, ring.pump)
        grad_middle, low, sums = norm_back(
            grad, terms, middles[depth], branches[depth][0], vectors, depth, 1, (depth, 0)
        )
        names += [(GAIN, depth, 1), (SHIFT, depth, 1), (SCALE, depth, 0), (OUT, depth, 0)]
        token_sums.append(sums)
        pieces = team_gather(low, ring.work, ring.pump)
        (att_low, mixed_low, sum_qkv, head_sum), own, peer = attn_backward(
            pieces, attn_weights, head_gain[depth], kept_attn, ids, head_size, frames, depth == 0
        )
        sums_qkv[depth], head_sums[depth] = sum_qkv, head_sum
        if quick:
            attn_parts = attn_weight_grads(first, mixed_low, flat, att_low, rest, shard_rows, table)
        else:
            grad_qkv = dot_tn(first, mixed_low).astype(LOW).reshape(rest, unit, 3 * part)
            grad_proj = dot_tn(flat, att_low).astype(LOW).reshape(rest, shard_rows, team, part)
            grad_proj = grad_proj.transpose(0, 2, 1, 3).reshape(rest, unit, part)
            attn = rest_sum(jnp.concatenate([grad_qkv, grad_proj], axis=2))
            end_attn(depth)(attn[: unit // 2], attn[unit // 2 :])
        if quick:
            ring.add(*attn_parts, end_attn(depth))
        terms = team_sum(own, peer, ring.work, ring.pump)
        if depth == 1:
            grad, low, sums = norm_back(
                grad_middle, terms, streams[1], branches[0][1], vectors, 1, 0, (0, 1)
            )
            names += [(GAIN, 1, 0), (SHIFT, 1, 0), (SCALE, 0, 1), (OUT, 0, 1)]
        else:
            input_grad, sums = norm_back(grad_middle, terms, tokens, None, vectors, 0, 0, None)
            names += [(GAIN, 0, 0), (SHIFT, 0, 0)]
        token_sums.append(sums)
    while ring.busy():
        ring.hop()

    proj_grad = lax.ppermute(
        jnp.stack([finals[0]["proj"], finals[1]["proj"]]), EVERY, [(b, a) for a, b in spread(count, team)]
    )
    if quick:
        qkv_grad, up_grad, proj_grad, down_grad = place_grads(
            [m["qkv"] for m in finals], [m["up"] for m in finals], proj_grad,
            [m["down"] for m in finals], part, rest, me,
        )
    else:
        proj_grad = proj_grad.astype(WIDE)
        qkv_grad, up_grad, down_grad = (
            jnp.stack([m[name] for m in finals]).astype(WIDE) for name in ("qkv", "up", "down")
        )

    full_qkv = lax.dynamic_update_slice(
        jnp.zeros((6, team, part), WIDE),
        jnp.concatenate(sums_qkv, axis=0).reshape(6, 1, part),
        (0, mine, 0),
    ).reshape(6, width)
    head_all = jnp.stack(head_sums).reshape(-1, heads, head_size).sum(axis=1).reshape(1, -1)
    head_all = jnp.pad(head_all, ((0, 0), (0, width - head_all.shape[1])))
    team_rows = jnp.concatenate([*token_sums, full_qkv, head_all], axis=0)
    team_rows = team_rows + swap(team_rows, "core")
    if frames == 2:
        team_rows = team_rows + swap(team_rows, "frame")
    else:
        team_rows = lax.psum(team_rows, "frame")
    sums_up = jnp.concatenate(sums_up, axis=0).reshape(2, rest, hidden // rest)
    sums_up = jnp.pad(sums_up, ((0, 0), (0, 0), (0, (width - hidden) // rest))).reshape(2, width)
    split = jnp.concatenate([team_rows[:16], sums_up], axis=0)
    split, common = small_sum(split, team_rows[16:])
    vector_grads = lax.dynamic_slice_in_dim(split[:16], mine * (width // count), width // count, 1)
    ordered = [(kind, depth, place) for kind in (OUT, GAIN, SHIFT, SCALE) for depth in (0, 1) for place in (0, 1)]
    vector_grads = jnp.stack([vector_grads[names.index(name)] for name in ordered]).reshape(4, 2, 2, -1)
    grad_bias_qkv = common[:6].reshape(2, -1)
    grad_bias_qkv = lax.dynamic_slice_in_dim(
        grad_bias_qkv, (here * team + mine) * qkv_bias.shape[1], qkv_bias.shape[1], 1
    )
    head_all = common[6, : 8 * head_size].reshape(2, 2, 2, head_size)
    return (
        activations,
        input_grad,
        qkv_grad,
        grad_bias_qkv,
        proj_grad,
        up_grad,
        split[16:, : hidden // rest],
        down_grad,
        vector_grads[0],
        vector_grads[1],
        vector_grads[2],
        vector_grads[3],
        head_all[:, 0],
        head_all[:, 1],
    )


def solution(mesh):
    scenes, frames = mesh.shape["scene"], mesh.shape["frame"]
    rest = scenes // 2
    outer = 4 if rest % 4 == 0 else rest
    grid = Mesh(mesh.devices.reshape(outer, rest // outer, 2, frames), EVERY)
    by_rows = P(EVERY, None)
    second = P(None, EVERY)
    second_rows = P(None, EVERY, None)
    last = P(None, None, EVERY)
    return jax.shard_map(
        on_device,
        mesh=grid,
        in_specs=(
            by_rows, by_rows, P(EVERY), P(EVERY), second_rows, second, second_rows, second_rows,
            second, second_rows, last, last, last, last, P(), P(),
        ),
        out_specs=(
            by_rows, by_rows, second_rows, second, second_rows, second_rows, second, second_rows,
            last, last, last, last, P(), P(),
        ),
        check_vma=False,
    )
```

```python
import jax
import jax.numpy as jnp
import numpy as np
from jax import lax
from jax.experimental import pallas as pl
from jax.experimental.pallas import tpu as pltpu
from jax.sharding import Mesh
from jax.sharding import PartitionSpec as P

EPSILON = 1e-06
FRAME_TOK = 64
LOW = jnp.bfloat16
WIDE = jnp.float32
EVERY = ("outer", "inner", "core", "frame")
REST = ("outer", "inner")
TEAM = ("core", "frame")
ROOT_HALF = 0.7071067811865476
ROOT_TWO_PI = 0.3989422804014327
MEBI = 1024 * 1024
OUT, GAIN, SHIFT, SCALE = 0, 4, 8, 12
HOPS = (0, 0, 1, 0, 1, 0, 1, 0) + (1, 0, 1, 1, 0, 0, 1, 0)
LEAD = (4, 4)


def dot(left, right):
    return jnp.dot(left, right, preferred_element_type=WIDE)


def dot_tn(left, right):
    return lax.dot_general(left, right, (((0,), (0,)), ((), ())), preferred_element_type=WIDE)


def dot_nt(left, right):
    return lax.dot_general(left, right, (((1,), (1,)), ((), ())), preferred_element_type=WIDE)


def normed(values):
    center = values - jnp.mean(values, axis=-1, keepdims=True)
    rate = lax.rsqrt(jnp.mean(center * center, axis=-1, keepdims=True) + EPSILON)
    return center * rate, rate


def normed_back(grad, unit, rate, gain):
    inner = grad * gain
    mean_one = jnp.mean(inner, axis=-1, keepdims=True)
    mean_two = jnp.mean(inner * unit, axis=-1, keepdims=True)
    return rate * (inner - mean_one - unit * mean_two)


def shape_of(shape, dtype):
    return jax.ShapeDtypeStruct(shape, dtype)


def call(kernel, outs, args, name, flops=0, scratch=(), scalars=0, far_in=(), far_out=()):
    hbm = pl.BlockSpec(memory_space=pltpu.HBM)
    vmem = pl.BlockSpec(memory_space=pltpu.VMEM)
    smem = pl.BlockSpec(memory_space=pltpu.SMEM)
    in_specs = [smem if i < scalars else hbm if i in far_in else vmem for i in range(len(args))]
    bytes_all = sum(m.size * m.dtype.itemsize for m in args)
    bytes_all += sum(int(np.prod(s.shape)) * s.dtype.itemsize for s in outs)
    sized = [s for s in scratch if hasattr(s, "shape") and s.memory_space == pltpu.VMEM]
    held = sum(int(np.prod(s.shape)) * s.dtype.itemsize for s in sized)
    limit = (held * 5 // 4 + bytes_all * 2 // 5 if flops else bytes_all) + (8 if flops else 3) * MEBI
    args = [pltpu.with_memory_space_constraint(m, pltpu.HBM) if i in far_in else m for i, m in enumerate(args)]
    outs = [pltpu.HBM(m.shape, m.dtype) if i in far_out else m for i, m in enumerate(outs)]
    return pl.pallas_call(
        kernel,
        out_shape=list(outs),
        in_specs=in_specs,
        out_specs=[hbm if i in far_out else vmem for i in range(len(outs))],
        scratch_shapes=list(scratch),
        compiler_params=pltpu.CompilerParams(vmem_limit_bytes=limit),
        cost_estimate=pl.CostEstimate(flops=flops, bytes_accessed=bytes_all, transcendentals=0),
        name=name,
    )(*args)


def swap(values, axis):
    return lax.ppermute(values, axis, [(0, 1), (1, 0)])


def cross(values):
    return lax.ppermute(values, TEAM, [(0, 3), (1, 2), (2, 1), (3, 0)])


def team_gather(values, work=None, pump=None):
    if lax.axis_size("frame") == 2:
        far = swap(values, "frame")
        near = swap(work(values) if work else values, "core")
        far = pump(far) if pump else far
        return [values, far, near, swap(far, "core")]
    both = lax.all_gather(values, "frame", axis=0, tiled=True)
    return [both, swap(both, "core")]


def team_sum(own, peer, work=None, pump=None):
    if lax.axis_size("frame") == 2:
        far = own[1] + swap(peer[1], "core").astype(WIDE)
        came = swap(far.astype(LOW), "frame")
        near = swap(work(peer[0]) if work else peer[0], "core")
        came = pump(came) if pump else came
        return [own[0], near, came]
    total = own[0] + swap(peer[0], "core").astype(WIDE)
    return [lax.psum_scatter(total.astype(LOW), "frame", scatter_dimension=0, tiled=True).astype(WIDE)]


def exchange_columns(values):
    parts = values.transpose(1, 0, 2)
    frames = lax.axis_size("frame")
    parts = parts.reshape((2, frames) + parts.shape[1:])
    both = lax.all_to_all(parts, "frame", 1, 1, tiled=True)
    here = lax.axis_index("core")
    keep = lax.dynamic_index_in_dim(both, here, 0, keepdims=False)
    came = swap(lax.dynamic_index_in_dim(both, 1 - here, 0, keepdims=False), "core")
    out = jnp.stack([jnp.where(here == 0, keep, came), jnp.where(here == 0, came, keep)], axis=0)
    return out.reshape((2 * frames,) + out.shape[2:])


SMALL_ROWS = 16


def split_weights(depth, weights, vectors, part, rest, me):
    qkv, up = weights
    _, rows, width = qkv.shape
    width //= 3
    hidden = up.shape[2] // 4
    lanes = hidden // rest
    extra = SMALL_ROWS if vectors else 0

    far = list(vectors)

    def kernel(me_ref, qkv_ref, up_ref, *refs):
        outs, small = refs[len(far) : len(far) + 4], refs[len(far) + 4 : -1]
        copies = []
        for source, target in zip(refs, small):
            copies.append(pltpu.make_async_copy(source, target, refs[-1].at[len(copies)]))
            copies[-1].start()
        wait_all(copies)
        for away, out in enumerate(outs):
            member = jnp.bitwise_xor(me_ref[0], away)
            for s in range(3):
                start = pl.multiple_of(s * width + member * part, 128)
                out[:rows, s * part : (s + 1) * part] = qkv_ref[depth, :, pl.ds(start, part)]
            for f in range(rest):
                start = pl.multiple_of((f * 4 + member) * lanes, 128)
                at = 3 * part + f * lanes
                out[:rows, at : at + lanes] = up_ref[depth, :, pl.ds(start, lanes)]
            if not vectors:
                continue
            out[rows:, :] = jnp.zeros((extra, out.shape[1]), LOW)
            bias_qkv, bias_up, ids = small[:3]
            for i, ref in enumerate(small[3:]):
                for d in range(2):
                    for j in range(2):
                        at = rows + 4 * i + 2 * d + j
                        out[at : at + 1, : ref.shape[2]] = ref[d, j : j + 1, :]
            out[rows : rows + 2, 128 : 128 + bias_qkv.shape[1]] = bias_qkv[...]
            out[rows : rows + 2, 256 : 256 + bias_up.shape[1]] = bias_up[...]
            out[rows : rows + 1, 512 : 512 + ids.shape[1]] = ids[...].astype(WIDE).astype(LOW)

    out = shape_of((rows + extra, 3 * part + hidden), qkv.dtype)
    scratch = [pltpu.VMEM(m.shape, m.dtype) for m in far] + [pltpu.SemaphoreType.DMA((len(far) + 1,))]
    args = [me, qkv, up, *far]
    return call(kernel, [out] * 4, args, "split_weights", 0, scratch, 1, far_in=range(3, 3 + len(far)))


def pack_weights(pieces, proj, down, depth, part, me, vectors):
    rows = proj.shape[1]
    unit = 4 * rows
    hidden = pieces[0].shape[1] - 3 * part

    def kernel(me_ref, p0, p1, p2, p3, proj_ref, down_ref, attn, up, small):
        for away, ref in enumerate((p0, p1, p2, p3)):
            member = jnp.bitwise_xor(me_ref[0], away)
            start = pl.multiple_of(member * rows, rows)
            attn[pl.ds(start, rows), : 3 * part] = ref[:rows, : 3 * part]
            up[pl.ds(start, rows), :] = ref[:rows, 3 * part :]
            if vectors:
                small[member] = ref[rows:, :640]
        for j in range(4):
            attn[j * rows : (j + 1) * rows, 3 * part :] = proj_ref[depth, :, j * part : (j + 1) * part]
        up[unit:, :] = down_ref[depth]
        if vectors:
            attn[unit:, :] = jnp.zeros((SMALL_ROWS, 4 * part), LOW)
            for at, start, size in ((0, 0, 32), (128, 128, 96), (512, 256, 128)):
                joined = [small[m, :, start : start + size].astype(WIDE) for m in range(4)]
                value = jnp.concatenate(joined, axis=1).astype(LOW)
                attn[unit:, at : at + 4 * size] = value

    extra = SMALL_ROWS if vectors else 0
    outs = [shape_of((unit + extra, 4 * part), LOW), shape_of((2 * unit, hidden), LOW)]
    scratch = [pltpu.VMEM((4, SMALL_ROWS, 640), LOW)]
    return call(kernel, outs, [me, *pieces, proj, down], "pack_weights", scratch=scratch, scalars=1)


def unpack_vectors(source, table, me):
    rest, _, width = source.shape
    part = width // 4

    def kernel(me_ref, table_ref, *refs):
        vec, bias_qkv, bias_up, small, whole, semaphores = refs[source.count :]
        wait_all(source.start(refs[: source.count], table_ref, small, semaphores))
        for f in range(rest):
            vec[:, f * 128 : (f + 1) * 128] = small[f, :, :128].astype(WIDE)
            whole[:, f * 384 : (f + 1) * 384] = small[f, :, 128:512].astype(WIDE)
            start = pl.multiple_of(512 + me_ref[0] * 128, 128)
            bias_up[:, f * 128 : (f + 1) * 128] = small[f, :, pl.ds(start, 128)].astype(WIDE)
        for s in range(3):
            start = pl.multiple_of(s * width + me_ref[0] * part, 128)
            bias_qkv[:, s * part : (s + 1) * part] = whole[:, pl.ds(start, part)]

    outs = [shape_of((16, width), WIDE), shape_of((16, 3 * part), WIDE), shape_of((16, width), WIDE)]
    scratch = [
        pltpu.VMEM((rest, SMALL_ROWS, width), LOW),
        pltpu.VMEM((16, 3 * width), WIDE),
        pltpu.SemaphoreType.DMA((source.count,)),
    ]
    args = [me, table, *source.args]
    return call(kernel, outs, args, "unpack_vectors", 0, scratch, 2, far_in=range(2, 2 + source.count))


def spread(count, team):
    rest = count // team
    return [(i, (i % rest) * team + i // rest) for i in range(count)]


def widen(rows, width):
    height, columns = rows.shape
    parts = columns // width
    if parts == 1:
        return rows
    return rows.reshape(height, parts, width).transpose(1, 0, 2).reshape(parts * height, width)


def narrow(stacked, height):
    lead = stacked.shape[:-2]
    parts = stacked.shape[-2] // height
    if parts == 1:
        return stacked
    width = stacked.shape[-1]
    shaped = stacked.reshape(lead + (parts, height, width))
    return jnp.moveaxis(shaped, -3, -2).reshape(lead + (height, parts * width))


def ring_order(outer, inner):
    order = []
    for a in range(outer):
        row = range(1, inner) if a % 2 == 0 else range(inner - 1, 0, -1)
        order += [a * inner + b for b in row]
    return order + [a * inner for a in range(outer - 1, -1, -1)]


def ring_table():
    outer, inner = lax.axis_size("outer"), lax.axis_size("inner")
    order = ring_order(outer, inner)
    rest = outer * inner
    place = {team: i for i, team in enumerate(order)}
    table = np.array(
        [
            [[order[(place[f] + sign * k) % rest] for k in range(rest)] for sign in (-1, 1)]
            for f in range(rest)
        ],
        np.int32,
    )
    here = lax.axis_index("outer") * inner + lax.axis_index("inner")
    return lax.dynamic_index_in_dim(jnp.asarray(table), here, 0, keepdims=False)


def ring_shift(values, sign):
    order = ring_order(lax.axis_size("outer"), lax.axis_size("inner"))
    rest = len(order)
    return lax.ppermute(values, REST, [(order[i], order[(i + sign) % rest]) for i in range(rest)])


def ring_step(low_half, high_half):
    low_half, high_half = ring_shift(low_half, 1), ring_shift(high_half, -1)
    return lax.optimization_barrier((low_half, high_half))


class RingGather:
    def __init__(self, shard, cut, rest):
        self.steps = rest // 2
        self.cut = cut
        self.back, self.ahead = [shard], [shard]
        self.came = (ring_shift(shard, 1), ring_shift(shard, -1))

    def take(self, came):
        self.back.append(came[0])
        self.ahead.append(came[1])
        self.came = None
        if len(self.back) == self.steps:
            came = (came[0][: self.cut], came[1][self.cut :])
        if len(self.back) <= self.steps:
            self.came = (ring_shift(came[0], 1), ring_shift(came[1], -1))

    def rows(self, first, count):
        out = []
        for side, arrays in enumerate((self.back, self.ahead)):
            out += [(m, side, k, 0, first, count) for k, m in enumerate(arrays[: self.steps]) if k or not side]
        stop = min(first + count, self.cut)
        if stop > first:
            out.append((self.back[self.steps], 0, self.steps, 0, first, stop - first))
        start = max(first, self.cut)
        if start < first + count:
            out.append(
                (self.ahead[self.steps], 1, self.steps, start - first, start - self.cut, first + count - start)
            )
        return Pieces(out, 2 * self.steps, count)


def steps(count, ring):
    came = ()
    for _ in range(count):
        if ring.came is None:
            break
        came = tie(*ring.came)
        ring.take(came)
    return came


class Pieces:
    def __init__(self, entries, rest, rows):
        self.entries = entries
        self.args = [entry[0] for entry in entries]
        self.count = len(entries)
        self.shape = (rest, rows, self.args[0].shape[1])

    def start(self, refs, table_ref, target, semaphores):
        copies = []
        for ref, (_, side, k, first, begin, rows) in zip(refs, self.entries):
            spot = target.at[table_ref[side, k], pl.ds(first, rows), :]
            copies.append(pltpu.make_async_copy(ref.at[pl.ds(begin, rows), :], spot, semaphores.at[len(copies)]))
            copies[-1].start()
        return copies


class Whole:
    count = 1

    def __init__(self, array, first, rows):
        self.first = first
        self.args = [array]
        self.shape = (array.shape[0], rows, array.shape[2])

    def start(self, refs, table_ref, target, semaphores):
        source = refs[0].at[:, pl.ds(self.first, self.shape[1]), :]
        copy = pltpu.make_async_copy(source, target, semaphores.at[0])
        copy.start()
        return [copy]


def wait_all(copies):
    for copy in copies:
        copy.wait()


def tie(*values):
    return lax.optimization_barrier(values)


class RingSums:
    def __init__(self, rest):
        self.steps = rest // 2
        self.active = []
        self.waiting = []
        self.came = None
        self.started = []
        self.plan = iter(HOPS)

    def work(self, value):
        if next(self.plan):
            if self.came is not None:
                self.came = tie(*self.came, value)[:2]
            self.hop()
        started, self.started = self.started, []
        return tie(value, *started)[0] if started else value

    def pump(self, value):
        return self.hop(value) if next(self.plan) else value

    def add(self, ahead, behind, own, done):
        self.waiting.append(
            {"parts": (ahead, behind), "own": own, "rows": own.shape[0], "done": done, "hop": 0}
        )
        self.started.append(own)

    def hop(self, *values):
        if self.came is not None:
            tied = tie(*values, *self.came)
            values, self.came = tied[: len(values)], tied[len(values) :]
        rings = self.active + self.waiting
        self.waiting = []
        result = values if len(values) != 1 else values[0]
        if not rings:
            return result
        columns = rings[0]["own"].shape[1]
        moving, start, ended, plans, args = 0, 0, [], [], []
        for ring in rings:
            rows, hop = ring["rows"], ring["hop"]
            came_rows = (0, rows // 2, rows)[min(hop, 2)]
            came_at = start
            start += came_rows
            if hop == self.steps:
                plans.append((rows, came_at, came_rows, None))
                args.append(ring["own"])
                ended.append(ring)
            else:
                plans.append((rows if hop else rows // 2, came_at, came_rows, moving))
                args += [ring["parts"][side][hop] for side in range(2)]
                moving += rows if hop else rows // 2
            ring["hop"] += 1
        came = list(self.came) if self.came is not None else []
        size = sum(m.shape[0] for m in args)

        def kernel(*refs):
            came_refs = refs[: len(came)]
            part_refs = refs[len(came) : len(came) + len(args)]
            outs, local, semaphores = refs[len(came) + len(args) : -2], refs[-2], refs[-1]
            copies, at = [], 0
            for ref in part_refs:
                spot = local.at[pl.ds(at, ref.shape[0]), :]
                copies.append(pltpu.make_async_copy(ref, spot, semaphores.at[len(copies)]))
                copies[-1].start()
                at += ref.shape[0]
            wait_all(copies)
            final, at = (2 if moving else 0), 0
            for rows, came_at, came_rows, goes_to in plans:
                others = [ref[came_at : came_at + came_rows, :] for ref in came_refs] if came_rows else []
                if goes_to is None:
                    total = local[at : at + rows, :].astype(WIDE)
                    total = total + others[0].astype(WIDE) + others[1].astype(WIDE)
                    outs[final][...] = total[: rows // 2]
                    outs[final + 1][...] = total[rows // 2 :]
                    final += 2
                    at += rows
                    continue
                for side in range(2):
                    outs[side][goes_to : goes_to + rows, :] = local[at : at + rows, :]
                    if came_rows:
                        first = side * came_rows if came_rows < rows else 0
                        total = local[at + first : at + first + came_rows, :].astype(WIDE)
                        total = (total + others[side].astype(WIDE)).astype(LOW)
                        outs[side][goes_to + first : goes_to + first + came_rows, :] = total
                    at += rows

        outs = [shape_of((moving, columns), LOW)] * 2 if moving else []
        for ring in ended:
            outs += [shape_of((ring["rows"] // 2, columns), WIDE)] * 2
        scratch = [pltpu.VMEM((size, columns), LOW), pltpu.SemaphoreType.DMA((len(args),))]
        far_in = range(len(came), len(came) + len(args))
        res = call(kernel, outs, came + args, "ring_add", 0, scratch, far_in=far_in)
        at = 2 if moving else 0
        for ring in ended:
            ring["done"](res[at], res[at + 1])
            at += 2
        self.active = [ring for ring in rings if ring["hop"] <= self.steps]
        self.started += list(res[:2])
        self.came = (ring_shift(res[0], 1), ring_shift(res[1], -1)) if moving else None
        return result

    def busy(self):
        return bool(self.active or self.waiting)


def hop_places(rest):
    steps = rest // 2
    return [(1, k) for k in range(steps, 0, -1)] + [(0, k) for k in range(steps, 0, -1)] + [(0, 0)]


def rest_sum(parts):
    return lax.psum_scatter(parts, REST, scatter_dimension=0, tiled=False)


def small_gather(values):
    out = values[None]
    for axis in ("frame", "core", "inner", "outer"):
        size, here, step = lax.axis_size(axis), lax.axis_index(axis), 1
        while step < size:
            came = lax.ppermute(out, axis, [(i, i ^ step) for i in range(size)])
            first = (here & step) == 0
            out = jnp.concatenate([jnp.where(first, out, came), jnp.where(first, came, out)], axis=0)
            step *= 2
    return out


def small_sum(split, common):
    for axis in ("outer", "inner"):
        size, here = lax.axis_size(axis), lax.axis_index(axis)
        step = size // 2
        while step >= 1:
            half = split.shape[1] // 2
            bit = (here // step) % 2
            keep = lax.dynamic_slice_in_dim(split, bit * half, half, 1)
            send = lax.dynamic_slice_in_dim(split, (1 - bit) * half, half, 1)
            pairs = [(i, i ^ step) for i in range(size)]
            packed = jnp.concatenate([send.reshape(-1), common.reshape(-1)])
            came = lax.ppermute(packed, axis, pairs)
            split = keep + came[: keep.size].reshape(keep.shape)
            common = common + came[keep.size :].reshape(common.shape)
            step //= 2
    return split, common


def head_means(part, head_size):
    row = lax.broadcasted_iota(jnp.int32, (part, part), 0) // head_size
    column = lax.broadcasted_iota(jnp.int32, (part, part), 1) // head_size
    return jnp.where(row == column, 1.0 / head_size, 0.0).astype(LOW)


def head_mean(values, matrix):
    high = values.astype(LOW)
    rest = (values - high.astype(WIDE)).astype(LOW)
    return dot(high, matrix) + dot(rest, matrix)


def head_normed(values, matrix):
    center = values - head_mean(values, matrix)
    rate = lax.rsqrt(head_mean(center * center, matrix) + EPSILON)
    return center * rate, rate


def join(refs, out_ref):
    start = 0
    for ref in refs:
        out_ref[start : start + ref.shape[0], :] = ref[...]
        start += ref.shape[0]


def spans(refs):
    start = 0
    for ref in refs:
        yield start, start + ref.shape[0], ref
        start += ref.shape[0]


def flat_rows(ref, first, height, columns):
    block = ref[:, first : first + height, columns]
    return block.reshape(block.shape[0] * height, block.shape[2])


def tiles_of(total, group, block):
    for base in range(0, total, group):
        for start in range(base, base + group, block):
            yield start, base


def allowed_of(ids_col, ids_row, start, base, block, group, use_frame):
    if use_frame:
        row = lax.broadcasted_iota(jnp.int32, (block, group), 0) // FRAME_TOK
        column = lax.broadcasted_iota(jnp.int32, (block, group), 1) // FRAME_TOK
        return row == column
    return ids_col[start : start + block, :] == ids_row[:, base : base + group]


def plan(frames, rows, use_frame):
    group = min(4 * FRAME_TOK, frames * rows) if use_frame else frames * rows
    return group, min(group, 256)


def part_shapes(pieces, width):
    half = len(pieces) // 2
    return [shape_of((m.shape[0], width), WIDE if i < half else LOW) for i, m in enumerate(pieces)]


def load_semaphores(sources):
    return [pltpu.SemaphoreType.DMA((source.count,)) for source in sources]


def start_loads(sources, table_ref, far_refs, targets, semaphores):
    at, copies = 0, []
    for source, target, semaphore in zip(sources, targets, semaphores):
        copies.append(source.start(far_refs[at : at + source.count], table_ref, target, semaphore))
        at += source.count
    return copies


def attn_forward(pieces, weights, bias, head_gain, head_shift, ids, head_size, frames, use_frame, vectors=None):
    attn, proj, height, wide, table = weights
    sources = [attn] if proj is None else [attn, proj]
    far = [m for source in sources for m in source.args]
    rest, unit, _ = attn.shape
    width, part = rest * unit, head_gain.shape[-1]
    total = sum(m.shape[0] for m in pieces)
    count = len(pieces)
    group, block = plan(frames, total // (2 * frames), use_frame)
    lanes = min(128, part)
    per = lanes // head_size
    scale = head_size ** (-0.5)
    more = 0 if vectors is None else 1

    def kernel(table_ref, *refs):
        far_refs, refs = refs[: len(far)], refs[len(far) :]
        semaphores, refs = refs[-len(sources) :], refs[: -len(sources)]
        targets, refs = refs[-len(sources) :], refs[: -len(sources)]
        copies = start_loads(sources, table_ref, far_refs, targets, semaphores)
        wq, wp = targets[0], targets[-1]
        piece_refs = refs[:count]
        bias_ref, gain_ref, shift_ref, ids_col, ids_row = refs[count : count + 5]
        first, raw, qkv, lse, flat = refs[count + 5 + more : count + 10 + more]
        outs = refs[count + 10 + more :]
        if more:
            vec = refs[count + 5]
            for start, stop, ref in spans(piece_refs):
                unit_one, _ = normed(ref[...].astype(WIDE))
                value = unit_one * row_of(vec, GAIN, 0, 0) + row_of(vec, SHIFT, 0, 0)
                first[start:stop, :] = value.astype(LOW)
        else:
            join(piece_refs, first)
        matrix = head_means(part, head_size)
        for group_copies in copies:
            wait_all(group_copies)
        mixed = dot(first[...], flat_rows(wq, 0, unit, slice(0, 3 * part))) + bias_ref[...]
        raw[...] = mixed[:, : 2 * part]
        for i in range(2):
            unit_i, _ = head_normed(mixed[:, i * part : (i + 1) * part], matrix)
            value = unit_i * gain_ref[i : i + 1, :] + shift_ref[i : i + 1, :]
            qkv[:, i * part : (i + 1) * part] = value.astype(LOW)
        qkv[:, 2 * part :] = mixed[:, 2 * part :].astype(LOW)
        place = lax.broadcasted_iota(jnp.int32, (1, lanes), 1) // head_size
        for start, base in tiles_of(total, group, block):
            allowed = allowed_of(ids_col, ids_row, start, base, block, group, use_frame)
            stats = []
            for lane in range(0, part, lanes):
                query = qkv[start : start + block, lane : lane + lanes] * jnp.asarray(scale, LOW)
                key = qkv[base : base + group, part + lane : part + lane + lanes]
                value = qkv[base : base + group, 2 * part + lane : 2 * part + lane + lanes]
                out = jnp.zeros((block, lanes), WIDE)
                for h in range(per):
                    mask = place == h
                    scores = dot_nt(jnp.where(mask, query, jnp.zeros_like(query)), key)
                    scores = jnp.where(allowed, scores, -jnp.inf)
                    top = jnp.max(scores, axis=-1, keepdims=True)
                    weight = jnp.exp(scores - top)
                    norm = jnp.sum(weight, axis=-1, keepdims=True)
                    stats.append(top + jnp.log(norm))
                    probs = (weight * (1.0 / norm)).astype(LOW)
                    out = jnp.where(mask, dot(probs, value), out)
                flat[start : start + block, lane : lane + lanes] = out.astype(LOW)
            lse[start : start + block, :] = jnp.concatenate(stats, axis=1)
        for a in range(0, width, wide):
            b = a + wide
            chunk = flat_rows(wp, a // wide * height, height, slice(wp.shape[2] - wide, wp.shape[2]))
            for start, stop, ref in spans(outs):
                ref[:, a:b] = dot(flat[start:stop, :], chunk).astype(ref.dtype)

    outs = [
        shape_of((total, width), LOW),
        shape_of((total, 2 * part), WIDE),
        shape_of((total, 3 * part), LOW),
        shape_of((total, part // head_size), WIDE),
        shape_of((total, part), LOW),
    ] + part_shapes(pieces, width)
    outs += [shape_of(source.shape, LOW) for source in sources]
    args = [table] + far + list(pieces)
    args += [bias, head_gain, head_shift, ids.reshape(-1, 1), ids.reshape(1, -1)]
    args += [vectors] if more else []
    flops = 2 * total * (width * 4 * part + group * 2 * part)
    scratch = load_semaphores(sources)
    res = call(kernel, outs, args, "attn_forward", flops, scratch, 1, far_in=range(1, 1 + len(far)))
    weights = (res[5 + count], None if proj is None else res[6 + count], height, wide)
    return res[:5], res[5 : 5 + count // 2], res[5 + count // 2 : 5 + count], weights


def attn_backward(pieces, weights, head_gain, kept, ids, head_size, frames, use_frame):
    _, raw, qkv, lse, _ = kept
    attn, proj, height, wide = weights
    rest, unit, _ = attn.shape
    width, part = rest * unit, head_gain.shape[-1]
    total = sum(m.shape[0] for m in pieces)
    count = len(pieces)
    group, block = plan(frames, total // (2 * frames), use_frame)
    lanes = min(128, part)
    per = lanes // head_size
    scale = head_size ** (-0.5)
    extra = 0 if proj is None else 1

    def kernel(*refs):
        piece_refs, wq, wp = refs[:count], refs[count], refs[count + extra]
        refs = refs[extra + 1 :]
        gain_ref, raw_ref, qkv_ref, lse_ref, ids_col, ids_row = refs[count : count + 6]
        joined, low_mixed, sums, head_sums = refs[count + 6 : count + 10]
        outs = refs[count + 10 : count + 10 + count]
        grad_out, grad_three = refs[count + 10 + count :]
        join(piece_refs, joined)
        grad_flat = jnp.zeros((total, part), WIDE)
        for a in range(0, width, wide):
            b = a + wide
            chunk = flat_rows(wp, a // wide * height, height, slice(wp.shape[2] - wide, wp.shape[2]))
            grad_flat += dot_nt(joined[:, a:b], chunk)
        grad_out[...] = grad_flat.astype(LOW)
        place = lax.broadcasted_iota(jnp.int32, (1, lanes), 1) // head_size
        for start, base in tiles_of(total, group, block):
            allowed = allowed_of(ids_col, ids_row, start, base, block, group, use_frame)
            stats = lse_ref[start : start + block, :]
            for lane in range(0, part, lanes):
                query = qkv_ref[start : start + block, lane : lane + lanes] * jnp.asarray(scale, LOW)
                key = qkv_ref[base : base + group, part + lane : part + lane + lanes]
                value = qkv_ref[base : base + group, 2 * part + lane : 2 * part + lane + lanes]
                grad_here = grad_out[start : start + block, lane : lane + lanes]
                grad_q = jnp.zeros((block, lanes), WIDE)
                grad_k = jnp.zeros((group, lanes), WIDE)
                grad_v = jnp.zeros((group, lanes), WIDE)
                for h in range(per):
                    mask = place == h
                    head = lane // head_size + h
                    scores = dot_nt(jnp.where(mask, query, jnp.zeros_like(query)), key)
                    probs = jnp.exp(jnp.where(allowed, scores - stats[:, head : head + 1], -jnp.inf))
                    grad_p = dot_nt(jnp.where(mask, grad_here, jnp.zeros_like(grad_here)), value)
                    delta = jnp.sum(probs * grad_p, axis=-1, keepdims=True)
                    grad_s = (probs * (grad_p - delta)).astype(LOW)
                    grad_q = jnp.where(mask, dot(grad_s, key), grad_q)
                    grad_k = jnp.where(mask, dot_tn(grad_s, query), grad_k)
                    grad_v = jnp.where(mask, dot_tn(probs.astype(LOW), grad_here), grad_v)
                grad_three[start : start + block, lane : lane + lanes] = grad_q * scale
                for at, grad in ((part, grad_k), (2 * part, grad_v)):
                    spot = (slice(base, base + group), slice(at + lane, at + lane + lanes))
                    if start == base:
                        grad_three[spot] = grad
                    else:
                        grad_three[spot] = grad_three[spot] + grad
        matrix = head_means(part, head_size)
        for i in range(2):
            here = slice(i * part, (i + 1) * part)
            grad = grad_three[:, here]
            unit_i, rate = head_normed(raw_ref[:, here], matrix)
            head_sums[i : i + 1, :] = jnp.sum(grad * unit_i, axis=0, keepdims=True)
            head_sums[2 + i : 3 + i, :] = jnp.sum(grad, axis=0, keepdims=True)
            inner = grad * gain_ref[i : i + 1, :]
            mean_one = head_mean(inner, matrix)
            mean_two = head_mean(inner * unit_i, matrix)
            result = rate * (inner - mean_one - unit_i * mean_two)
            sums[:, here] = jnp.sum(result, axis=0, keepdims=True)
            low_mixed[:, here] = result.astype(LOW)
        result = grad_three[:, 2 * part :]
        sums[:, 2 * part :] = jnp.sum(result, axis=0, keepdims=True)
        low_mixed[:, 2 * part :] = result.astype(LOW)
        weight = flat_rows(wq, 0, unit, slice(0, 3 * part))
        for start, stop, ref in spans(outs):
            ref[...] = dot_nt(low_mixed[start:stop, :], weight).astype(ref.dtype)

    outs = [
        shape_of((total, width), LOW),
        shape_of((total, 3 * part), LOW),
        shape_of((1, 3 * part), WIDE),
        shape_of((4, part), WIDE),
    ] + part_shapes(pieces, width)
    scratch = [pltpu.VMEM((total, part), LOW), pltpu.VMEM((total, 3 * part), WIDE)]
    args = list(pieces) + [attn] + ([] if proj is None else [proj])
    args += [head_gain, raw, qkv, lse, ids.reshape(-1, 1), ids.reshape(1, -1)]
    flops = 2 * total * (width * 4 * part + group * 5 * part)
    res = call(kernel, outs, args, "attn_backward", flops, scratch)
    return res[:4], res[4 : 4 + count // 2], res[4 + count // 2 :]


def attn_weight_grads(first, low_mixed, flat, att_low, rest, height, table):
    width, part = first.shape[1], flat.shape[1]
    unit = width // rest
    wide = width * height // unit
    places = hop_places(rest)
    steps = rest // 2

    def kernel(table_ref, first_ref, mixed_ref, flat_ref, att_ref, *refs):
        outs, packed, semaphores = refs[:-2], refs[-2], refs[-1]
        product = dot_tn(first_ref[...], mixed_ref[...]).astype(LOW)
        packed[:, :, : 3 * part] = product.reshape(rest, unit, 3 * part)
        product = dot_tn(flat_ref[...], att_ref[...]).astype(LOW)
        for j in range(unit // height):
            chunk = product[:, j * wide : (j + 1) * wide].reshape(rest, height, wide)
            packed[:, j * height : (j + 1) * height, 3 * part :] = chunk
        copies = []
        for i, (side, k) in enumerate(places):
            first_row = unit // 2 if i == steps else 0
            source = packed.at[table_ref[side, k], pl.ds(first_row, outs[i].shape[0]), :]
            copies.append(pltpu.make_async_copy(source, outs[i], semaphores.at[i]))
            copies[-1].start()
        wait_all(copies)

    flops = 8 * first.shape[0] * width * part
    outs = [shape_of((unit // 2 if k == steps else unit, 4 * part), LOW) for _, k in places]
    scratch = [pltpu.VMEM((rest, unit, 4 * part), LOW), pltpu.SemaphoreType.DMA((len(places),))]
    args = [table, first, low_mixed, flat, att_low]
    res = call(kernel, outs, args, "attn_weight_grads", flops, scratch, 1, far_out=range(len(outs)))
    return res[:steps], res[steps : 2 * steps], res[2 * steps]


def mlp_weight_grads(second, pre_low, act, branch_low, rest, table):
    width, hidden = second.shape[1], act.shape[1]
    rows = width // rest
    places = hop_places(rest)
    steps = rest // 2

    def kernel(table_ref, second_ref, pre_ref, act_ref, branch_ref, *refs):
        outs, packs, semaphores = refs[:-3], refs[-3:-1], refs[-1]
        copies = []
        for which, (left, right) in enumerate(((second_ref, pre_ref), (act_ref, branch_ref))):
            pack = packs[which]
            pack[...] = dot_tn(left[...], right[...]).astype(LOW).reshape(pack.shape)
            for i, (side, k) in enumerate(places):
                if k == steps and i // steps != which:
                    continue
                spot = outs[i].at[pl.ds(0 if k == steps else which * rows, rows), :]
                source = pack.at[table_ref[side, k]]
                copies.append(pltpu.make_async_copy(source, spot, semaphores.at[len(copies)]))
                copies[-1].start()
        wait_all(copies)

    flops = 4 * second.shape[0] * width * hidden
    outs = [shape_of((rows if k == steps else 2 * rows, width), LOW) for _, k in places]
    scratch = [pltpu.VMEM((rest, rows, width), LOW)] * 2 + [pltpu.SemaphoreType.DMA((2 * len(places),))]
    args = [table, second, pre_low, act, branch_low]
    res = call(kernel, outs, args, "mlp_weight_grads", flops, scratch, 1, far_out=range(len(outs)))
    return res[:steps], res[steps : 2 * steps], res[2 * steps]


def mlp_forward(pieces, sources, table, bias):
    rest, unit, hidden = sources[0].shape
    width = rest * unit
    far = [m for source in sources for m in source.args]
    total = sum(m.shape[0] for m in pieces)
    count = len(pieces)

    def kernel(table_ref, *refs):
        far_refs, refs, (up, down), semaphores = refs[: len(far)], refs[len(far) : -4], refs[-4:-2], refs[-2:]
        copies, more_copies = start_loads(sources, table_ref, far_refs, (up, down), semaphores)
        piece_refs = refs[:count]
        bias_ref = refs[count]
        second, act, slope = refs[count + 1 : count + 4]
        outs = refs[count + 4 :]
        join(piece_refs, second)
        wait_all(copies)
        pre = dot(second[...], flat_rows(up, 0, unit, slice(None))) + bias_ref[...]
        below = 0.5 * (1.0 + lax.erf(pre * ROOT_HALF))
        act[...] = (pre * below).astype(LOW)
        slope[...] = (below + pre * (ROOT_TWO_PI * jnp.exp(-0.5 * pre * pre))).astype(LOW)
        wait_all(more_copies)
        weight = flat_rows(down, 0, down.shape[1], slice(None))
        for start, stop, ref in spans(outs):
            ref[...] = dot(act[start:stop, :], weight).astype(ref.dtype)

    outs = [
        shape_of((total, width), LOW),
        shape_of((total, hidden), LOW),
        shape_of((total, hidden), LOW),
    ] + part_shapes(pieces, width)
    outs += [shape_of(source.shape, LOW) for source in sources]
    args = [table] + far + list(pieces) + [bias]
    flops, far_in = 4 * total * width * hidden, range(1, 1 + len(far))
    res = call(kernel, outs, args, "mlp_forward", flops, load_semaphores(sources), 1, far_in=far_in)
    return res[:3], res[3 : 3 + count // 2], res[3 + count // 2 : 3 + count], res[3 + count :]


def mlp_backward(pieces, weight_up, weight_down, slope):
    rest, unit, hidden = weight_up.shape
    width = rest * unit
    total = sum(m.shape[0] for m in pieces)
    count = len(pieces)

    def kernel(*refs):
        piece_refs = refs[:count]
        up, down, slope_ref = refs[count : count + 3]
        joined, low_pre, sums = refs[count + 3 : count + 6]
        outs = refs[count + 6 :]
        join(piece_refs, joined)
        weight = flat_rows(down, 0, down.shape[1], slice(None))
        grad = dot_nt(joined[...], weight) * slope_ref[...].astype(WIDE)
        sums[...] = jnp.sum(grad, axis=0, keepdims=True)
        low_pre[...] = grad.astype(LOW)
        weight = flat_rows(up, 0, unit, slice(None))
        for start, stop, ref in spans(outs):
            ref[...] = dot_nt(low_pre[start:stop, :], weight).astype(ref.dtype)

    outs = [
        shape_of((total, width), LOW),
        shape_of((total, hidden), LOW),
        shape_of((1, hidden), WIDE),
    ] + part_shapes(pieces, width)
    args = list(pieces) + [weight_up, weight_down, slope]
    res = call(kernel, outs, args, "mlp_backward", 4 * total * width * hidden)
    return res[:3], res[3 : 3 + count // 2], res[3 + count // 2 :]


def added(refs):
    total = refs[0][...]
    for ref in refs[1:]:
        total = total + ref[...].astype(WIDE)
    return total


def row_of(vectors, kind, depth, which):
    at = kind + 2 * depth + which
    return vectors[at : at + 1, :]


def branch_norm(stream, terms, vectors, depth, which):
    after = (depth, 1) if which == 0 else (depth + 1, 0)

    def kernel(stream_ref, *refs):
        (vec, branch, result, low), term_refs = refs[-4:], refs[:-4]
        value = added(term_refs) + row_of(vec, OUT, depth, which)
        branch[...] = value
        value = stream_ref[...].astype(WIDE) + row_of(vec, SCALE, depth, which) * value
        result[...] = value
        unit, _ = normed(value)
        low[...] = (unit * row_of(vec, GAIN, *after) + row_of(vec, SHIFT, *after)).astype(LOW)

    outs = [shape_of(stream.shape, WIDE), shape_of(stream.shape, WIDE), shape_of(stream.shape, LOW)]
    return call(kernel, outs, [stream, *terms, vectors], "branch_norm")


def turn(middle, terms, cotangent, vectors):
    def kernel(middle_ref, *refs):
        (cot, vec, result, low, sums), term_refs = refs[-5:], refs[:-5]
        branch = added(term_refs) + row_of(vec, OUT, 1, 1)
        scale = row_of(vec, SCALE, 1, 1)
        result[...] = (middle_ref[...] + scale * branch).astype(LOW)
        grad = cot[...].astype(WIDE)
        grad_branch = grad * scale
        low[...] = grad_branch.astype(LOW)
        sums[0:1, :] = jnp.sum(grad * branch, axis=0, keepdims=True)
        sums[1:2, :] = jnp.sum(grad_branch, axis=0, keepdims=True)

    shape = middle.shape
    outs = [shape_of(shape, LOW), shape_of(shape, LOW), shape_of((2, shape[1]), WIDE)]
    return call(kernel, outs, [middle, *terms, cotangent, vectors], "turn")


def norm_back(grad, terms, stream, branch, vectors, depth, which, before):
    def kernel(*refs):
        grad_ref, stream_ref, vec = refs[0], refs[1], refs[2]
        inputs = 4 if before else 3
        term_refs = refs[inputs : inputs + len(terms)]
        result, low, sums = (refs[inputs + len(terms) :] + (None,))[:3] if before else (
            None, refs[inputs + len(terms)], refs[inputs + len(terms) + 1],
        )
        came = added(term_refs)
        unit, rate = normed(stream_ref[...].astype(WIDE))
        sums[0:1, :] = jnp.sum(came * unit, axis=0, keepdims=True)
        sums[1:2, :] = jnp.sum(came, axis=0, keepdims=True)
        value = grad_ref[...].astype(WIDE)
        value = value + normed_back(came, unit, rate, row_of(vec, GAIN, depth, which))
        if not before:
            low[...] = value.astype(LOW)
            return
        result[...] = value
        sums[2:3, :] = jnp.sum(value * refs[3][...], axis=0, keepdims=True)
        value = value * row_of(vec, SCALE, *before)
        sums[3:4, :] = jnp.sum(value, axis=0, keepdims=True)
        low[...] = value.astype(LOW)

    shape = grad.shape
    outs = [shape_of(shape, LOW), shape_of((4 if before else 2, shape[1]), WIDE)]
    args = [grad, stream, vectors]
    if before:
        outs = [shape_of(shape, WIDE)] + outs
        args = args + [branch]
    return call(kernel, outs, args + list(terms), "norm_back")


def split_grads(grads, me):
    rows, width = grads[0].shape[0] * len(grads) // 4, grads[0].shape[1]

    def kernel(me_ref, *refs):
        ins, outs = refs[: len(grads)], refs[len(grads) : len(grads) + 4]
        joined = refs[-1]
        join(ins, joined)
        for away, out in enumerate(outs):
            member = jnp.bitwise_xor(me_ref[0], away)
            out[...] = joined[pl.ds(pl.multiple_of(member * rows, rows), rows), :].astype(LOW)

    scratch = [pltpu.VMEM((4 * rows, width), grads[0].dtype)]
    out = shape_of((rows, width), LOW)
    return call(kernel, [out] * 4, [me, *grads], "split_grads", scratch=scratch, scalars=1)


def place_grads(qkv_pieces, up_pieces, proj, down, part, rest, me):
    rows, hidden = up_pieces[0][0].shape
    width = 4 * part
    lanes = hidden // rest

    def kernel(me_ref, *refs):
        pieces, (proj_ref, down0, down1) = refs[:16], refs[16:19]
        qkv_out, up_out, proj_out, down_out = refs[19:]
        for depth in range(2):
            for away in range(4):
                member = jnp.bitwise_xor(me_ref[0], away)
                ref = pieces[4 * depth + away]
                for s in range(3):
                    start = pl.multiple_of(s * width + member * part, 128)
                    value = ref[:, s * part : (s + 1) * part].astype(WIDE)
                    qkv_out[depth, :, pl.ds(start, part)] = value
                ref = pieces[8 + 4 * depth + away]
                for f in range(rest):
                    start = pl.multiple_of((f * 4 + member) * lanes, 128)
                    value = ref[:, f * lanes : (f + 1) * lanes].astype(WIDE)
                    up_out[depth, :, pl.ds(start, lanes)] = value
            down_out[depth] = (down0, down1)[depth][...].astype(WIDE)
        proj_out[...] = proj_ref[...].astype(WIDE)

    outs = [
        shape_of((2, rows, 3 * width), WIDE),
        shape_of((2, rows, 4 * hidden), WIDE),
        shape_of(proj.shape, WIDE),
        shape_of((2,) + down[0].shape, WIDE),
    ]
    args = [me, *qkv_pieces[0], *qkv_pieces[1], *up_pieces[0], *up_pieces[1], proj, *down]
    return call(kernel, outs, args, "place_grads", scalars=1)


def on_device(
    tokens,
    cotangent,
    scene_ids,
    frame_index,
    qkv_weight,
    qkv_bias,
    proj_weight,
    fc1_weight,
    fc1_bias,
    fc2_weight,
    out_bias,
    norm_gain,
    norm_bias,
    layer_scale,
    qk_gain,
    qk_bias,
):
    frames = lax.axis_size("frame")
    team = 2 * frames
    rest = lax.axis_size("outer") * lax.axis_size("inner")
    count = team * rest
    rows, width = tokens.shape
    head_size = qk_gain.shape[-1]
    heads = width // head_size // team
    part = heads * head_size
    hidden = fc1_weight.shape[-1] // team
    mine = lax.axis_index("core") * frames + lax.axis_index("frame")
    here = lax.axis_index("outer") * lax.axis_size("inner") + lax.axis_index("inner")
    me = mine.reshape(1).astype(jnp.int32)
    shard_rows = qkv_weight.shape[1]
    fc2_rows = fc2_weight.shape[1]
    unit = team * shard_rows
    table = ring_table()
    quick = frames == 2 and shard_rows % 32 == 0 and part % 128 == 0 and (hidden // rest) % 128 == 0
    quick = quick and hidden == width and width // count == 32 and count * rows // FRAME_TOK <= 256

    small_parts = (qkv_bias, fc1_bias, out_bias, norm_gain, norm_bias, layer_scale)
    head_gain = jnp.tile(qk_gain.astype(WIDE), (1, 1, heads))
    head_shift = jnp.tile(qk_bias.astype(WIDE), (1, 1, heads))
    weights = []
    if quick:
        proj_here = lax.ppermute(proj_weight, EVERY, spread(count, team))
        shards, below = [], None
        for depth in range(2):
            small = (qkv_bias, fc1_bias, scene_ids.reshape(1, rows)) + small_parts[2:]
            split = split_weights(depth, (qkv_weight, fc1_weight), () if depth else small, part, rest, me)
            pieces = [split[0], swap(split[1], "frame"), swap(split[2], "core"), cross(split[3])]
            if depth == 0:
                below = pieces
            shards.append(pack_weights(pieces, proj_here, fc2_weight, depth, part, me, depth == 0))
        ids = jnp.concatenate([m[shard_rows, 512 : 512 + rows] for m in below]).astype(jnp.int32)
        tokens_all = team_gather(tokens)
        rings = []
        for depth in range(2):
            attn, both = shards[depth]
            ring = RingGather(attn, unit // 2, rest)
            if depth == 0:
                steps(1, ring)
                ring.came = tie(*ring.came, *shards[1])[:2]
            came = steps(LEAD[depth] - 1 if depth == 0 else LEAD[depth], ring)
            both = tie(both, *came)[0] if came else both
            rings.append((ring, RingGather(both, unit, rest)))
            for ring in rings[depth]:
                steps(rest, ring)
        vectors, bias_qkv, bias_up = unpack_vectors(rings[0][0].rows(unit, SMALL_ROWS), table, me)
    else:
        proj_here = lax.ppermute(proj_weight, EVERY, spread(count, team))
        for depth in range(2):
            attn = exchange_columns(
                qkv_weight[depth]
                .reshape(shard_rows, 3, team, part)
                .transpose(0, 2, 1, 3)
                .reshape(shard_rows, team, 3 * part)
            ).reshape(unit, 3 * part)
            attn = jnp.concatenate([attn, widen(proj_here[depth], part)], axis=1)
            up = exchange_columns(
                fc1_weight[depth]
                .reshape(shard_rows, rest, team, hidden // rest)
                .transpose(0, 2, 1, 3)
                .reshape(shard_rows, team, hidden)
            ).reshape(unit, hidden)
            down = widen(fc2_weight[depth], hidden)
            attn, up, down = (lax.all_gather(m, REST, axis=0, tiled=False) for m in (attn, up, down))
            proj = Whole(narrow(attn[:, :, 3 * part :], shard_rows).reshape(1, part, width), 0, part)
            down = Whole(narrow(down, fc2_rows).reshape(1, hidden, width), 0, hidden)
            weights.append(((Whole(attn, 0, unit), proj, part, width, table), (Whole(up, 0, unit), down)))
        small = small_gather(jnp.concatenate([m.reshape(-1) for m in small_parts])).astype(WIDE)
        n_qkv, n_up = qkv_bias.size, fc1_bias.size
        bias_qkv = small[:, :n_qkv].reshape(count, 2, -1).transpose(1, 0, 2).reshape(2, 3, team, part)
        bias_qkv = lax.dynamic_index_in_dim(bias_qkv, mine, 2, keepdims=False).reshape(2, 3 * part)
        bias_up = small[:, n_qkv : n_qkv + n_up].reshape(rest, team, 2, -1)
        bias_up = lax.dynamic_index_in_dim(bias_up, mine, 1, keepdims=False)
        bias_up = bias_up.transpose(1, 0, 2).reshape(2, hidden)
        vectors = small[:, n_qkv + n_up :].reshape(count, 16, -1).transpose(1, 0, 2).reshape(16, width)
        ids = jnp.concatenate([m.reshape(-1) for m in team_gather(scene_ids.reshape(1, rows))])
        tokens_all = team_gather(tokens)

    gathered = []
    streams, middles, branches, kept = [tokens], [], [], []
    for depth in range(2):
        work = None
        if quick:
            attn_weights = (rings[depth][0].rows(0, unit), None, shard_rows, part, table)
        else:
            attn_weights, mlp_sources = weights[depth]
        kept_attn, own, peer, attn_weights = attn_forward(
            team_gather(low, work, work) if depth else tokens_all, attn_weights, bias_qkv[depth : depth + 1],
            head_gain[depth], head_shift[depth], ids, head_size, frames, depth == 0, None if depth else vectors,
        )
        terms = team_sum(own, peer, work)
        branch_one, middle, low = branch_norm(streams[depth], terms, vectors, depth, 0)
        pieces = team_gather(low, work, work)
        if quick:
            mlp_sources = (rings[depth][1].rows(0, unit), rings[depth][1].rows(unit, unit))
        kept_mlp, own, peer, mlp_weights = mlp_forward(pieces, mlp_sources, table, bias_up[depth : depth + 1])
        gathered.append((attn_weights, mlp_weights))
        terms = team_sum(own, peer, work)
        branch_two = None
        if depth == 0:
            branch_two, stream, low = branch_norm(middle, terms, vectors, 0, 1)
            streams.append(stream)
        middles.append(middle)
        branches.append((branch_one, branch_two))
        kept.append((kept_attn, kept_mlp))

    activations, low, turn_sums = turn(middles[1], terms, cotangent, vectors)
    grad = cotangent
    names, token_sums = [(SCALE, 1, 1), (OUT, 1, 1)], [turn_sums]
    sums_up, sums_qkv, head_sums = [None, None], [None, None], [None, None]
    finals = [{}, {}]
    ring = RingSums(rest)

    def end_mlp(depth):
        def end(up_sum, down_sum):
            if not quick:
                up = exchange_columns(up_sum.astype(LOW).reshape(team, shard_rows, hidden).transpose(1, 0, 2))
                up = up.reshape(team, shard_rows, rest, hidden // rest).transpose(1, 2, 0, 3)
                finals[depth].update(up=up.reshape(shard_rows, -1), down=narrow(down_sum, fc2_rows))
                return
            end_up(depth)(up_sum)
            finals[depth].update(down=down_sum)

        return end

    def end_up(depth):
        def end(*halves):
            m = split_grads(halves, me)
            pieces = [m[0], swap(m[1], "frame"), swap(m[2], "core"), cross(m[3])]
            ring.started += pieces[1:]
            finals[depth].update(up=pieces)

        return end

    def end_attn(depth):
        def end(low_sum, high_sum):
            if not quick:
                both = jnp.concatenate([low_sum, high_sum], axis=0)
                qkv = exchange_columns(
                    both[:, : 3 * part].astype(LOW).reshape(team, shard_rows, 3 * part).transpose(1, 0, 2)
                )
                qkv = qkv.reshape(team, shard_rows, 3, part).transpose(1, 2, 0, 3)
                proj = narrow(both[:, 3 * part :], shard_rows)
                finals[depth].update(qkv=qkv.reshape(shard_rows, -1), proj=proj.astype(LOW))
                return
            m = split_grads([low_sum[:, : 3 * part], high_sum[:, : 3 * part]], me)
            proj = jnp.concatenate([n[:, 3 * part :] for n in (low_sum, high_sum)], axis=0)
            pieces = [m[0], swap(m[1], "frame"), swap(m[2], "core"), cross(m[3])]
            ring.started += pieces[1:] if depth else []
            finals[depth].update(
                qkv=pieces,
                proj=narrow(proj, shard_rows).astype(LOW),
            )

        return end

    for depth in (1, 0):
        attn_weights, (weight_up, weight_down) = gathered[depth]
        kept_attn, (second, act, slope) = kept[depth]
        first, flat = kept_attn[0], kept_attn[4]
        pieces = team_gather(low, ring.work, ring.pump)
        (branch_low, pre_low, sum_up), own, peer = mlp_backward(pieces, weight_up, weight_down, slope)
        sums_up[depth] = sum_up
        if quick:
            mlp_parts = mlp_weight_grads(second, pre_low, act, branch_low, rest, table)
        else:
            grad_up = dot_tn(second, pre_low).astype(LOW).reshape(rest, unit, hidden)
            grad_down = dot_tn(act, branch_low).astype(LOW)
            grad_down = grad_down.reshape(rest, fc2_rows, width // hidden, hidden)
            grad_down = grad_down.transpose(0, 2, 1, 3).reshape(rest, -1, hidden)
            end_mlp(depth)(rest_sum(grad_up), rest_sum(grad_down))
        if quick:
            ring.add(*mlp_parts, end_mlp(depth))
        terms = team_sum(own, peer, ring.work, ring.pump)
        grad_middle, low, sums = norm_back(
            grad, terms, middles[depth], branches[depth][0], vectors, depth, 1, (depth, 0)
        )
        names += [(GAIN, depth, 1), (SHIFT, depth, 1), (SCALE, depth, 0), (OUT, depth, 0)]
        token_sums.append(sums)
        pieces = team_gather(low, ring.work, ring.pump)
        (att_low, mixed_low, sum_qkv, head_sum), own, peer = attn_backward(
            pieces, attn_weights, head_gain[depth], kept_attn, ids, head_size, frames, depth == 0
        )
        sums_qkv[depth], head_sums[depth] = sum_qkv, head_sum
        if quick:
            attn_parts = attn_weight_grads(first, mixed_low, flat, att_low, rest, shard_rows, table)
        else:
            grad_qkv = dot_tn(first, mixed_low).astype(LOW).reshape(rest, unit, 3 * part)
            grad_proj = dot_tn(flat, att_low).astype(LOW).reshape(rest, shard_rows, team, part)
            grad_proj = grad_proj.transpose(0, 2, 1, 3).reshape(rest, unit, part)
            attn = rest_sum(jnp.concatenate([grad_qkv, grad_proj], axis=2))
            end_attn(depth)(attn[: unit // 2], attn[unit // 2 :])
        if quick:
            ring.add(*attn_parts, end_attn(depth))
        terms = team_sum(own, peer, ring.work, ring.pump)
        if depth == 1:
            grad, low, sums = norm_back(
                grad_middle, terms, streams[1], branches[0][1], vectors, 1, 0, (0, 1)
            )
            names += [(GAIN, 1, 0), (SHIFT, 1, 0), (SCALE, 0, 1), (OUT, 0, 1)]
        else:
            input_grad, sums = norm_back(grad_middle, terms, tokens, None, vectors, 0, 0, None)
            names += [(GAIN, 0, 0), (SHIFT, 0, 0)]
        token_sums.append(sums)
    while ring.busy():
        ring.hop()

    proj_grad = lax.ppermute(
        jnp.stack([finals[0]["proj"], finals[1]["proj"]]), EVERY, [(b, a) for a, b in spread(count, team)]
    )
    if quick:
        qkv_grad, up_grad, proj_grad, down_grad = place_grads(
            [m["qkv"] for m in finals], [m["up"] for m in finals], proj_grad,
            [m["down"] for m in finals], part, rest, me,
        )
    else:
        proj_grad = proj_grad.astype(WIDE)
        qkv_grad, up_grad, down_grad = (
            jnp.stack([m[name] for m in finals]).astype(WIDE) for name in ("qkv", "up", "down")
        )

    full_qkv = lax.dynamic_update_slice(
        jnp.zeros((6, team, part), WIDE),
        jnp.concatenate(sums_qkv, axis=0).reshape(6, 1, part),
        (0, mine, 0),
    ).reshape(6, width)
    head_all = jnp.stack(head_sums).reshape(-1, heads, head_size).sum(axis=1).reshape(1, -1)
    head_all = jnp.pad(head_all, ((0, 0), (0, width - head_all.shape[1])))
    team_rows = jnp.concatenate([*token_sums, full_qkv, head_all], axis=0)
    team_rows = team_rows + swap(team_rows, "core")
    if frames == 2:
        team_rows = team_rows + swap(team_rows, "frame")
    else:
        team_rows = lax.psum(team_rows, "frame")
    sums_up = jnp.concatenate(sums_up, axis=0).reshape(2, rest, hidden // rest)
    sums_up = jnp.pad(sums_up, ((0, 0), (0, 0), (0, (width - hidden) // rest))).reshape(2, width)
    split = jnp.concatenate([team_rows[:16], sums_up], axis=0)
    split, common = small_sum(split, team_rows[16:])
    vector_grads = lax.dynamic_slice_in_dim(split[:16], mine * (width // count), width // count, 1)
    ordered = [(kind, depth, place) for kind in (OUT, GAIN, SHIFT, SCALE) for depth in (0, 1) for place in (0, 1)]
    vector_grads = jnp.stack([vector_grads[names.index(name)] for name in ordered]).reshape(4, 2, 2, -1)
    grad_bias_qkv = common[:6].reshape(2, -1)
    grad_bias_qkv = lax.dynamic_slice_in_dim(
        grad_bias_qkv, (here * team + mine) * qkv_bias.shape[1], qkv_bias.shape[1], 1
    )
    head_all = common[6, : 8 * head_size].reshape(2, 2, 2, head_size)
    return (
        activations,
        input_grad,
        qkv_grad,
        grad_bias_qkv,
        proj_grad,
        up_grad,
        split[16:, : hidden // rest],
        down_grad,
        vector_grads[0],
        vector_grads[1],
        vector_grads[2],
        vector_grads[3],
        head_all[:, 0],
        head_all[:, 1],
    )


def solution(mesh):
    scenes, frames = mesh.shape["scene"], mesh.shape["frame"]
    rest = scenes // 2
    outer = 4 if rest % 4 == 0 else rest
    grid = Mesh(mesh.devices.reshape(outer, rest // outer, 2, frames), EVERY)
    by_rows = P(EVERY, None)
    second = P(None, EVERY)
    second_rows = P(None, EVERY, None)
    last = P(None, None, EVERY)
    return jax.shard_map(
        on_device,
        mesh=grid,
        in_specs=(
            by_rows, by_rows, P(EVERY), P(EVERY), second_rows, second, second_rows, second_rows,
            second, second_rows, last, last, last, last, P(), P(),
        ),
        out_specs=(
            by_rows, by_rows, second_rows, second, second_rows, second_rows, second, second_rows,
            last, last, last, last, P(), P(),
        ),
        check_vma=False,
    )
```

```python
import jax
import jax.numpy as jnp
import numpy as np
from jax import lax
from jax.experimental import pallas as pl
from jax.experimental.pallas import tpu as pltpu
from jax.sharding import Mesh
from jax.sharding import PartitionSpec as P

EPSILON = 1e-06
FRAME_TOK = 64
LOW = jnp.bfloat16
WIDE = jnp.float32
EVERY = ("outer", "inner", "core", "frame")
REST = ("outer", "inner")
TEAM = ("core", "frame")
ROOT_HALF = 0.7071067811865476
ROOT_TWO_PI = 0.3989422804014327
MEBI = 1024 * 1024
OUT, GAIN, SHIFT, SCALE = 0, 4, 8, 12
HOPS = (0, 0, 1, 0, 1, 0, 1, 0) + (1, 0, 1, 1, 0, 0, 1, 0)
LEAD = (4, 4)


def dot(left, right):
    return jnp.dot(left, right, preferred_element_type=WIDE)


def dot_tn(left, right):
    return lax.dot_general(left, right, (((0,), (0,)), ((), ())), preferred_element_type=WIDE)


def dot_nt(left, right):
    return lax.dot_general(left, right, (((1,), (1,)), ((), ())), preferred_element_type=WIDE)


def normed(values):
    center = values - jnp.mean(values, axis=-1, keepdims=True)
    rate = lax.rsqrt(jnp.mean(center * center, axis=-1, keepdims=True) + EPSILON)
    return center * rate, rate


def normed_back(grad, unit, rate, gain):
    inner = grad * gain
    mean_one = jnp.mean(inner, axis=-1, keepdims=True)
    mean_two = jnp.mean(inner * unit, axis=-1, keepdims=True)
    return rate * (inner - mean_one - unit * mean_two)


def shape_of(shape, dtype):
    return jax.ShapeDtypeStruct(shape, dtype)


def call(kernel, outs, args, name, flops=0, scratch=(), scalars=0, far_in=(), far_out=()):
    hbm = pl.BlockSpec(memory_space=pltpu.HBM)
    vmem = pl.BlockSpec(memory_space=pltpu.VMEM)
    smem = pl.BlockSpec(memory_space=pltpu.SMEM)
    in_specs = [smem if i < scalars else hbm if i in far_in else vmem for i in range(len(args))]
    bytes_all = sum(m.size * m.dtype.itemsize for m in args)
    bytes_all += sum(int(np.prod(s.shape)) * s.dtype.itemsize for s in outs)
    sized = [s for s in scratch if hasattr(s, "shape") and s.memory_space == pltpu.VMEM]
    held = sum(int(np.prod(s.shape)) * s.dtype.itemsize for s in sized)
    limit = (held * 5 // 4 + bytes_all * 2 // 5 if flops else bytes_all) + (8 if flops else 3) * MEBI
    args = [pltpu.with_memory_space_constraint(m, pltpu.HBM) if i in far_in else m for i, m in enumerate(args)]
    outs = [pltpu.HBM(m.shape, m.dtype) if i in far_out else m for i, m in enumerate(outs)]
    return pl.pallas_call(
        kernel,
        out_shape=list(outs),
        in_specs=in_specs,
        out_specs=[hbm if i in far_out else vmem for i in range(len(outs))],
        scratch_shapes=list(scratch),
        compiler_params=pltpu.CompilerParams(vmem_limit_bytes=limit),
        cost_estimate=pl.CostEstimate(flops=flops, bytes_accessed=bytes_all, transcendentals=0),
        name=name,
    )(*args)


def swap(values, axis):
    return lax.ppermute(values, axis, [(0, 1), (1, 0)])


def cross(values):
    return lax.ppermute(values, TEAM, [(0, 3), (1, 2), (2, 1), (3, 0)])


def team_gather(values, work=None, pump=None):
    if lax.axis_size("frame") == 2:
        far = swap(values, "frame")
        near = swap(work(values) if work else values, "core")
        far = pump(far) if pump else far
        return [values, far, near, swap(far, "core")]
    both = lax.all_gather(values, "frame", axis=0, tiled=True)
    return [both, swap(both, "core")]


def team_sum(own, peer, work=None, pump=None):
    if lax.axis_size("frame") == 2:
        far = own[1] + swap(peer[1], "core").astype(WIDE)
        came = swap(far.astype(LOW), "frame")
        near = swap(work(peer[0]) if work else peer[0], "core")
        came = pump(came) if pump else came
        return [own[0], near, came]
    total = own[0] + swap(peer[0], "core").astype(WIDE)
    return [lax.psum_scatter(total.astype(LOW), "frame", scatter_dimension=0, tiled=True).astype(WIDE)]


def exchange_columns(values):
    parts = values.transpose(1, 0, 2)
    frames = lax.axis_size("frame")
    parts = parts.reshape((2, frames) + parts.shape[1:])
    both = lax.all_to_all(parts, "frame", 1, 1, tiled=True)
    here = lax.axis_index("core")
    keep = lax.dynamic_index_in_dim(both, here, 0, keepdims=False)
    came = swap(lax.dynamic_index_in_dim(both, 1 - here, 0, keepdims=False), "core")
    out = jnp.stack([jnp.where(here == 0, keep, came), jnp.where(here == 0, came, keep)], axis=0)
    return out.reshape((2 * frames,) + out.shape[2:])


SMALL_ROWS = 16


def split_weights(depth, weights, vectors, part, rest, me):
    qkv, up = weights
    _, rows, width = qkv.shape
    width //= 3
    hidden = up.shape[2] // 4
    lanes = hidden // rest
    extra = SMALL_ROWS if vectors else 0

    far = list(vectors)

    def kernel(me_ref, qkv_ref, up_ref, *refs):
        outs, small = refs[len(far) : len(far) + 4], refs[len(far) + 4 : -1]
        copies = []
        for source, target in zip(refs, small):
            copies.append(pltpu.make_async_copy(source, target, refs[-1].at[len(copies)]))
            copies[-1].start()
        wait_all(copies)
        for away, out in enumerate(outs):
            member = jnp.bitwise_xor(me_ref[0], away)
            for s in range(3):
                start = pl.multiple_of(s * width + member * part, 128)
                out[:rows, s * part : (s + 1) * part] = qkv_ref[depth, :, pl.ds(start, part)]
            for f in range(rest):
                start = pl.multiple_of((f * 4 + member) * lanes, 128)
                at = 3 * part + f * lanes
                out[:rows, at : at + lanes] = up_ref[depth, :, pl.ds(start, lanes)]
            if not vectors:
                continue
            out[rows:, :] = jnp.zeros((extra, out.shape[1]), LOW)
            bias_qkv, bias_up, ids = small[:3]
            for i, ref in enumerate(small[3:]):
                for d in range(2):
                    for j in range(2):
                        at = rows + 4 * i + 2 * d + j
                        out[at : at + 1, : ref.shape[2]] = ref[d, j : j + 1, :]
            out[rows : rows + 2, 128 : 128 + bias_qkv.shape[1]] = bias_qkv[...]
            out[rows : rows + 2, 256 : 256 + bias_up.shape[1]] = bias_up[...]
            out[rows : rows + 1, 512 : 512 + ids.shape[1]] = ids[...].astype(WIDE).astype(LOW)

    out = shape_of((rows + extra, 3 * part + hidden), qkv.dtype)
    scratch = [pltpu.VMEM(m.shape, m.dtype) for m in far] + [pltpu.SemaphoreType.DMA((len(far) + 1,))]
    args = [me, qkv, up, *far]
    return call(kernel, [out] * 4, args, "split_weights", 0, scratch, 1, far_in=range(3, 3 + len(far)))


def pack_weights(pieces, proj, down, depth, part, me, vectors):
    rows = proj.shape[1]
    unit = 4 * rows
    hidden = pieces[0].shape[1] - 3 * part

    def kernel(me_ref, p0, p1, p2, p3, proj_ref, down_ref, attn, up, small):
        for away, ref in enumerate((p0, p1, p2, p3)):
            member = jnp.bitwise_xor(me_ref[0], away)
            start = pl.multiple_of(member * rows, rows)
            attn[pl.ds(start, rows), : 3 * part] = ref[:rows, : 3 * part]
            up[pl.ds(start, rows), :] = ref[:rows, 3 * part :]
            if vectors:
                small[member] = ref[rows:, :640]
        for j in range(4):
            attn[j * rows : (j + 1) * rows, 3 * part :] = proj_ref[depth, :, j * part : (j + 1) * part]
        up[unit:, :] = down_ref[depth]
        if vectors:
            attn[unit:, :] = jnp.zeros((SMALL_ROWS, 4 * part), LOW)
            for at, start, size in ((0, 0, 32), (128, 128, 96), (512, 256, 128)):
                joined = [small[m, :, start : start + size].astype(WIDE) for m in range(4)]
                value = jnp.concatenate(joined, axis=1).astype(LOW)
                attn[unit:, at : at + 4 * size] = value

    extra = SMALL_ROWS if vectors else 0
    outs = [shape_of((unit + extra, 4 * part), LOW), shape_of((2 * unit, hidden), LOW)]
    scratch = [pltpu.VMEM((4, SMALL_ROWS, 640), LOW)]
    return call(kernel, outs, [me, *pieces, proj, down], "pack_weights", scratch=scratch, scalars=1)


def unpack_vectors(source, table, me):
    rest, _, width = source.shape
    part = width // 4

    def kernel(me_ref, table_ref, *refs):
        vec, bias_qkv, bias_up, small, whole, semaphores = refs[source.count :]
        wait_all(source.start(refs[: source.count], table_ref, small, semaphores))
        for f in range(rest):
            vec[:, f * 128 : (f + 1) * 128] = small[f, :, :128].astype(WIDE)
            whole[:, f * 384 : (f + 1) * 384] = small[f, :, 128:512].astype(WIDE)
            start = pl.multiple_of(512 + me_ref[0] * 128, 128)
            bias_up[:, f * 128 : (f + 1) * 128] = small[f, :, pl.ds(start, 128)].astype(WIDE)
        for s in range(3):
            start = pl.multiple_of(s * width + me_ref[0] * part, 128)
            bias_qkv[:, s * part : (s + 1) * part] = whole[:, pl.ds(start, part)]

    outs = [shape_of((16, width), WIDE), shape_of((16, 3 * part), WIDE), shape_of((16, width), WIDE)]
    scratch = [
        pltpu.VMEM((rest, SMALL_ROWS, width), LOW),
        pltpu.VMEM((16, 3 * width), WIDE),
        pltpu.SemaphoreType.DMA((source.count,)),
    ]
    args = [me, table, *source.args]
    return call(kernel, outs, args, "unpack_vectors", 0, scratch, 2, far_in=range(2, 2 + source.count))


def spread(count, team):
    rest = count // team
    return [(i, (i % rest) * team + i // rest) for i in range(count)]


def widen(rows, width):
    height, columns = rows.shape
    parts = columns // width
    if parts == 1:
        return rows
    return rows.reshape(height, parts, width).transpose(1, 0, 2).reshape(parts * height, width)


def narrow(stacked, height):
    lead = stacked.shape[:-2]
    parts = stacked.shape[-2] // height
    if parts == 1:
        return stacked
    width = stacked.shape[-1]
    shaped = stacked.reshape(lead + (parts, height, width))
    return jnp.moveaxis(shaped, -3, -2).reshape(lead + (height, parts * width))


def ring_order(outer, inner):
    order = []
    for a in range(outer):
        row = range(1, inner) if a % 2 == 0 else range(inner - 1, 0, -1)
        order += [a * inner + b for b in row]
    return order + [a * inner for a in range(outer - 1, -1, -1)]


def ring_table():
    outer, inner = lax.axis_size("outer"), lax.axis_size("inner")
    order = ring_order(outer, inner)
    rest = outer * inner
    place = {team: i for i, team in enumerate(order)}
    table = np.array(
        [
            [[order[(place[f] + sign * k) % rest] for k in range(rest)] for sign in (-1, 1)]
            for f in range(rest)
        ],
        np.int32,
    )
    here = lax.axis_index("outer") * inner + lax.axis_index("inner")
    return lax.dynamic_index_in_dim(jnp.asarray(table), here, 0, keepdims=False)


def ring_shift(values, sign):
    order = ring_order(lax.axis_size("outer"), lax.axis_size("inner"))
    rest = len(order)
    return lax.ppermute(values, REST, [(order[i], order[(i + sign) % rest]) for i in range(rest)])


def ring_step(low_half, high_half):
    low_half, high_half = ring_shift(low_half, 1), ring_shift(high_half, -1)
    return lax.optimization_barrier((low_half, high_half))


class RingGather:
    def __init__(self, shard, cut, rest):
        self.steps = rest // 2
        self.cut = cut
        self.back, self.ahead = [shard], [shard]
        self.came = (ring_shift(shard, 1), ring_shift(shard, -1))

    def take(self, came):
        self.back.append(came[0])
        self.ahead.append(came[1])
        self.came = None
        if len(self.back) == self.steps:
            came = (came[0][: self.cut], came[1][self.cut :])
        if len(self.back) <= self.steps:
            self.came = (ring_shift(came[0], 1), ring_shift(came[1], -1))

    def rows(self, first, count):
        out = []
        for side, arrays in enumerate((self.back, self.ahead)):
            out += [(m, side, k, 0, first, count) for k, m in enumerate(arrays[: self.steps]) if k or not side]
        stop = min(first + count, self.cut)
        if stop > first:
            out.append((self.back[self.steps], 0, self.steps, 0, first, stop - first))
        start = max(first, self.cut)
        if start < first + count:
            out.append(
                (self.ahead[self.steps], 1, self.steps, start - first, start - self.cut, first + count - start)
            )
        return Pieces(out, 2 * self.steps, count)


def steps(count, ring):
    came = ()
    for _ in range(count):
        if ring.came is None:
            break
        came = tie(*ring.came)
        ring.take(came)
    return came


class Pieces:
    def __init__(self, entries, rest, rows):
        self.entries = entries
        self.args = [entry[0] for entry in entries]
        self.count = len(entries)
        self.shape = (rest, rows, self.args[0].shape[1])

    def start(self, refs, table_ref, target, semaphores):
        copies = []
        for ref, (_, side, k, first, begin, rows) in zip(refs, self.entries):
            spot = target.at[table_ref[side, k], pl.ds(first, rows), :]
            copies.append(pltpu.make_async_copy(ref.at[pl.ds(begin, rows), :], spot, semaphores.at[len(copies)]))
            copies[-1].start()
        return copies


class Whole:
    count = 1

    def __init__(self, array, first, rows):
        self.first = first
        self.args = [array]
        self.shape = (array.shape[0], rows, array.shape[2])

    def start(self, refs, table_ref, target, semaphores):
        source = refs[0].at[:, pl.ds(self.first, self.shape[1]), :]
        copy = pltpu.make_async_copy(source, target, semaphores.at[0])
        copy.start()
        return [copy]


def wait_all(copies):
    for copy in copies:
        copy.wait()


def tie(*values):
    return lax.optimization_barrier(values)


class RingSums:
    def __init__(self, rest):
        self.steps = rest // 2
        self.active = []
        self.waiting = []
        self.came = None
        self.started = []
        self.plan = iter(HOPS)

    def work(self, value):
        if next(self.plan):
            if self.came is not None:
                self.came = tie(*self.came, value)[:2]
            self.hop()
        started, self.started = self.started, []
        return tie(value, *started)[0] if started else value

    def pump(self, value):
        return self.hop(value) if next(self.plan) else value

    def add(self, ahead, behind, own, done):
        self.waiting.append(
            {"parts": (ahead, behind), "own": own, "rows": own.shape[0], "done": done, "hop": 0}
        )
        self.started.append(own)

    def hop(self, *values):
        if self.came is not None:
            tied = tie(*values, *self.came)
            values, self.came = tied[: len(values)], tied[len(values) :]
        rings = self.active + self.waiting
        self.waiting = []
        result = values if len(values) != 1 else values[0]
        if not rings:
            return result
        columns = rings[0]["own"].shape[1]
        moving, start, ended, plans, args = 0, 0, [], [], []
        for ring in rings:
            rows, hop = ring["rows"], ring["hop"]
            came_rows = (0, rows // 2, rows)[min(hop, 2)]
            came_at = start
            start += came_rows
            if hop == self.steps:
                plans.append((rows, came_at, came_rows, None))
                args.append(ring["own"])
                ended.append(ring)
            else:
                plans.append((rows if hop else rows // 2, came_at, came_rows, moving))
                args += [ring["parts"][side][hop] for side in range(2)]
                moving += rows if hop else rows // 2
            ring["hop"] += 1
        came = list(self.came) if self.came is not None else []
        size = sum(m.shape[0] for m in args)

        def kernel(*refs):
            came_refs = refs[: len(came)]
            part_refs = refs[len(came) : len(came) + len(args)]
            outs, local, semaphores = refs[len(came) + len(args) : -2], refs[-2], refs[-1]
            copies, at = [], 0
            for ref in part_refs:
                spot = local.at[pl.ds(at, ref.shape[0]), :]
                copies.append(pltpu.make_async_copy(ref, spot, semaphores.at[len(copies)]))
                copies[-1].start()
                at += ref.shape[0]
            wait_all(copies)
            final, at = (2 if moving else 0), 0
            for rows, came_at, came_rows, goes_to in plans:
                others = [ref[came_at : came_at + came_rows, :] for ref in came_refs] if came_rows else []
                if goes_to is None:
                    total = local[at : at + rows, :].astype(WIDE)
                    total = total + others[0].astype(WIDE) + others[1].astype(WIDE)
                    outs[final][...] = total[: rows // 2]
                    outs[final + 1][...] = total[rows // 2 :]
                    final += 2
                    at += rows
                    continue
                for side in range(2):
                    outs[side][goes_to : goes_to + rows, :] = local[at : at + rows, :]
                    if came_rows:
                        first = side * came_rows if came_rows < rows else 0
                        total = local[at + first : at + first + came_rows, :].astype(WIDE)
                        total = (total + others[side].astype(WIDE)).astype(LOW)
                        outs[side][goes_to + first : goes_to + first + came_rows, :] = total
                    at += rows

        outs = [shape_of((moving, columns), LOW)] * 2 if moving else []
        for ring in ended:
            outs += [shape_of((ring["rows"] // 2, columns), WIDE)] * 2
        scratch = [pltpu.VMEM((size, columns), LOW), pltpu.SemaphoreType.DMA((len(args),))]
        far_in = range(len(came), len(came) + len(args))
        res = call(kernel, outs, came + args, "ring_add", 0, scratch, far_in=far_in)
        at = 2 if moving else 0
        for ring in ended:
            ring["done"](res[at], res[at + 1])
            at += 2
        self.active = [ring for ring in rings if ring["hop"] <= self.steps]
        self.started += list(res[:2])
        self.came = (ring_shift(res[0], 1), ring_shift(res[1], -1)) if moving else None
        return result

    def busy(self):
        return bool(self.active or self.waiting)


def hop_places(rest):
    steps = rest // 2
    return [(1, k) for k in range(steps, 0, -1)] + [(0, k) for k in range(steps, 0, -1)] + [(0, 0)]


def rest_sum(parts):
    return lax.psum_scatter(parts, REST, scatter_dimension=0, tiled=False)


def small_gather(values):
    out = values[None]
    for axis in ("frame", "core", "inner", "outer"):
        size, here, step = lax.axis_size(axis), lax.axis_index(axis), 1
        while step < size:
            came = lax.ppermute(out, axis, [(i, i ^ step) for i in range(size)])
            first = (here & step) == 0
            out = jnp.concatenate([jnp.where(first, out, came), jnp.where(first, came, out)], axis=0)
            step *= 2
    return out


def small_sum(split, common):
    for axis in ("outer", "inner"):
        size, here = lax.axis_size(axis), lax.axis_index(axis)
        step = size // 2
        while step >= 1:
            half = split.shape[1] // 2
            bit = (here // step) % 2
            keep = lax.dynamic_slice_in_dim(split, bit * half, half, 1)
            send = lax.dynamic_slice_in_dim(split, (1 - bit) * half, half, 1)
            pairs = [(i, i ^ step) for i in range(size)]
            packed = jnp.concatenate([send.reshape(-1), common.reshape(-1)])
            came = lax.ppermute(packed, axis, pairs)
            split = keep + came[: keep.size].reshape(keep.shape)
            common = common + came[keep.size :].reshape(common.shape)
            step //= 2
    return split, common


def head_means(part, head_size):
    row = lax.broadcasted_iota(jnp.int32, (part, part), 0) // head_size
    column = lax.broadcasted_iota(jnp.int32, (part, part), 1) // head_size
    return jnp.where(row == column, 1.0 / head_size, 0.0).astype(LOW)


def head_mean(values, matrix):
    high = values.astype(LOW)
    rest = (values - high.astype(WIDE)).astype(LOW)
    return dot(high, matrix) + dot(rest, matrix)


def head_normed(values, matrix):
    center = values - head_mean(values, matrix)
    rate = lax.rsqrt(head_mean(center * center, matrix) + EPSILON)
    return center * rate, rate


def join(refs, out_ref):
    start = 0
    for ref in refs:
        out_ref[start : start + ref.shape[0], :] = ref[...]
        start += ref.shape[0]


def spans(refs):
    start = 0
    for ref in refs:
        yield start, start + ref.shape[0], ref
        start += ref.shape[0]


def flat_rows(ref, first, height, columns):
    block = ref[:, first : first + height, columns]
    return block.reshape(block.shape[0] * height, block.shape[2])


def tiles_of(total, group, block):
    for base in range(0, total, group):
        for start in range(base, base + group, block):
            yield start, base


def allowed_of(ids_col, ids_row, start, base, block, group, use_frame):
    if use_frame:
        row = lax.broadcasted_iota(jnp.int32, (block, group), 0) // FRAME_TOK
        column = lax.broadcasted_iota(jnp.int32, (block, group), 1) // FRAME_TOK
        return row == column
    return ids_col[start : start + block, :] == ids_row[:, base : base + group]


def plan(frames, rows, use_frame):
    group = min(4 * FRAME_TOK, frames * rows) if use_frame else frames * rows
    return group, min(group, 256)


def part_shapes(pieces, width):
    half = len(pieces) // 2
    return [shape_of((m.shape[0], width), WIDE if i < half else LOW) for i, m in enumerate(pieces)]


def load_semaphores(sources):
    return [pltpu.SemaphoreType.DMA((source.count,)) for source in sources]


def start_loads(sources, table_ref, far_refs, targets, semaphores):
    at, copies = 0, []
    for source, target, semaphore in zip(sources, targets, semaphores):
        copies.append(source.start(far_refs[at : at + source.count], table_ref, target, semaphore))
        at += source.count
    return copies


def attn_forward(pieces, weights, bias, head_gain, head_shift, ids, head_size, frames, use_frame, vectors=None):
    attn, proj, height, wide, table = weights
    sources = [attn] if proj is None else [attn, proj]
    far = [m for source in sources for m in source.args]
    rest, unit, _ = attn.shape
    width, part = rest * unit, head_gain.shape[-1]
    total = sum(m.shape[0] for m in pieces)
    count = len(pieces)
    group, block = plan(frames, total // (2 * frames), use_frame)
    lanes = min(128, part)
    per = lanes // head_size
    scale = head_size ** (-0.5)
    more = 0 if vectors is None else 1

    def kernel(table_ref, *refs):
        far_refs, refs = refs[: len(far)], refs[len(far) :]
        semaphores, refs = refs[-len(sources) :], refs[: -len(sources)]
        targets, refs = refs[-len(sources) :], refs[: -len(sources)]
        copies = start_loads(sources, table_ref, far_refs, targets, semaphores)
        wq, wp = targets[0], targets[-1]
        piece_refs = refs[:count]
        bias_ref, gain_ref, shift_ref, ids_col, ids_row = refs[count : count + 5]
        first, raw, qkv, lse, flat = refs[count + 5 + more : count + 10 + more]
        outs = refs[count + 10 + more :]
        if more:
            vec = refs[count + 5]
            for start, stop, ref in spans(piece_refs):
                unit_one, _ = normed(ref[...].astype(WIDE))
                value = unit_one * row_of(vec, GAIN, 0, 0) + row_of(vec, SHIFT, 0, 0)
                first[start:stop, :] = value.astype(LOW)
        else:
            join(piece_refs, first)
        matrix = head_means(part, head_size)
        for group_copies in copies:
            wait_all(group_copies)
        mixed = dot(first[...], flat_rows(wq, 0, unit, slice(0, 3 * part))) + bias_ref[...]
        raw[...] = mixed[:, : 2 * part]
        for i in range(2):
            unit_i, _ = head_normed(mixed[:, i * part : (i + 1) * part], matrix)
            value = unit_i * gain_ref[i : i + 1, :] + shift_ref[i : i + 1, :]
            qkv[:, i * part : (i + 1) * part] = value.astype(LOW)
        qkv[:, 2 * part :] = mixed[:, 2 * part :].astype(LOW)
        place = lax.broadcasted_iota(jnp.int32, (1, lanes), 1) // head_size
        for start, base in tiles_of(total, group, block):
            allowed = allowed_of(ids_col, ids_row, start, base, block, group, use_frame)
            stats = []
            for lane in range(0, part, lanes):
                query = qkv[start : start + block, lane : lane + lanes] * jnp.asarray(scale, LOW)
                key = qkv[base : base + group, part + lane : part + lane + lanes]
                value = qkv[base : base + group, 2 * part + lane : 2 * part + lane + lanes]
                out = jnp.zeros((block, lanes), WIDE)
                for h in range(per):
                    mask = place == h
                    scores = dot_nt(jnp.where(mask, query, jnp.zeros_like(query)), key)
                    scores = jnp.where(allowed, scores, -jnp.inf)
                    top = jnp.max(scores, axis=-1, keepdims=True)
                    weight = jnp.exp(scores - top)
                    norm = jnp.sum(weight, axis=-1, keepdims=True)
                    stats.append(top + jnp.log(norm))
                    probs = (weight * (1.0 / norm)).astype(LOW)
                    out = jnp.where(mask, dot(probs, value), out)
                flat[start : start + block, lane : lane + lanes] = out.astype(LOW)
            lse[start : start + block, :] = jnp.concatenate(stats, axis=1)
        for a in range(0, width, wide):
            b = a + wide
            chunk = flat_rows(wp, a // wide * height, height, slice(wp.shape[2] - wide, wp.shape[2]))
            for start, stop, ref in spans(outs):
                ref[:, a:b] = dot(flat[start:stop, :], chunk).astype(ref.dtype)

    outs = [
        shape_of((total, width), LOW),
        shape_of((total, 2 * part), WIDE),
        shape_of((total, 3 * part), LOW),
        shape_of((total, part // head_size), WIDE),
        shape_of((total, part), LOW),
    ] + part_shapes(pieces, width)
    outs += [shape_of(source.shape, LOW) for source in sources]
    args = [table] + far + list(pieces)
    args += [bias, head_gain, head_shift, ids.reshape(-1, 1), ids.reshape(1, -1)]
    args += [vectors] if more else []
    flops = 2 * total * (width * 4 * part + group * 2 * part)
    scratch = load_semaphores(sources)
    res = call(kernel, outs, args, "attn_forward", flops, scratch, 1, far_in=range(1, 1 + len(far)))
    weights = (res[5 + count], None if proj is None else res[6 + count], height, wide)
    return res[:5], res[5 : 5 + count // 2], res[5 + count // 2 : 5 + count], weights


def attn_backward(pieces, weights, head_gain, kept, ids, head_size, frames, use_frame):
    _, raw, qkv, lse, _ = kept
    attn, proj, height, wide = weights
    rest, unit, _ = attn.shape
    width, part = rest * unit, head_gain.shape[-1]
    total = sum(m.shape[0] for m in pieces)
    count = len(pieces)
    group, block = plan(frames, total // (2 * frames), use_frame)
    lanes = min(128, part)
    per = lanes // head_size
    scale = head_size ** (-0.5)
    extra = 0 if proj is None else 1

    def kernel(*refs):
        piece_refs, wq, wp = refs[:count], refs[count], refs[count + extra]
        refs = refs[extra + 1 :]
        gain_ref, raw_ref, qkv_ref, lse_ref, ids_col, ids_row = refs[count : count + 6]
        joined, low_mixed, sums, head_sums = refs[count + 6 : count + 10]
        outs = refs[count + 10 : count + 10 + count]
        grad_out, grad_three = refs[count + 10 + count :]
        join(piece_refs, joined)
        grad_flat = jnp.zeros((total, part), WIDE)
        for a in range(0, width, wide):
            b = a + wide
            chunk = flat_rows(wp, a // wide * height, height, slice(wp.shape[2] - wide, wp.shape[2]))
            grad_flat += dot_nt(joined[:, a:b], chunk)
        grad_out[...] = grad_flat.astype(LOW)
        place = lax.broadcasted_iota(jnp.int32, (1, lanes), 1) // head_size
        for start, base in tiles_of(total, group, block):
            allowed = allowed_of(ids_col, ids_row, start, base, block, group, use_frame)
            stats = lse_ref[start : start + block, :]
            for lane in range(0, part, lanes):
                query = qkv_ref[start : start + block, lane : lane + lanes] * jnp.asarray(scale, LOW)
                key = qkv_ref[base : base + group, part + lane : part + lane + lanes]
                value = qkv_ref[base : base + group, 2 * part + lane : 2 * part + lane + lanes]
                grad_here = grad_out[start : start + block, lane : lane + lanes]
                grad_q = jnp.zeros((block, lanes), WIDE)
                grad_k = jnp.zeros((group, lanes), WIDE)
                grad_v = jnp.zeros((group, lanes), WIDE)
                for h in range(per):
                    mask = place == h
                    head = lane // head_size + h
                    scores = dot_nt(jnp.where(mask, query, jnp.zeros_like(query)), key)
                    probs = jnp.exp(jnp.where(allowed, scores - stats[:, head : head + 1], -jnp.inf))
                    grad_p = dot_nt(jnp.where(mask, grad_here, jnp.zeros_like(grad_here)), value)
                    delta = jnp.sum(probs * grad_p, axis=-1, keepdims=True)
                    grad_s = (probs * (grad_p - delta)).astype(LOW)
                    grad_q = jnp.where(mask, dot(grad_s, key), grad_q)
                    grad_k = jnp.where(mask, dot_tn(grad_s, query), grad_k)
                    grad_v = jnp.where(mask, dot_tn(probs.astype(LOW), grad_here), grad_v)
                grad_three[start : start + block, lane : lane + lanes] = grad_q * scale
                for at, grad in ((part, grad_k), (2 * part, grad_v)):
                    spot = (slice(base, base + group), slice(at + lane, at + lane + lanes))
                    if start == base:
                        grad_three[spot] = grad
                    else:
                        grad_three[spot] = grad_three[spot] + grad
        matrix = head_means(part, head_size)
        for i in range(2):
            here = slice(i * part, (i + 1) * part)
            grad = grad_three[:, here]
            unit_i, rate = head_normed(raw_ref[:, here], matrix)
            head_sums[i : i + 1, :] = jnp.sum(grad * unit_i, axis=0, keepdims=True)
            head_sums[2 + i : 3 + i, :] = jnp.sum(grad, axis=0, keepdims=True)
            inner = grad * gain_ref[i : i + 1, :]
            mean_one = head_mean(inner, matrix)
            mean_two = head_mean(inner * unit_i, matrix)
            result = rate * (inner - mean_one - unit_i * mean_two)
            sums[:, here] = jnp.sum(result, axis=0, keepdims=True)
            low_mixed[:, here] = result.astype(LOW)
        result = grad_three[:, 2 * part :]
        sums[:, 2 * part :] = jnp.sum(result, axis=0, keepdims=True)
        low_mixed[:, 2 * part :] = result.astype(LOW)
        weight = flat_rows(wq, 0, unit, slice(0, 3 * part))
        for start, stop, ref in spans(outs):
            ref[...] = dot_nt(low_mixed[start:stop, :], weight).astype(ref.dtype)

    outs = [
        shape_of((total, width), LOW),
        shape_of((total, 3 * part), LOW),
        shape_of((1, 3 * part), WIDE),
        shape_of((4, part), WIDE),
    ] + part_shapes(pieces, width)
    scratch = [pltpu.VMEM((total, part), LOW), pltpu.VMEM((total, 3 * part), WIDE)]
    args = list(pieces) + [attn] + ([] if proj is None else [proj])
    args += [head_gain, raw, qkv, lse, ids.reshape(-1, 1), ids.reshape(1, -1)]
    flops = 2 * total * (width * 4 * part + group * 5 * part)
    res = call(kernel, outs, args, "attn_backward", flops, scratch)
    return res[:4], res[4 : 4 + count // 2], res[4 + count // 2 :]


def attn_weight_grads(first, low_mixed, flat, att_low, rest, height, table):
    width, part = first.shape[1], flat.shape[1]
    unit = width // rest
    wide = width * height // unit
    places = hop_places(rest)
    steps = rest // 2

    def kernel(table_ref, first_ref, mixed_ref, flat_ref, att_ref, *refs):
        outs, packed, semaphores = refs[:-2], refs[-2], refs[-1]
        product = dot_tn(first_ref[...], mixed_ref[...]).astype(LOW)
        packed[:, :, : 3 * part] = product.reshape(rest, unit, 3 * part)
        product = dot_tn(flat_ref[...], att_ref[...]).astype(LOW)
        for j in range(unit // height):
            chunk = product[:, j * wide : (j + 1) * wide].reshape(rest, height, wide)
            packed[:, j * height : (j + 1) * height, 3 * part :] = chunk
        copies = []
        for i, (side, k) in enumerate(places):
            first_row = unit // 2 if i == steps else 0
            source = packed.at[table_ref[side, k], pl.ds(first_row, outs[i].shape[0]), :]
            copies.append(pltpu.make_async_copy(source, outs[i], semaphores.at[i]))
            copies[-1].start()
        wait_all(copies)

    flops = 8 * first.shape[0] * width * part
    outs = [shape_of((unit // 2 if k == steps else unit, 4 * part), LOW) for _, k in places]
    scratch = [pltpu.VMEM((rest, unit, 4 * part), LOW), pltpu.SemaphoreType.DMA((len(places),))]
    args = [table, first, low_mixed, flat, att_low]
    res = call(kernel, outs, args, "attn_weight_grads", flops, scratch, 1, far_out=range(len(outs)))
    return res[:steps], res[steps : 2 * steps], res[2 * steps]


def mlp_weight_grads(second, pre_low, act, branch_low, rest, table):
    width, hidden = second.shape[1], act.shape[1]
    rows = width // rest
    places = hop_places(rest)
    steps = rest // 2

    def kernel(table_ref, second_ref, pre_ref, act_ref, branch_ref, *refs):
        outs, packs, semaphores = refs[:-3], refs[-3:-1], refs[-1]
        copies = []
        for which, (left, right) in enumerate(((second_ref, pre_ref), (act_ref, branch_ref))):
            pack = packs[which]
            pack[...] = dot_tn(left[...], right[...]).astype(LOW).reshape(pack.shape)
            for i, (side, k) in enumerate(places):
                if k == steps and i // steps != which:
                    continue
                spot = outs[i].at[pl.ds(0 if k == steps else which * rows, rows), :]
                source = pack.at[table_ref[side, k]]
                copies.append(pltpu.make_async_copy(source, spot, semaphores.at[len(copies)]))
                copies[-1].start()
        wait_all(copies)

    flops = 4 * second.shape[0] * width * hidden
    outs = [shape_of((rows if k == steps else 2 * rows, width), LOW) for _, k in places]
    scratch = [pltpu.VMEM((rest, rows, width), LOW)] * 2 + [pltpu.SemaphoreType.DMA((2 * len(places),))]
    args = [table, second, pre_low, act, branch_low]
    res = call(kernel, outs, args, "mlp_weight_grads", flops, scratch, 1, far_out=range(len(outs)))
    return res[:steps], res[steps : 2 * steps], res[2 * steps]


def mlp_forward(pieces, sources, table, bias):
    rest, unit, hidden = sources[0].shape
    width = rest * unit
    far = [m for source in sources for m in source.args]
    total = sum(m.shape[0] for m in pieces)
    count = len(pieces)

    def kernel(table_ref, *refs):
        far_refs, refs, (up, down), semaphores = refs[: len(far)], refs[len(far) : -4], refs[-4:-2], refs[-2:]
        copies, more_copies = start_loads(sources, table_ref, far_refs, (up, down), semaphores)
        piece_refs = refs[:count]
        bias_ref = refs[count]
        second, act, slope = refs[count + 1 : count + 4]
        outs = refs[count + 4 :]
        join(piece_refs, second)
        wait_all(copies)
        pre = dot(second[...], flat_rows(up, 0, unit, slice(None))) + bias_ref[...]
        below = 0.5 * (1.0 + lax.erf(pre * ROOT_HALF))
        act[...] = (pre * below).astype(LOW)
        slope[...] = (below + pre * (ROOT_TWO_PI * jnp.exp(-0.5 * pre * pre))).astype(LOW)
        wait_all(more_copies)
        weight = flat_rows(down, 0, down.shape[1], slice(None))
        for start, stop, ref in spans(outs):
            ref[...] = dot(act[start:stop, :], weight).astype(ref.dtype)

    outs = [
        shape_of((total, width), LOW),
        shape_of((total, hidden), LOW),
        shape_of((total, hidden), LOW),
    ] + part_shapes(pieces, width)
    outs += [shape_of(source.shape, LOW) for source in sources]
    args = [table] + far + list(pieces) + [bias]
    flops, far_in = 4 * total * width * hidden, range(1, 1 + len(far))
    res = call(kernel, outs, args, "mlp_forward", flops, load_semaphores(sources), 1, far_in=far_in)
    return res[:3], res[3 : 3 + count // 2], res[3 + count // 2 : 3 + count], res[3 + count :]


def mlp_backward(pieces, weight_up, weight_down, slope):
    rest, unit, hidden = weight_up.shape
    width = rest * unit
    total = sum(m.shape[0] for m in pieces)
    count = len(pieces)

    def kernel(*refs):
        piece_refs = refs[:count]
        up, down, slope_ref = refs[count : count + 3]
        joined, low_pre, sums = refs[count + 3 : count + 6]
        outs = refs[count + 6 :]
        join(piece_refs, joined)
        weight = flat_rows(down, 0, down.shape[1], slice(None))
        grad = dot_nt(joined[...], weight) * slope_ref[...].astype(WIDE)
        sums[...] = jnp.sum(grad, axis=0, keepdims=True)
        low_pre[...] = grad.astype(LOW)
        weight = flat_rows(up, 0, unit, slice(None))
        for start, stop, ref in spans(outs):
            ref[...] = dot_nt(low_pre[start:stop, :], weight).astype(ref.dtype)

    outs = [
        shape_of((total, width), LOW),
        shape_of((total, hidden), LOW),
        shape_of((1, hidden), WIDE),
    ] + part_shapes(pieces, width)
    args = list(pieces) + [weight_up, weight_down, slope]
    res = call(kernel, outs, args, "mlp_backward", 4 * total * width * hidden)
    return res[:3], res[3 : 3 + count // 2], res[3 + count // 2 :]


def added(refs):
    total = refs[0][...]
    for ref in refs[1:]:
        total = total + ref[...].astype(WIDE)
    return total


def row_of(vectors, kind, depth, which):
    at = kind + 2 * depth + which
    return vectors[at : at + 1, :]


def branch_norm(stream, terms, vectors, depth, which):
    after = (depth, 1) if which == 0 else (depth + 1, 0)

    def kernel(stream_ref, *refs):
        (vec, branch, result, low), term_refs = refs[-4:], refs[:-4]
        value = added(term_refs) + row_of(vec, OUT, depth, which)
        branch[...] = value
        value = stream_ref[...].astype(WIDE) + row_of(vec, SCALE, depth, which) * value
        result[...] = value
        unit, _ = normed(value)
        low[...] = (unit * row_of(vec, GAIN, *after) + row_of(vec, SHIFT, *after)).astype(LOW)

    outs = [shape_of(stream.shape, WIDE), shape_of(stream.shape, WIDE), shape_of(stream.shape, LOW)]
    return call(kernel, outs, [stream, *terms, vectors], "branch_norm")


def turn(middle, terms, cotangent, vectors):
    def kernel(middle_ref, *refs):
        (cot, vec, result, low, sums), term_refs = refs[-5:], refs[:-5]
        branch = added(term_refs) + row_of(vec, OUT, 1, 1)
        scale = row_of(vec, SCALE, 1, 1)
        result[...] = (middle_ref[...] + scale * branch).astype(LOW)
        grad = cot[...].astype(WIDE)
        grad_branch = grad * scale
        low[...] = grad_branch.astype(LOW)
        sums[0:1, :] = jnp.sum(grad * branch, axis=0, keepdims=True)
        sums[1:2, :] = jnp.sum(grad_branch, axis=0, keepdims=True)

    shape = middle.shape
    outs = [shape_of(shape, LOW), shape_of(shape, LOW), shape_of((2, shape[1]), WIDE)]
    return call(kernel, outs, [middle, *terms, cotangent, vectors], "turn")


def norm_back(grad, terms, stream, branch, vectors, depth, which, before):
    def kernel(*refs):
        grad_ref, stream_ref, vec = refs[0], refs[1], refs[2]
        inputs = 4 if before else 3
        term_refs = refs[inputs : inputs + len(terms)]
        result, low, sums = (refs[inputs + len(terms) :] + (None,))[:3] if before else (
            None, refs[inputs + len(terms)], refs[inputs + len(terms) + 1],
        )
        came = added(term_refs)
        unit, rate = normed(stream_ref[...].astype(WIDE))
        sums[0:1, :] = jnp.sum(came * unit, axis=0, keepdims=True)
        sums[1:2, :] = jnp.sum(came, axis=0, keepdims=True)
        value = grad_ref[...].astype(WIDE)
        value = value + normed_back(came, unit, rate, row_of(vec, GAIN, depth, which))
        if not before:
            low[...] = value.astype(LOW)
            return
        result[...] = value
        sums[2:3, :] = jnp.sum(value * refs[3][...], axis=0, keepdims=True)
        value = value * row_of(vec, SCALE, *before)
        sums[3:4, :] = jnp.sum(value, axis=0, keepdims=True)
        low[...] = value.astype(LOW)

    shape = grad.shape
    outs = [shape_of(shape, LOW), shape_of((4 if before else 2, shape[1]), WIDE)]
    args = [grad, stream, vectors]
    if before:
        outs = [shape_of(shape, WIDE)] + outs
        args = args + [branch]
    return call(kernel, outs, args + list(terms), "norm_back")


def split_grads(grads, me):
    rows, width = grads[0].shape[0] * len(grads) // 4, grads[0].shape[1]

    def kernel(me_ref, *refs):
        ins, outs = refs[: len(grads)], refs[len(grads) : len(grads) + 4]
        joined = refs[-1]
        join(ins, joined)
        for away, out in enumerate(outs):
            member = jnp.bitwise_xor(me_ref[0], away)
            out[...] = joined[pl.ds(pl.multiple_of(member * rows, rows), rows), :].astype(LOW)

    scratch = [pltpu.VMEM((4 * rows, width), grads[0].dtype)]
    out = shape_of((rows, width), LOW)
    return call(kernel, [out] * 4, [me, *grads], "split_grads", scratch=scratch, scalars=1)


def place_grads(qkv_pieces, up_pieces, proj, down, part, rest, me):
    rows, hidden = up_pieces[0][0].shape
    width = 4 * part
    lanes = hidden // rest

    def kernel(me_ref, *refs):
        pieces, (proj0, proj1, down0, down1) = refs[:16], refs[16:20]
        qkv_out, up_out, proj_out, down_out = refs[20:]
        for depth in range(2):
            for away in range(4):
                member = jnp.bitwise_xor(me_ref[0], away)
                ref = pieces[4 * depth + away]
                for s in range(3):
                    start = pl.multiple_of(s * width + member * part, 128)
                    value = ref[:, s * part : (s + 1) * part].astype(WIDE)
                    qkv_out[depth, :, pl.ds(start, part)] = value
                ref = pieces[8 + 4 * depth + away]
                for f in range(rest):
                    start = pl.multiple_of((f * 4 + member) * lanes, 128)
                    value = ref[:, f * lanes : (f + 1) * lanes].astype(WIDE)
                    up_out[depth, :, pl.ds(start, lanes)] = value
            down_out[depth] = (down0, down1)[depth][...].astype(WIDE)
            proj_out[depth] = (proj0, proj1)[depth][...].astype(WIDE)

    outs = [
        shape_of((2, rows, 3 * width), WIDE),
        shape_of((2, rows, 4 * hidden), WIDE),
        shape_of((2,) + proj[0].shape, WIDE),
        shape_of((2,) + down[0].shape, WIDE),
    ]
    args = [me, *qkv_pieces[0], *qkv_pieces[1], *up_pieces[0], *up_pieces[1], *proj, *down]
    return call(kernel, outs, args, "place_grads", scalars=1)


def on_device(
    tokens,
    cotangent,
    scene_ids,
    frame_index,
    qkv_weight,
    qkv_bias,
    proj_weight,
    fc1_weight,
    fc1_bias,
    fc2_weight,
    out_bias,
    norm_gain,
    norm_bias,
    layer_scale,
    qk_gain,
    qk_bias,
):
    frames = lax.axis_size("frame")
    team = 2 * frames
    rest = lax.axis_size("outer") * lax.axis_size("inner")
    count = team * rest
    rows, width = tokens.shape
    head_size = qk_gain.shape[-1]
    heads = width // head_size // team
    part = heads * head_size
    hidden = fc1_weight.shape[-1] // team
    mine = lax.axis_index("core") * frames + lax.axis_index("frame")
    here = lax.axis_index("outer") * lax.axis_size("inner") + lax.axis_index("inner")
    me = mine.reshape(1).astype(jnp.int32)
    shard_rows = qkv_weight.shape[1]
    fc2_rows = fc2_weight.shape[1]
    unit = team * shard_rows
    table = ring_table()
    quick = frames == 2 and shard_rows % 32 == 0 and part % 128 == 0 and (hidden // rest) % 128 == 0
    quick = quick and hidden == width and width // count == 32 and count * rows // FRAME_TOK <= 256

    small_parts = (qkv_bias, fc1_bias, out_bias, norm_gain, norm_bias, layer_scale)
    head_gain = jnp.tile(qk_gain.astype(WIDE), (1, 1, heads))
    head_shift = jnp.tile(qk_bias.astype(WIDE), (1, 1, heads))
    weights = []
    if quick:
        proj_here = lax.ppermute(proj_weight, EVERY, spread(count, team))
        shards, below = [], None
        for depth in range(2):
            small = (qkv_bias, fc1_bias, scene_ids.reshape(1, rows)) + small_parts[2:]
            split = split_weights(depth, (qkv_weight, fc1_weight), () if depth else small, part, rest, me)
            pieces = [split[0], swap(split[1], "frame"), swap(split[2], "core"), cross(split[3])]
            if depth == 0:
                below = pieces
            shards.append(pack_weights(pieces, proj_here, fc2_weight, depth, part, me, depth == 0))
        ids = jnp.concatenate([m[shard_rows, 512 : 512 + rows] for m in below]).astype(jnp.int32)
        tokens_all = team_gather(tokens)
        rings = []
        for depth in range(2):
            attn, both = shards[depth]
            ring = RingGather(attn, unit // 2, rest)
            if depth == 0:
                steps(1, ring)
                ring.came = tie(*ring.came, *shards[1])[:2]
            came = steps(LEAD[depth] - 1 if depth == 0 else LEAD[depth], ring)
            both = tie(both, *came)[0] if came else both
            rings.append((ring, RingGather(both, unit, rest)))
            for ring in rings[depth]:
                steps(rest, ring)
        vectors, bias_qkv, bias_up = unpack_vectors(rings[0][0].rows(unit, SMALL_ROWS), table, me)
    else:
        proj_here = lax.ppermute(proj_weight, EVERY, spread(count, team))
        for depth in range(2):
            attn = exchange_columns(
                qkv_weight[depth]
                .reshape(shard_rows, 3, team, part)
                .transpose(0, 2, 1, 3)
                .reshape(shard_rows, team, 3 * part)
            ).reshape(unit, 3 * part)
            attn = jnp.concatenate([attn, widen(proj_here[depth], part)], axis=1)
            up = exchange_columns(
                fc1_weight[depth]
                .reshape(shard_rows, rest, team, hidden // rest)
                .transpose(0, 2, 1, 3)
                .reshape(shard_rows, team, hidden)
            ).reshape(unit, hidden)
            down = widen(fc2_weight[depth], hidden)
            attn, up, down = (lax.all_gather(m, REST, axis=0, tiled=False) for m in (attn, up, down))
            proj = Whole(narrow(attn[:, :, 3 * part :], shard_rows).reshape(1, part, width), 0, part)
            down = Whole(narrow(down, fc2_rows).reshape(1, hidden, width), 0, hidden)
            weights.append(((Whole(attn, 0, unit), proj, part, width, table), (Whole(up, 0, unit), down)))
        small = small_gather(jnp.concatenate([m.reshape(-1) for m in small_parts])).astype(WIDE)
        n_qkv, n_up = qkv_bias.size, fc1_bias.size
        bias_qkv = small[:, :n_qkv].reshape(count, 2, -1).transpose(1, 0, 2).reshape(2, 3, team, part)
        bias_qkv = lax.dynamic_index_in_dim(bias_qkv, mine, 2, keepdims=False).reshape(2, 3 * part)
        bias_up = small[:, n_qkv : n_qkv + n_up].reshape(rest, team, 2, -1)
        bias_up = lax.dynamic_index_in_dim(bias_up, mine, 1, keepdims=False)
        bias_up = bias_up.transpose(1, 0, 2).reshape(2, hidden)
        vectors = small[:, n_qkv + n_up :].reshape(count, 16, -1).transpose(1, 0, 2).reshape(16, width)
        ids = jnp.concatenate([m.reshape(-1) for m in team_gather(scene_ids.reshape(1, rows))])
        tokens_all = team_gather(tokens)

    gathered = []
    streams, middles, branches, kept = [tokens], [], [], []
    for depth in range(2):
        work = None
        if quick:
            attn_weights = (rings[depth][0].rows(0, unit), None, shard_rows, part, table)
        else:
            attn_weights, mlp_sources = weights[depth]
        kept_attn, own, peer, attn_weights = attn_forward(
            team_gather(low, work, work) if depth else tokens_all, attn_weights, bias_qkv[depth : depth + 1],
            head_gain[depth], head_shift[depth], ids, head_size, frames, depth == 0, None if depth else vectors,
        )
        terms = team_sum(own, peer, work)
        branch_one, middle, low = branch_norm(streams[depth], terms, vectors, depth, 0)
        pieces = team_gather(low, work, work)
        if quick:
            mlp_sources = (rings[depth][1].rows(0, unit), rings[depth][1].rows(unit, unit))
        kept_mlp, own, peer, mlp_weights = mlp_forward(pieces, mlp_sources, table, bias_up[depth : depth + 1])
        gathered.append((attn_weights, mlp_weights))
        terms = team_sum(own, peer, work)
        branch_two = None
        if depth == 0:
            branch_two, stream, low = branch_norm(middle, terms, vectors, 0, 1)
            streams.append(stream)
        middles.append(middle)
        branches.append((branch_one, branch_two))
        kept.append((kept_attn, kept_mlp))

    activations, low, turn_sums = turn(middles[1], terms, cotangent, vectors)
    grad = cotangent
    names, token_sums = [(SCALE, 1, 1), (OUT, 1, 1)], [turn_sums]
    sums_up, sums_qkv, head_sums = [None, None], [None, None], [None, None]
    finals = [{}, {}]
    ring = RingSums(rest)

    home = [(b, a) for a, b in spread(count, team)]

    def end_mlp(depth):
        def end(up_sum, down_sum):
            if not quick:
                up = exchange_columns(up_sum.astype(LOW).reshape(team, shard_rows, hidden).transpose(1, 0, 2))
                up = up.reshape(team, shard_rows, rest, hidden // rest).transpose(1, 2, 0, 3)
                finals[depth].update(up=up.reshape(shard_rows, -1), down=narrow(down_sum, fc2_rows))
                return
            end_up(depth)(up_sum)
            finals[depth].update(down=down_sum)

        return end

    def end_up(depth):
        def end(*halves):
            m = split_grads(halves, me)
            pieces = [m[0], swap(m[1], "frame"), swap(m[2], "core"), cross(m[3])]
            ring.started += pieces[1:]
            finals[depth].update(up=pieces)

        return end

    def end_attn(depth):
        def end(low_sum, high_sum):
            if not quick:
                both = jnp.concatenate([low_sum, high_sum], axis=0)
                qkv = exchange_columns(
                    both[:, : 3 * part].astype(LOW).reshape(team, shard_rows, 3 * part).transpose(1, 0, 2)
                )
                qkv = qkv.reshape(team, shard_rows, 3, part).transpose(1, 2, 0, 3)
                proj = narrow(both[:, 3 * part :], shard_rows)
                proj = lax.ppermute(proj.astype(LOW), EVERY, home)
                finals[depth].update(qkv=qkv.reshape(shard_rows, -1), proj=proj)
                return
            m = split_grads([low_sum[:, : 3 * part], high_sum[:, : 3 * part]], me)
            proj = jnp.concatenate([n[:, 3 * part :] for n in (low_sum, high_sum)], axis=0)
            pieces = [m[0], swap(m[1], "frame"), swap(m[2], "core"), cross(m[3])]
            ring.started += pieces[1:] if depth else []
            finals[depth].update(
                qkv=pieces,
                proj=lax.ppermute(narrow(proj, shard_rows).astype(LOW), EVERY, home),
            )

        return end

    for depth in (1, 0):
        attn_weights, (weight_up, weight_down) = gathered[depth]
        kept_attn, (second, act, slope) = kept[depth]
        first, flat = kept_attn[0], kept_attn[4]
        pieces = team_gather(low, ring.work, ring.pump)
        (branch_low, pre_low, sum_up), own, peer = mlp_backward(pieces, weight_up, weight_down, slope)
        sums_up[depth] = sum_up
        if quick:
            mlp_parts = mlp_weight_grads(second, pre_low, act, branch_low, rest, table)
        else:
            grad_up = dot_tn(second, pre_low).astype(LOW).reshape(rest, unit, hidden)
            grad_down = dot_tn(act, branch_low).astype(LOW)
            grad_down = grad_down.reshape(rest, fc2_rows, width // hidden, hidden)
            grad_down = grad_down.transpose(0, 2, 1, 3).reshape(rest, -1, hidden)
            end_mlp(depth)(rest_sum(grad_up), rest_sum(grad_down))
        if quick:
            ring.add(*mlp_parts, end_mlp(depth))
        terms = team_sum(own, peer, ring.work, ring.pump)
        grad_middle, low, sums = norm_back(
            grad, terms, middles[depth], branches[depth][0], vectors, depth, 1, (depth, 0)
        )
        names += [(GAIN, depth, 1), (SHIFT, depth, 1), (SCALE, depth, 0), (OUT, depth, 0)]
        token_sums.append(sums)
        pieces = team_gather(low, ring.work, ring.pump)
        (att_low, mixed_low, sum_qkv, head_sum), own, peer = attn_backward(
            pieces, attn_weights, head_gain[depth], kept_attn, ids, head_size, frames, depth == 0
        )
        sums_qkv[depth], head_sums[depth] = sum_qkv, head_sum
        if quick:
            attn_parts = attn_weight_grads(first, mixed_low, flat, att_low, rest, shard_rows, table)
        else:
            grad_qkv = dot_tn(first, mixed_low).astype(LOW).reshape(rest, unit, 3 * part)
            grad_proj = dot_tn(flat, att_low).astype(LOW).reshape(rest, shard_rows, team, part)
            grad_proj = grad_proj.transpose(0, 2, 1, 3).reshape(rest, unit, part)
            attn = rest_sum(jnp.concatenate([grad_qkv, grad_proj], axis=2))
            end_attn(depth)(attn[: unit // 2], attn[unit // 2 :])
        if quick:
            ring.add(*attn_parts, end_attn(depth))
        terms = team_sum(own, peer, ring.work, ring.pump)
        if depth == 1:
            grad, low, sums = norm_back(
                grad_middle, terms, streams[1], branches[0][1], vectors, 1, 0, (0, 1)
            )
            names += [(GAIN, 1, 0), (SHIFT, 1, 0), (SCALE, 0, 1), (OUT, 0, 1)]
        else:
            input_grad, sums = norm_back(grad_middle, terms, tokens, None, vectors, 0, 0, None)
            names += [(GAIN, 0, 0), (SHIFT, 0, 0)]
        token_sums.append(sums)
    while ring.busy():
        ring.hop()

    if quick:
        qkv_grad, up_grad, proj_grad, down_grad = place_grads(
            [m["qkv"] for m in finals], [m["up"] for m in finals], [m["proj"] for m in finals],
            [m["down"] for m in finals], part, rest, me,
        )
    else:
        proj_grad = jnp.stack([m["proj"] for m in finals]).astype(WIDE)
        qkv_grad, up_grad, down_grad = (
            jnp.stack([m[name] for m in finals]).astype(WIDE) for name in ("qkv", "up", "down")
        )

    full_qkv = lax.dynamic_update_slice(
        jnp.zeros((6, team, part), WIDE),
        jnp.concatenate(sums_qkv, axis=0).reshape(6, 1, part),
        (0, mine, 0),
    ).reshape(6, width)
    head_all = jnp.stack(head_sums).reshape(-1, heads, head_size).sum(axis=1).reshape(1, -1)
    head_all = jnp.pad(head_all, ((0, 0), (0, width - head_all.shape[1])))
    team_rows = jnp.concatenate([*token_sums, full_qkv, head_all], axis=0)
    team_rows = team_rows + swap(team_rows, "core")
    if frames == 2:
        team_rows = team_rows + swap(team_rows, "frame")
    else:
        team_rows = lax.psum(team_rows, "frame")
    sums_up = jnp.concatenate(sums_up, axis=0).reshape(2, rest, hidden // rest)
    sums_up = jnp.pad(sums_up, ((0, 0), (0, 0), (0, (width - hidden) // rest))).reshape(2, width)
    split = jnp.concatenate([team_rows[:16], sums_up], axis=0)
    split, common = small_sum(split, team_rows[16:])
    vector_grads = lax.dynamic_slice_in_dim(split[:16], mine * (width // count), width // count, 1)
    ordered = [(kind, depth, place) for kind in (OUT, GAIN, SHIFT, SCALE) for depth in (0, 1) for place in (0, 1)]
    vector_grads = jnp.stack([vector_grads[names.index(name)] for name in ordered]).reshape(4, 2, 2, -1)
    grad_bias_qkv = common[:6].reshape(2, -1)
    grad_bias_qkv = lax.dynamic_slice_in_dim(
        grad_bias_qkv, (here * team + mine) * qkv_bias.shape[1], qkv_bias.shape[1], 1
    )
    head_all = common[6, : 8 * head_size].reshape(2, 2, 2, head_size)
    return (
        activations,
        input_grad,
        qkv_grad,
        grad_bias_qkv,
        proj_grad,
        up_grad,
        split[16:, : hidden // rest],
        down_grad,
        vector_grads[0],
        vector_grads[1],
        vector_grads[2],
        vector_grads[3],
        head_all[:, 0],
        head_all[:, 1],
    )


def solution(mesh):
    scenes, frames = mesh.shape["scene"], mesh.shape["frame"]
    rest = scenes // 2
    outer = 4 if rest % 4 == 0 else rest
    grid = Mesh(mesh.devices.reshape(outer, rest // outer, 2, frames), EVERY)
    by_rows = P(EVERY, None)
    second = P(None, EVERY)
    second_rows = P(None, EVERY, None)
    last = P(None, None, EVERY)
    return jax.shard_map(
        on_device,
        mesh=grid,
        in_specs=(
            by_rows, by_rows, P(EVERY), P(EVERY), second_rows, second, second_rows, second_rows,
            second, second_rows, last, last, last, last, P(), P(),
        ),
        out_specs=(
            by_rows, by_rows, second_rows, second, second_rows, second_rows, second, second_rows,
            last, last, last, last, P(), P(),
        ),
        check_vma=False,
    )
```
